32 devices in a mesh: pair: 8 (over y, x, core), row: 4 (over z).
Axes of the slice: x: 2, y: 2, z: 4, core: 2. Of those that a mesh axis runs over, the one named last changes fastest.
Arguments:
- r_factor: float32 [4096, 4096], P(('row', 'pair')), may hold values from -40 to 40, as said below
- block_slots: int32 [64], replicated, may hold values from 0 to 63, as said below
Outputs:
- rotated: float32 [4096, 4096], P('row', 'pair')
- off_ratio: float32 [], replicated
The draws below stay inside these ranges and needn't reach their ends.
Inputs may be any that keep to these rules, and one draw needn't show every extreme that they name: `block_slots`: each of the 64 column blocks appears exactly once. `r_factor`: entries below the diagonal are zero and the diagonal is positive.
All inputs are finite; a program needn't handle non-finite values.
Results may differ from the reference program's by a relative error of at most 0.0001.
Values sent between devices are 32-bit elements; how exact they have to be, the bound alone decides.
No kernel may reach another device: no remote copies, remote signals or barrier semaphores. Data moves between devices by JAX's collectives and lax.ppermute only.
A program may use at most 64 MiB of HBM per device.

```python
import jax
import jax.numpy as jnp
from jax import lax

BLOCK = 64
ITERS = 3
BLOCKS = 64
ORDER = 4096


def slot_order(key):
    return jax.random.permutation(jax.random.fold_in(key, 11), BLOCKS).astype(jnp.int32)


def draw_block_slots(key, part):
    return slot_order(key)


def draw_r_factor(key, part):
    slots = slot_order(key)
    inverse = jnp.zeros((BLOCKS,), jnp.int32).at[slots].set(jnp.arange(BLOCKS, dtype=jnp.int32))
    columns = jnp.arange(ORDER, dtype=jnp.int32)
    col_block = columns // BLOCK
    col_slot = inverse[col_block]
    partner_block = slots[jnp.bitwise_xor(col_slot, 1)]
    partner_col = partner_block * BLOCK + columns % BLOCK
    level = 0.3 * 10.0 ** (col_slot.astype(jnp.float32) / (BLOCKS - 1))
    first, second, third = jax.random.split(jax.random.fold_in(key, 5), 3)
    noise = jnp.clip(jax.random.normal(first, (ORDER, ORDER), jnp.float32), -4.0, 4.0)
    factor = jnp.exp(jax.random.uniform(second, (ORDER,), jnp.float32, 0.0, 0.9))
    mixed = noise + 0.35 * noise[:, partner_col] + 0.5 * jnp.roll(noise, 1, axis=1)
    row_ids = jnp.arange(ORDER, dtype=jnp.int32)[:, None]
    upper = row_ids < columns[None, :]
    spread = mixed / jnp.sqrt(columns.astype(jnp.float32) + 1.0)[None, :]
    diag_vals = 1.0 + 0.5 * jax.random.uniform(third, (ORDER,), jnp.float32)
    entries = jnp.where(upper, spread, 0.0) + jnp.where(row_ids == columns[None, :], diag_vals[None, :], 0.0)
    return (entries * (level * factor)[None, :]).astype(jnp.float32)


def setup_inputs(seed: int = 0) -> dict:
    key_of = jax.random.split(jax.random.key(seed), 3)
    return {
        "r_factor": draw_r_factor(jax.random.fold_in(key_of[2], 71), 0),
        "block_slots": draw_block_slots(jax.random.fold_in(key_of[2], 71), 0),
    }


def cayley(pair_gram):
    size_n = pair_gram.shape[0]
    diag_vals = jnp.diagonal(pair_gram)
    spread = diag_vals[:, None] - diag_vals[None, :]
    denom = 2.0 * (diag_vals[:, None] ** 2 + diag_vals[None, :] ** 2)
    skew_part = pair_gram * spread / denom
    unit_matrix = jnp.eye(size_n, dtype=pair_gram.dtype)
    minus_part = unit_matrix - skew_part
    system = unit_matrix - jnp.dot(skew_part, skew_part, precision=lax.Precision.HIGHEST)
    product = jnp.dot(minus_part, minus_part, precision=lax.Precision.HIGHEST)
    factor = jnp.linalg.cholesky(system)
    return jax.scipy.linalg.cho_solve((factor, True), product.T).T

def reference(r_factor, block_slots):
    pair_width = 2 * BLOCK
    pair_total = BLOCKS // 2
    unit_mask = jnp.eye(pair_width, dtype=jnp.bool_)

    def solve_pair(pair_index, carry):
        rotated, off_total, diag_total = carry
        first_block = block_slots[2 * pair_index].astype(jnp.int32)
        second_block = block_slots[2 * pair_index + 1].astype(jnp.int32)
        column = jnp.concatenate([lax.dynamic_slice_in_dim(r_factor, (first_block * BLOCK).astype(jnp.int32), BLOCK, 1), lax.dynamic_slice_in_dim(r_factor, (second_block * BLOCK).astype(jnp.int32), BLOCK, 1)], axis=1)
        for sweep in range(ITERS):
            pair_gram = jnp.dot(column.T, column, precision=lax.Precision.HIGHEST)
            if sweep == 0:
                squares = pair_gram * pair_gram
                off_total = off_total + jnp.sum(jnp.where(unit_mask, 0.0, squares))
                diag_total = diag_total + jnp.sum(jnp.where(unit_mask, squares, 0.0))
            column = jnp.dot(column, cayley(pair_gram), precision=lax.Precision.HIGHEST)
        upper_slot = jnp.where(pair_index == 0, 0, jnp.where(pair_index == pair_total - 1, 2 * pair_index + 1, 2 * pair_index + 2)).astype(jnp.int32)
        lower_slot = jnp.where(pair_index == 0, 2, 2 * pair_index - 1).astype(jnp.int32)
        zero_index = jnp.zeros((), jnp.int32)
        rotated = lax.dynamic_update_slice(rotated, column[:, :BLOCK], (zero_index, (upper_slot * BLOCK).astype(jnp.int32)))
        rotated = lax.dynamic_update_slice(rotated, column[:, BLOCK:], (zero_index, (lower_slot * BLOCK).astype(jnp.int32)))
        return (rotated, off_total, diag_total)
    start = (jnp.zeros_like(r_factor), jnp.zeros((), r_factor.dtype), jnp.zeros((), r_factor.dtype))
    rotated, off_total, diag_total = lax.fori_loop(0, pair_total, solve_pair, start)
    off_ratio = jnp.sqrt(off_total / diag_total)
    return (rotated, off_ratio)
```

```python
import functools

import jax
import jax.numpy as jnp
from jax import lax
from jax.experimental import pallas as pl
from jax.experimental.pallas import tpu as pltpu
from jax.sharding import PartitionSpec as P

BLOCK = 64
WIDTH = 2 * BLOCK
ITERS = 3
TOLERANCE = 1e-8
VMEM = pl.BlockSpec(memory_space=pltpu.VMEM)
SMEM = pl.BlockSpec(memory_space=pltpu.SMEM)
PARAMS = pltpu.CompilerParams(vmem_limit_bytes=48 * 1024 * 1024)


def split(value):
    high = value.astype(jnp.bfloat16)
    low = (value - high.astype(jnp.float32)).astype(jnp.bfloat16)
    return jnp.concatenate([high, low], axis=1)


def product(left, right):
    both = jnp.dot(left, jnp.concatenate([right, right], axis=0), preferred_element_type=jnp.float32)
    half = both.shape[1] // 2
    return both[:, :half] + both[:, half:]


def unit(size):
    row_ids = lax.broadcasted_iota(jnp.int32, (size, size), 0)
    col_ids = lax.broadcasted_iota(jnp.int32, (size, size), 1)
    return row_ids == col_ids


def total(value):
    return jnp.sum(jnp.sum(value, axis=1, keepdims=True), axis=0, keepdims=True)


def gather_kernel(slots, source, out):
    groups, rows, cols = out.shape
    pairs = cols // WIDTH
    low_lanes = lax.broadcasted_iota(jnp.int32, (rows, WIDTH), 1) < BLOCK

    def tile(block, lane_half):
        start = pl.multiple_of((block // 2) * WIDTH, WIDTH)
        value = source[:, pl.ds(start, WIDTH)]
        return jnp.where(block % 2 == lane_half, value, pltpu.roll(value, BLOCK, 1))

    def one_group(group, carry):
        for pair in range(pairs):
            slot = 2 * (group * pairs + pair)
            upper = tile(slots[slot], 0)
            lower = tile(slots[slot + 1], 1)
            out[group, :, pair * WIDTH : (pair + 1) * WIDTH] = jnp.where(low_lanes, upper, lower)
        return carry

    lax.fori_loop(0, groups, one_group, 0)


def gather(r_factor, block_slots, groups):
    rows, cols = r_factor.shape
    return pl.pallas_call(
        gather_kernel,
        out_shape=jax.ShapeDtypeStruct((groups, rows, cols // groups), jnp.float32),
        in_specs=[SMEM, VMEM],
        out_specs=VMEM,
        compiler_params=PARAMS,
        name="gather",
    )(block_slots, r_factor)


def gram_kernel(shift, column, out):
    pairs = out.shape[0]
    for pair in range(pairs):
        parts = split(column[:, pair * WIDTH : (pair + 1) * WIDTH])
        four = lax.dot_general(parts, parts, (((0,), (0,)), ((), ())), preferred_element_type=jnp.float32)
        half = four[:WIDTH] + four[WIDTH:]
        out[lax.rem(pair + shift[0], pairs)] = half[:, :WIDTH] + half[:, WIDTH:]


def grams(column, shift):
    pairs = column.shape[1] // WIDTH
    return pl.pallas_call(
        gram_kernel,
        out_shape=jax.ShapeDtypeStruct((pairs, WIDTH, WIDTH), jnp.float32),
        in_specs=[SMEM, VMEM],
        out_specs=VMEM,
        compiler_params=PARAMS,
        name="grams",
    )(shift, column)


def rotation(gram, on_diag, even, odd, power):
    diag_part = jnp.where(on_diag, gram, 0.0)
    across = jnp.sum(diag_part, axis=1, keepdims=True)
    down = jnp.sum(diag_part, axis=0, keepdims=True)
    skew = gram * (across - down) / (2.0 * (across * across + down * down))
    skew_parts = split(skew)
    square = product(skew_parts, skew_parts)
    bound = jnp.sqrt(0.5 * total(square * square))
    scale = 2.0 / (2.0 + bound)
    rate = bound / (2.0 + bound)
    diag_one = jnp.where(on_diag, 1.0, 0.0)
    rest = (1.0 - scale) * diag_one + scale * square
    rest_parts = split(rest)
    size = gram.shape[0]
    first = product(jnp.concatenate([skew_parts, rest_parts], axis=0), rest_parts)
    even_now = scale * (diag_one + rest)
    odd_now = scale * (skew + first[:size])
    rest_parts = split(first[size:])
    second = product(jnp.concatenate([split(even_now), split(odd_now), rest_parts], axis=0), rest_parts)
    even_now = even_now + second[:size]
    odd_now = odd_now + second[size : 2 * size]
    rest_parts = split(second[2 * size :])
    third = product(jnp.concatenate([split(even_now), split(odd_now)], axis=0), rest_parts)
    even[...] = even_now + third[:size]
    odd[...] = odd_now + third[size:]
    power[...] = rest_parts

    def more(left):
        return left > TOLERANCE

    def step(left):
        old = power[...]
        parts = split(product(old, old))
        power[...] = parts
        even[...] += product(split(even[...]), parts)
        odd[...] += product(split(odd[...]), parts)
        return left * left

    rate = rate * rate
    rate = rate * rate
    lax.while_loop(more, step, (rate * rate)[0, 0])
    even_now = 2.0 * even[...] - diag_one
    odd_now = 2.0 * odd[...]
    return split(even_now - odd_now), split(even_now + odd_now)


def solve_kernel(count, *refs):
    parts, out, sums, even, odd, power = refs[:count], *refs[count:]
    on_diag = unit(WIDTH)
    off_total = jnp.zeros((1, 1), jnp.float32)
    diag_total = jnp.zeros((1, 1), jnp.float32)
    for pair in range(out.shape[0]):
        gram = parts[0][pair]
        for part in parts[1:]:
            gram = gram + part[pair]
        squares = gram * gram
        off_total += total(jnp.where(on_diag, 0.0, squares))
        diag_total += total(jnp.where(on_diag, squares, 0.0))
        so_far = None
        for sweep in range(ITERS):
            turn, back = rotation(gram, on_diag, even, odd, power)
            if sweep < ITERS - 1:
                gram = product(back, split(product(split(gram), turn)))
            so_far = turn if so_far is None else split(product(so_far, turn))
        out[pair] = so_far[:, :WIDTH].astype(jnp.float32) + so_far[:, WIDTH:].astype(jnp.float32)
    first_lane = lax.broadcasted_iota(jnp.int32, sums.shape, 1) == 0
    sums[...] = jnp.where(first_lane, off_total, diag_total)


def solve(parts):
    pairs = parts[0].shape[0]
    return pl.pallas_call(
        functools.partial(solve_kernel, len(parts)),
        out_shape=(
            jax.ShapeDtypeStruct((pairs, WIDTH, WIDTH), jnp.float32),
            jax.ShapeDtypeStruct((8, 128), jnp.float32),
        ),
        in_specs=[VMEM] * len(parts),
        out_specs=(VMEM, VMEM),
        scratch_shapes=[
            pltpu.VMEM((WIDTH, WIDTH), jnp.float32),
            pltpu.VMEM((WIDTH, WIDTH), jnp.float32),
            pltpu.VMEM((WIDTH, 2 * WIDTH), jnp.bfloat16),
        ],
        compiler_params=PARAMS,
        name="solve",
    )(*parts)


def load_turns(where, turns, held):
    count = len(turns)
    each = turns[0].shape[0]
    for step in range(count):
        held[pl.ds(lax.rem(where[1] + count - step, count) * each, each)] = turns[step][...]


def edge_kernel(count, where, column, *refs):
    turns, up, down, held = refs[:count], *refs[count:]
    load_turns(where, turns, held)
    pairs = held.shape[0]
    rows = column.shape[0]
    half = rows // 2
    low_lanes = lax.broadcasted_iota(jnp.int32, (half, WIDTH), 1) < BLOCK
    last = product(split(column[:, (pairs - 1) * WIDTH :]), split(held[pairs - 1]))
    up[...] = jnp.where(low_lanes, last[:half], pltpu.roll(last[half:], BLOCK, 1))
    first = product(split(column[:, :WIDTH]), split(held[0]))
    down[...] = jnp.where(low_lanes, pltpu.roll(first[:half], BLOCK, 1), first[half:])


def edges(where, column, turns):
    rows = column.shape[0]
    pairs = column.shape[1] // WIDTH
    shape = jax.ShapeDtypeStruct((rows // 2, WIDTH), jnp.float32)
    return pl.pallas_call(
        functools.partial(edge_kernel, len(turns)),
        out_shape=(shape, shape),
        in_specs=[SMEM] + [VMEM] * (1 + len(turns)),
        out_specs=(VMEM, VMEM),
        scratch_shapes=[pltpu.VMEM((pairs, WIDTH, WIDTH), jnp.float32)],
        compiler_params=PARAMS,
        name="edges",
    )(where, column, *turns)


def place_kernel(count, where, column, came_up, came_down, *refs):
    turns, out, held = refs[:count], *refs[count:]
    load_turns(where, turns, held)
    pairs = held.shape[0]
    rows = column.shape[0]
    half = rows // 2
    is_first = where[0] == 0
    is_last = where[0] == where[2] - 1
    low_lanes = lax.broadcasted_iota(jnp.int32, (half, WIDTH), 1) < BLOCK
    rotated = []
    for pair in range(pairs):
        rotated.append(product(split(column[:, pair * WIDTH : (pair + 1) * WIDTH]), split(held[pair])))
    for part in range(2):
        span = slice(part * half, (part + 1) * half)
        for pair in range(pairs):
            if pair == 0:
                arrived = came_up[...] if part == 0 else pltpu.roll(came_up[...], BLOCK, 1)
                upper = jnp.where(is_first, rotated[0][span], arrived)
            else:
                upper = rotated[pair - 1][span]
                if pair == 1:
                    upper = jnp.where(is_first, pltpu.roll(upper, BLOCK, 1), upper)
            if pair == pairs - 1:
                arrived = came_down[...] if part == 1 else pltpu.roll(came_down[...], BLOCK, 1)
                lower = jnp.where(is_last, pltpu.roll(rotated[pair][span], BLOCK, 1), arrived)
            else:
                lower = rotated[pair + 1][span]
            out[span, pair * WIDTH : (pair + 1) * WIDTH] = jnp.where(low_lanes, upper, lower)


def place(where, column, came_up, came_down, turns):
    pairs = column.shape[1] // WIDTH
    return pl.pallas_call(
        functools.partial(place_kernel, len(turns)),
        out_shape=jax.ShapeDtypeStruct(column.shape, jnp.float32),
        in_specs=[SMEM] + [VMEM] * (3 + len(turns)),
        out_specs=VMEM,
        scratch_shapes=[pltpu.VMEM((pairs, WIDTH, WIDTH), jnp.float32)],
        compiler_params=PARAMS,
        name="place",
    )(where, column, came_up, came_down, *turns)


def passed_along(value, axis, by):
    count = lax.axis_size(axis)
    pairs = [(i, i + by) for i in range(count) if 0 <= i + by < count]
    return lax.ppermute(value, axis, pairs)


def passed_round(value, axis, by):
    count = lax.axis_size(axis)
    return lax.ppermute(value, axis, [(i, (i + by) % count) for i in range(count)])


def summed(value, axis):
    count = lax.axis_size(axis)
    if count & (count - 1):
        return lax.psum(value, axis)
    step = 1
    while step < count:
        value = value + lax.ppermute(value, axis, [(i, i ^ step) for i in range(count)])
        step *= 2
    return value


def on_device(r_factor, block_slots):
    pair_count = lax.axis_size("pair")
    row_count = lax.axis_size("row")
    pair_index = lax.axis_index("pair")
    row_index = lax.axis_index("row")
    arranged = gather(r_factor, block_slots, pair_count)
    received = lax.all_to_all(arranged, "pair", split_axis=0, concat_axis=0, tiled=True)
    column = received.reshape(-1, received.shape[2])
    local_pairs = column.shape[1] // WIDTH
    shared = local_pairs % row_count == 0
    if shared:
        each = local_pairs // row_count
        shift = (row_count - row_index) * each
    else:
        shift = jnp.zeros((), jnp.int32)
    partial_grams = grams(column, shift.astype(jnp.int32).reshape(1))
    if shared:
        parts = [partial_grams[:each]]
        for by in range(1, row_count):
            parts.append(passed_round(partial_grams[by * each : (by + 1) * each], "row", by))
        turn, sums = solve(parts)
        turns = [turn] + [passed_round(turn, "row", by) for by in range(1, row_count)]
        sums = summed(sums, "row")
    else:
        turn, sums = solve([lax.psum(partial_grams, "row")])
        turns = [turn]
    where = jnp.stack([pair_index, row_index if shared else jnp.zeros_like(row_index), jnp.int32(pair_count)]).astype(jnp.int32)
    up, down = edges(where, column, turns)
    came_up = passed_along(up, "pair", 1)
    came_down = passed_along(down, "pair", -1)
    rotated = place(where, column, came_up, came_down, turns)
    sums = summed(sums, "pair")
    off_ratio = jnp.sqrt(sums[0, 0] / sums[0, 1])
    return (rotated, off_ratio)


def solution(mesh):
    in_specs = (P(("row", "pair"), None), P())
    out_specs = (P("row", "pair"), P())
    return jax.shard_map(
        on_device, mesh=mesh, in_specs=in_specs, out_specs=out_specs, check_vma=False
    )
```

```python
import functools

import jax
import jax.numpy as jnp
from jax import lax
from jax.experimental import pallas as pl
from jax.experimental.pallas import tpu as pltpu
from jax.sharding import PartitionSpec as P

BLOCK = 64
WIDTH = 2 * BLOCK
ITERS = 3
TOLERANCE = 1e-8
LAST_ROWS = 8
VMEM = pl.BlockSpec(memory_space=pltpu.VMEM)
SMEM = pl.BlockSpec(memory_space=pltpu.SMEM)
PARAMS = pltpu.CompilerParams(vmem_limit_bytes=48 * 1024 * 1024)


def split(value):
    high = value.astype(jnp.bfloat16)
    low = (value - high.astype(jnp.float32)).astype(jnp.bfloat16)
    return jnp.concatenate([high, low], axis=1)


def product(left, right):
    both = jnp.dot(left, jnp.concatenate([right, right], axis=0), preferred_element_type=jnp.float32)
    half = both.shape[1] // 2
    return both[:, :half] + both[:, half:]


def unit(size):
    row_ids = lax.broadcasted_iota(jnp.int32, (size, size), 0)
    col_ids = lax.broadcasted_iota(jnp.int32, (size, size), 1)
    return row_ids == col_ids


def total(value):
    return jnp.sum(jnp.sum(value, axis=1, keepdims=True), axis=0, keepdims=True)


def gather_kernel(plan, slots, base, source, *outs):
    rows = source.shape[0]
    local = plan[0][0]
    low_lanes = lax.broadcasted_iota(jnp.int32, (rows, WIDTH), 1) < BLOCK

    def tile(block, lane_half):
        start = pl.multiple_of((block // 2) * WIDTH, WIDTH)
        value = source[:, pl.ds(start, WIDTH)]
        return jnp.where(block % 2 == lane_half, value, pltpu.roll(value, BLOCK, 1))

    for (_, first, positions), out in zip(plan, outs):
        count = out.shape[2] // WIDTH

        def one(group, place, first=first, count=count, out=out):
            for pair in range(count):
                slot = 2 * (group * local + first + pair)
                upper = tile(slots[slot], 0)
                lower = tile(slots[slot + 1], 1)
                out[place, :, pair * WIDTH : (pair + 1) * WIDTH] = jnp.where(low_lanes, upper, lower)

        if positions is None:

            def step(group, carry, one=one):
                one(group, group)
                return carry

            lax.fori_loop(0, out.shape[0], step, 0)
        else:
            for place, position in enumerate(positions):
                one(jnp.bitwise_xor(base[0], position), place)


def gather(r_factor, block_slots, base, plan):
    rows = r_factor.shape[0]
    groups = r_factor.shape[1] // WIDTH // plan[0][0]
    shapes = []
    for _, _, taken, positions in plan:
        count = groups if positions is None else len(positions)
        shapes.append(jax.ShapeDtypeStruct((count, rows, taken * WIDTH), jnp.float32))
    return pl.pallas_call(
        functools.partial(gather_kernel, tuple((local, first, positions) for local, first, _, positions in plan)),
        out_shape=tuple(shapes),
        in_specs=[SMEM, SMEM, VMEM],
        out_specs=(VMEM,) * len(shapes),
        compiler_params=PARAMS,
        name="gather",
    )(block_slots, base, r_factor)


def gram(pieces):
    parts = split(jnp.concatenate(pieces, axis=0))
    four = lax.dot_general(parts, parts, (((0,), (0,)), ((), ())), preferred_element_type=jnp.float32)
    half = four[:WIDTH] + four[WIDTH:]
    return half[:, :WIDTH] + half[:, WIDTH:]


def piece(refs, where, pair):
    operand, place = where
    return refs[operand][place, :, pair * WIDTH : (pair + 1) * WIDTH]


def deal(row, held, outs):
    each = outs[0].shape[0]
    for by, out in enumerate(outs):
        out[...] = held[pl.ds(jnp.bitwise_xor(row, by) * each, each)]


def grams_kernel(row, column, *refs):
    outs, held = refs[:-1], refs[-1]
    groups = column.shape[0]
    for pair in range(held.shape[0]):
        held[pair] = gram([piece([column], (0, group), pair) for group in range(groups)])
    deal(row[0], held, outs)


def grams(row, column, shares):
    pairs = column.shape[2] // WIDTH
    return pl.pallas_call(
        grams_kernel,
        out_shape=(jax.ShapeDtypeStruct((pairs // shares, WIDTH, WIDTH), jnp.float32),) * shares,
        in_specs=[SMEM, VMEM],
        out_specs=(VMEM,) * shares,
        scratch_shapes=[pltpu.VMEM((pairs, WIDTH, WIDTH), jnp.float32)],
        compiler_params=PARAMS,
        name="grams",
    )(row, column)


def pack(gram_matrix):
    half = WIDTH // 2
    top = gram_matrix[:half]
    last = pltpu.roll(gram_matrix[half:], half, 1)
    row_ids = lax.broadcasted_iota(jnp.int32, (half, WIDTH), 0)
    col_ids = lax.broadcasted_iota(jnp.int32, (half, WIDTH), 1)
    ends = jnp.sum(jnp.where(row_ids == col_ids, last, 0.0), axis=0, keepdims=True)
    both = jnp.where((col_ids < half) & (row_ids > col_ids), last, top)
    return jnp.concatenate([both, jnp.broadcast_to(ends, (LAST_ROWS, WIDTH))], axis=0)


def unpack(packed):
    half = WIDTH // 2
    both = packed[:half]
    ends = packed[half : half + 1]
    mirrored = jnp.transpose(jnp.concatenate([both, both], axis=0))
    row_ids = lax.broadcasted_iota(jnp.int32, (half, WIDTH), 0)
    col_ids = lax.broadcasted_iota(jnp.int32, (half, WIDTH), 1)
    top = jnp.where((col_ids < half) & (row_ids > col_ids), mirrored[:half], both)
    last = jnp.where(row_ids > col_ids, both, mirrored[:half])
    last = jnp.where(row_ids == col_ids, ends, last)
    bottom = jnp.where(col_ids < half, mirrored[half:], pltpu.roll(last, half, 1))
    return jnp.concatenate([top, bottom], axis=0)


PACKED = WIDTH // 2 + LAST_ROWS


def near_grams_kernel(*refs):
    count = len(refs) // 3
    for place in range(count):
        here, near, out = refs[place], refs[count + place], refs[2 * count + place]
        for pair in range(out.shape[0]):
            out[pair] = pack(gram([piece([ref], (0, 0), pair) for ref in (here, near)]))


def near_grams(here, near):
    pairs = here[0].shape[2] // WIDTH
    return pl.pallas_call(
        near_grams_kernel,
        out_shape=(jax.ShapeDtypeStruct((pairs, PACKED, WIDTH), jnp.float32),) * len(here),
        in_specs=[VMEM] * (2 * len(here)),
        out_specs=(VMEM,) * len(here),
        compiler_params=PARAMS,
        name="near_grams",
    )(*here, *near)


def joined_kernel(*refs):
    half = len(refs) // 3
    for side in range(half):
        for place in range(2):
            refs[2 * half + side][place] = refs[2 * side + place][0]


def joined(*sides):
    _, rows, cols = sides[0][0].shape
    return pl.pallas_call(
        joined_kernel,
        out_shape=(jax.ShapeDtypeStruct((2, rows, cols), jnp.float32),) * len(sides),
        in_specs=[VMEM] * (2 * len(sides)),
        out_specs=(VMEM,) * len(sides),
        compiler_params=PARAMS,
        name="joined",
    )(*[value for side in sides for value in side])


def merge_kernel(count, row, *refs):
    parts, outs, held = refs[:count], refs[count:-1], refs[-1]
    value = parts[0][...]
    for part in parts[1:]:
        value = value + part[...]
    held[...] = value
    deal(row[0], held, outs)


def merge(row, parts, shares):
    pairs, height, _ = parts[0].shape
    return pl.pallas_call(
        functools.partial(merge_kernel, len(parts)),
        out_shape=(jax.ShapeDtypeStruct((pairs // shares, height, WIDTH), jnp.float32),) * shares,
        in_specs=[SMEM] + [VMEM] * len(parts),
        out_specs=(VMEM,) * shares,
        scratch_shapes=[pltpu.VMEM((pairs, height, WIDTH), jnp.float32)],
        compiler_params=PARAMS,
        name="merge",
    )(row, *parts)


def rotation(gram, on_diag, even, odd, power):
    diag_part = jnp.where(on_diag, gram, 0.0)
    across = jnp.sum(diag_part, axis=1, keepdims=True)
    down = jnp.sum(diag_part, axis=0, keepdims=True)
    skew = gram * (across - down) / (2.0 * (across * across + down * down))
    skew_parts = split(skew)
    square = product(skew_parts, skew_parts)
    bound = jnp.sqrt(0.5 * total(square * square))
    scale = 2.0 / (2.0 + bound)
    rate = bound / (2.0 + bound)
    diag_one = jnp.where(on_diag, 1.0, 0.0)
    rest = (1.0 - scale) * diag_one + scale * square
    rest_parts = split(rest)
    size = gram.shape[0]
    first = product(jnp.concatenate([skew_parts, rest_parts], axis=0), rest_parts)
    even_now = scale * (diag_one + rest)
    odd_now = scale * (skew + first[:size])
    rest_parts = split(first[size:])
    second = product(jnp.concatenate([split(even_now), split(odd_now), rest_parts], axis=0), rest_parts)
    even_now = even_now + second[:size]
    odd_now = odd_now + second[size : 2 * size]
    rest_parts = split(second[2 * size :])
    third = product(jnp.concatenate([split(even_now), split(odd_now)], axis=0), rest_parts)
    even[...] = even_now + third[:size]
    odd[...] = odd_now + third[size:]
    power[...] = rest_parts

    def more(left):
        return left > TOLERANCE

    def step(left):
        old = power[...]
        parts = split(product(old, old))
        power[...] = parts
        even[...] += product(split(even[...]), parts)
        odd[...] += product(split(odd[...]), parts)
        return left * left

    rate = rate * rate
    rate = rate * rate
    lax.while_loop(more, step, (rate * rate)[0, 0])
    even_now = 2.0 * even[...] - diag_one
    odd_now = 2.0 * odd[...]
    return split(even_now - odd_now), split(even_now + odd_now)


def solve_kernel(count, *refs):
    parts, out, even, odd, power = refs[:count], *refs[count:]
    on_diag = unit(WIDTH)
    off_total = jnp.zeros((1, 1), jnp.float32)
    diag_total = jnp.zeros((1, 1), jnp.float32)
    for pair in range(parts[0].shape[0]):
        gram = parts[0][pair]
        for part in parts[1:]:
            gram = gram + part[pair]
        if gram.shape[0] != WIDTH:
            gram = unpack(gram)
        squares = gram * gram
        off_total += total(jnp.where(on_diag, 0.0, squares))
        diag_total += total(jnp.where(on_diag, squares, 0.0))
        so_far = None
        for sweep in range(ITERS):
            turn, back = rotation(gram, on_diag, even, odd, power)
            if sweep < ITERS - 1:
                gram = product(back, split(product(split(gram), turn)))
            so_far = turn if so_far is None else split(product(so_far, turn))
        rows = slice(pair * WIDTH, (pair + 1) * WIDTH)
        out[rows] = so_far[:, :WIDTH].astype(jnp.float32) + so_far[:, WIDTH:].astype(jnp.float32)
    first_lane = lax.broadcasted_iota(jnp.int32, (LAST_ROWS, WIDTH), 1) == 0
    out[-LAST_ROWS:] = jnp.where(first_lane, off_total, diag_total)


def solve(parts):
    pairs = parts[0].shape[0]
    return pl.pallas_call(
        functools.partial(solve_kernel, len(parts)),
        out_shape=jax.ShapeDtypeStruct((pairs * WIDTH + LAST_ROWS, WIDTH), jnp.float32),
        in_specs=[VMEM] * len(parts),
        out_specs=VMEM,
        scratch_shapes=[
            pltpu.VMEM((WIDTH, WIDTH), jnp.float32),
            pltpu.VMEM((WIDTH, WIDTH), jnp.float32),
            pltpu.VMEM((WIDTH, 2 * WIDTH), jnp.bfloat16),
        ],
        compiler_params=PARAMS,
        name="solve",
    )(*parts)


def load_turns(where, turns, held):
    count = len(turns)
    each = (turns[0].shape[0] - LAST_ROWS) // WIDTH
    for step in range(count):
        start = jnp.bitwise_xor(where[1], step) * each
        for pair in range(each):
            held[start + pair] = turns[step][pair * WIDTH : (pair + 1) * WIDTH]


def turned(tracks, columns, held):
    results = []
    for pairs, places in tracks:
        for pair in range(pairs):
            value = jnp.concatenate([piece(columns, place, pair) for place in places], axis=0)
            results.append((value, len(results)))
    return lambda index: product(split(results[index][0]), split(held[index]))


def edge_kernel(tracks, count, where, *refs):
    turns, columns = refs[:count], refs[count:-4]
    up, down, sums, held = refs[-4:]
    load_turns(where, turns, held)
    rows = columns[0].shape[1]
    half = rows // 2
    blocks = len(tracks[0][1])
    low_lanes = lax.broadcasted_iota(jnp.int32, (half, WIDTH), 1) < BLOCK
    result = turned(tracks, columns, held)
    last = result(held.shape[0] - 1)
    first = result(0)
    for block in range(blocks):
        span = slice(block * half, (block + 1) * half)
        one = last[block * rows : (block + 1) * rows]
        up[span] = jnp.where(low_lanes, one[:half], pltpu.roll(one[half:], BLOCK, 1))
        one = first[block * rows : (block + 1) * rows]
        down[span] = jnp.where(low_lanes, pltpu.roll(one[:half], BLOCK, 1), one[half:])
    value = turns[0][-LAST_ROWS:]
    for turn in turns[1:]:
        value = value + turn[-LAST_ROWS:]
    sums[...] = value


def edges(tracks, where, columns, turns):
    rows = columns[0].shape[1]
    blocks = len(tracks[0][1])
    pairs = sum(track[0] for track in tracks)
    shape = jax.ShapeDtypeStruct((blocks * rows // 2, WIDTH), jnp.float32)
    return pl.pallas_call(
        functools.partial(edge_kernel, tracks, len(turns)),
        out_shape=(shape, shape, jax.ShapeDtypeStruct((LAST_ROWS, WIDTH), jnp.float32)),
        in_specs=[SMEM] + [VMEM] * (len(turns) + len(columns)),
        out_specs=(VMEM,) * 3,
        scratch_shapes=[pltpu.VMEM((pairs, WIDTH, WIDTH), jnp.float32)],
        compiler_params=PARAMS,
        name="edges",
    )(where, *turns, *columns)


def place_kernel(tracks, count, where, came_up, came_down, *refs):
    turns, columns = refs[:count], refs[count:-2]
    out, held = refs[-2:]
    load_turns(where, turns, held)
    pairs = held.shape[0]
    rows = columns[0].shape[1]
    half = rows // 2
    blocks = len(tracks[0][1])
    is_first = where[0] == 0
    is_last = where[0] == where[2] - 1
    low_lanes = lax.broadcasted_iota(jnp.int32, (rows, WIDTH), 1) < BLOCK
    result = turned(tracks, columns, held)
    rotated = [result(pair) for pair in range(pairs)]
    for block in range(blocks):
        span = slice(block * rows, (block + 1) * rows)
        own_place = jnp.bitwise_xor(where[3], block)
        own_rows = pl.ds(pl.multiple_of(own_place * rows, rows), rows)
        place_up = jnp.bitwise_xor(own_place, where[4])
        place_down = jnp.bitwise_xor(own_place, where[5])
        arrived_up = came_up[pl.ds(pl.multiple_of(place_up * half, half), half)]
        arrived_up = jnp.concatenate([arrived_up, pltpu.roll(arrived_up, BLOCK, 1)], axis=0)
        arrived_down = came_down[pl.ds(pl.multiple_of(place_down * half, half), half)]
        arrived_down = jnp.concatenate([pltpu.roll(arrived_down, BLOCK, 1), arrived_down], axis=0)
        for pair in range(pairs):
            if pair == 0:
                upper = jnp.where(is_first, rotated[0][span], arrived_up)
            else:
                upper = rotated[pair - 1][span]
                if pair == 1:
                    upper = jnp.where(is_first, pltpu.roll(upper, BLOCK, 1), upper)
            if pair == pairs - 1:
                lower = jnp.where(is_last, pltpu.roll(rotated[pair][span], BLOCK, 1), arrived_down)
            else:
                lower = rotated[pair + 1][span]
            out[own_rows, pair * WIDTH : (pair + 1) * WIDTH] = jnp.where(low_lanes, upper, lower)


def place(tracks, where, columns, came_up, came_down, turns):
    rows = columns[0].shape[1]
    blocks = len(tracks[0][1])
    pairs = sum(track[0] for track in tracks)
    return pl.pallas_call(
        functools.partial(place_kernel, tracks, len(turns)),
        out_shape=jax.ShapeDtypeStruct((blocks * rows, pairs * WIDTH), jnp.float32),
        in_specs=[SMEM] + [VMEM] * (2 + len(turns) + len(columns)),
        out_specs=VMEM,
        scratch_shapes=[pltpu.VMEM((pairs, WIDTH, WIDTH), jnp.float32)],
        compiler_params=PARAMS,
        name="place",
    )(where, came_up, came_down, *turns, *columns)


def passed_along(value, axis, by):
    count = lax.axis_size(axis)
    pairs = [(i, i + by) for i in range(count) if 0 <= i + by < count]
    return lax.ppermute(value, axis, pairs)


def swapped(value, axis, by):
    count = lax.axis_size(axis)
    return lax.ppermute(value, axis, [(i, i ^ by) for i in range(count)])


def summed(value, axis, last):
    count = lax.axis_size(axis)
    if count & (count - 1):
        return lax.psum(value, axis), last
    step = 1
    while step < count:
        other = swapped(value, axis, step)
        step *= 2
        if step >= count:
            value, other, last = lax.optimization_barrier((value, other, last))
        value = value + other
    return value, last


def on_device(r_factor, block_slots):
    pair_count = lax.axis_size("pair")
    row_count = lax.axis_size("row")
    pair_index = lax.axis_index("pair")
    row_index = lax.axis_index("row")
    local = r_factor.shape[1] // WIDTH // pair_count
    shared = local % row_count == 0 and row_count & (row_count - 1) == 0
    shares = row_count if shared else 1
    row = (row_index if shared else jnp.zeros_like(row_index)).astype(jnp.int32).reshape(1)
    base = pair_index.astype(jnp.int32).reshape(1)
    if shared and pair_count == 8:
        plan = [(local, 0, local, (position,)) for position in range(pair_count)]
        arranged = gather(r_factor, block_slots, base, tuple(plan))
        here = arranged[0::2]
        near = [swapped(value, "pair", 1) for value in arranged[1::2]]
        here_two = swapped(here[1], "pair", 2)
        here_four = swapped(here[2], "pair", 4)
        own, *given = near_grams(here, near)
        taken = [swapped(value, "pair", by) for by, value in zip((2, 4, 6), given)]
        on_two, on_four = joined((near[1], here[3]), (near[2], near[3]))
        here_two, here_four, on_two, on_four, taken = lax.optimization_barrier((here_two, here_four, on_two, on_four, taken))
        parts = merge(row, [own] + taken, shares)
        from_two = swapped(on_two, "pair", 2)
        from_four = swapped(on_four, "pair", 4)
        tracks = ((local, tuple((position, 0) for position in range(pair_count))),)
        bases = (pair_index, pair_index - 1, pair_index + 1)
    else:
        (arranged,) = gather(r_factor, block_slots, base, ((local, 0, local, None),))
        column = lax.all_to_all(arranged, "pair", split_axis=0, concat_axis=0, tiled=True)
        parts = grams(row, column, shares)
        columns = (column,)
        tracks = ((local, tuple((0, group) for group in range(pair_count))),)
        bases = (jnp.zeros_like(pair_index),) * 3
    if shared:
        turn = solve([parts[0]] + [swapped(parts[by], "row", by) for by in range(1, row_count)])
        if pair_count == 8:
            from_two, from_four, turn = lax.optimization_barrier((from_two, from_four, turn))
            here_six = swapped(from_two[1:], "pair", 4)
            near_six = swapped(from_four[1:], "pair", 2)
            columns = (here[0], near[0], here_two, from_two, here_four, from_four, here_six, near_six)
        turns = [turn] + [swapped(turn, "row", by) for by in range(1, row_count)]
    else:
        turns = [solve([lax.psum(parts[0], "row")])]
    bases = [jnp.clip(value, 0, pair_count - 1) for value in bases]
    where = jnp.stack([pair_index, row[0], jnp.int32(pair_count)] + bases).astype(jnp.int32)
    up, down, sums = edges(tracks, where, columns, turns)
    came_up = passed_along(up, "pair", 1)
    came_down = passed_along(down, "pair", -1)
    rotated = place(tracks, where, columns, came_up, came_down, turns)
    sums, rotated = summed(sums, "pair", rotated)
    off_ratio = jnp.sqrt(sums[0, 0] / sums[0, 1])
    return (rotated, off_ratio)


def solution(mesh):
    in_specs = (P(("row", "pair"), None), P())
    out_specs = (P("row", "pair"), P())
    return jax.shard_map(
        on_device, mesh=mesh, in_specs=in_specs, out_specs=out_specs, check_vma=False
    )
```

```python
import functools

import jax
import jax.numpy as jnp
from jax import lax
from jax.experimental import pallas as pl
from jax.experimental.pallas import tpu as pltpu
from jax.sharding import PartitionSpec as P

BLOCK = 64
WIDTH = 2 * BLOCK
ITERS = 3
TOLERANCE = 1e-8
LAST_ROWS = 8
VMEM = pl.BlockSpec(memory_space=pltpu.VMEM)
SMEM = pl.BlockSpec(memory_space=pltpu.SMEM)
PARAMS = pltpu.CompilerParams(vmem_limit_bytes=48 * 1024 * 1024)


def split(value):
    high = value.astype(jnp.bfloat16)
    low = (value - high.astype(jnp.float32)).astype(jnp.bfloat16)
    return jnp.concatenate([high, low], axis=1)


def product(left, right):
    both = jnp.dot(left, jnp.concatenate([right, right], axis=0), preferred_element_type=jnp.float32)
    half = both.shape[1] // 2
    return both[:, :half] + both[:, half:]


def unit(size):
    row_ids = lax.broadcasted_iota(jnp.int32, (size, size), 0)
    col_ids = lax.broadcasted_iota(jnp.int32, (size, size), 1)
    return row_ids == col_ids


def total(value):
    return jnp.sum(jnp.sum(value, axis=1, keepdims=True), axis=0, keepdims=True)


def gather_kernel(plan, slots, base, source, *outs):
    rows = source.shape[0]
    local = plan[0][0]
    low_lanes = lax.broadcasted_iota(jnp.int32, (rows, WIDTH), 1) < BLOCK

    def tile(block, lane_half):
        start = pl.multiple_of((block // 2) * WIDTH, WIDTH)
        value = source[:, pl.ds(start, WIDTH)]
        return jnp.where(block % 2 == lane_half, value, pltpu.roll(value, BLOCK, 1))

    for (_, first, positions), out in zip(plan, outs):
        count = out.shape[2] // WIDTH

        def one(group, place, first=first, count=count, out=out):
            for pair in range(count):
                slot = 2 * (group * local + first + pair)
                upper = tile(slots[slot], 0)
                lower = tile(slots[slot + 1], 1)
                out[place, :, pair * WIDTH : (pair + 1) * WIDTH] = jnp.where(low_lanes, upper, lower)

        if positions is None:

            def step(group, carry, one=one):
                one(group, group)
                return carry

            lax.fori_loop(0, out.shape[0], step, 0)
        else:
            for place, position in enumerate(positions):
                one(jnp.bitwise_xor(base[0], position), place)


def gather(r_factor, block_slots, base, plan):
    rows = r_factor.shape[0]
    groups = r_factor.shape[1] // WIDTH // plan[0][0]
    shapes = []
    for _, _, taken, positions in plan:
        count = groups if positions is None else len(positions)
        shapes.append(jax.ShapeDtypeStruct((count, rows, taken * WIDTH), jnp.float32))
    return pl.pallas_call(
        functools.partial(gather_kernel, tuple((local, first, positions) for local, first, _, positions in plan)),
        out_shape=tuple(shapes),
        in_specs=[SMEM, SMEM, VMEM],
        out_specs=(VMEM,) * len(shapes),
        compiler_params=PARAMS,
        name="gather",
    )(block_slots, base, r_factor)


def gram(pieces):
    parts = split(jnp.concatenate(pieces, axis=0))
    four = lax.dot_general(parts, parts, (((0,), (0,)), ((), ())), preferred_element_type=jnp.float32)
    half = four[:WIDTH] + four[WIDTH:]
    return half[:, :WIDTH] + half[:, WIDTH:]


def piece(refs, where, pair):
    operand, place = where
    return refs[operand][place, :, pair * WIDTH : (pair + 1) * WIDTH]


def deal(row, held, outs):
    each = outs[0].shape[0]
    for by, out in enumerate(outs):
        out[...] = held[pl.ds(jnp.bitwise_xor(jnp.bitwise_and(row, len(outs) - 1), by) * each, each)]


def grams_kernel(row, column, *refs):
    outs, held = refs[:-1], refs[-1]
    groups = column.shape[0]
    for pair in range(held.shape[0]):
        held[pair] = gram([piece([column], (0, group), pair) for group in range(groups)])
    deal(row[0], held, outs)


def grams(row, column, shares):
    pairs = column.shape[2] // WIDTH
    return pl.pallas_call(
        grams_kernel,
        out_shape=(jax.ShapeDtypeStruct((pairs // shares, WIDTH, WIDTH), jnp.float32),) * shares,
        in_specs=[SMEM, VMEM],
        out_specs=(VMEM,) * shares,
        scratch_shapes=[pltpu.VMEM((pairs, WIDTH, WIDTH), jnp.float32)],
        compiler_params=PARAMS,
        name="grams",
    )(row, column)


def pack(gram_matrix):
    half = WIDTH // 2
    top = gram_matrix[:half]
    last = pltpu.roll(gram_matrix[half:], half, 1)
    row_ids = lax.broadcasted_iota(jnp.int32, (half, WIDTH), 0)
    col_ids = lax.broadcasted_iota(jnp.int32, (half, WIDTH), 1)
    ends = jnp.sum(jnp.where(row_ids == col_ids, last, 0.0), axis=0, keepdims=True)
    both = jnp.where((col_ids < half) & (row_ids > col_ids), last, top)
    return jnp.concatenate([both, jnp.broadcast_to(ends, (LAST_ROWS, WIDTH))], axis=0)


def unpack(packed):
    half = WIDTH // 2
    both = packed[:half]
    ends = packed[half : half + 1]
    mirrored = jnp.transpose(jnp.concatenate([both, both], axis=0))
    row_ids = lax.broadcasted_iota(jnp.int32, (half, WIDTH), 0)
    col_ids = lax.broadcasted_iota(jnp.int32, (half, WIDTH), 1)
    top = jnp.where((col_ids < half) & (row_ids > col_ids), mirrored[:half], both)
    last = jnp.where(row_ids > col_ids, both, mirrored[:half])
    last = jnp.where(row_ids == col_ids, ends, last)
    bottom = jnp.where(col_ids < half, mirrored[half:], pltpu.roll(last, half, 1))
    return jnp.concatenate([top, bottom], axis=0)


PACKED = WIDTH // 2 + LAST_ROWS


def near_grams_kernel(*refs):
    count = len(refs) // 3
    for place in range(count):
        here, near, out = refs[place], refs[count + place], refs[2 * count + place]
        for pair in range(out.shape[0]):
            out[pair] = pack(gram([piece([ref], (0, 0), pair) for ref in (here, near)]))


def near_grams(here, near):
    pairs = here[0].shape[2] // WIDTH
    return pl.pallas_call(
        near_grams_kernel,
        out_shape=(jax.ShapeDtypeStruct((pairs, PACKED, WIDTH), jnp.float32),) * len(here),
        in_specs=[VMEM] * (2 * len(here)),
        out_specs=(VMEM,) * len(here),
        compiler_params=PARAMS,
        name="near_grams",
    )(*here, *near)


def joined_kernel(*refs):
    half = len(refs) // 3
    for side in range(half):
        for place in range(2):
            refs[2 * half + side][place] = refs[2 * side + place][0]


def joined(*sides):
    _, rows, cols = sides[0][0].shape
    return pl.pallas_call(
        joined_kernel,
        out_shape=(jax.ShapeDtypeStruct((2, rows, cols), jnp.float32),) * len(sides),
        in_specs=[VMEM] * (2 * len(sides)),
        out_specs=(VMEM,) * len(sides),
        compiler_params=PARAMS,
        name="joined",
    )(*[value for side in sides for value in side])


def merge_kernel(count, row, *refs):
    parts, outs, held = refs[:count], refs[count:-1], refs[-1]
    value = parts[0][...]
    for part in parts[1:]:
        value = value + part[...]
    held[...] = value
    deal(row[0], held, outs)


def merge(row, parts, shares):
    pairs, height, _ = parts[0].shape
    return pl.pallas_call(
        functools.partial(merge_kernel, len(parts)),
        out_shape=(jax.ShapeDtypeStruct((pairs // shares, height, WIDTH), jnp.float32),) * shares,
        in_specs=[SMEM] + [VMEM] * len(parts),
        out_specs=(VMEM,) * shares,
        scratch_shapes=[pltpu.VMEM((pairs, height, WIDTH), jnp.float32)],
        compiler_params=PARAMS,
        name="merge",
    )(row, *parts)


def rotations(grams_now, on_diag, even, odd, power):
    diag_one = jnp.where(on_diag, 1.0, 0.0)
    size = diag_one.shape[0]
    skews, skews_parts, squares = [], [], []
    for gram_now in grams_now:
        diag_part = jnp.where(on_diag, gram_now, 0.0)
        across = jnp.sum(diag_part, axis=1, keepdims=True)
        down = jnp.sum(diag_part, axis=0, keepdims=True)
        skews.append(gram_now * (across - down) / (2.0 * (across * across + down * down)))
    for skew in skews:
        skews_parts.append(split(skew))
        squares.append(product(skews_parts[-1], skews_parts[-1]))
    evens, odds, rests, worst = [], [], [], None
    for skew, parts, square in zip(skews, skews_parts, squares):
        bound = jnp.sqrt(0.5 * total(square * square))
        scale = 2.0 / (2.0 + bound)
        rate = bound / (2.0 + bound)
        worst = rate if worst is None else jnp.maximum(worst, rate)
        rest = (1.0 - scale) * diag_one + scale * square
        rest_parts = split(rest)
        first = product(jnp.concatenate([parts, rest_parts], axis=0), rest_parts)
        evens.append(scale * (diag_one + rest))
        odds.append(scale * (skew + first[:size]))
        rests.append(split(first[size:]))
    for index, rest_parts in enumerate(rests):
        stack = jnp.concatenate([split(evens[index]), split(odds[index]), rest_parts], axis=0)
        second = product(stack, rest_parts)
        evens[index] = evens[index] + second[:size]
        odds[index] = odds[index] + second[size : 2 * size]
        rests[index] = split(second[2 * size :])
    for index, rest_parts in enumerate(rests):
        third = product(jnp.concatenate([split(evens[index]), split(odds[index])], axis=0), rest_parts)
        even[index] = evens[index] + third[:size]
        odd[index] = odds[index] + third[size:]
        power[index] = rest_parts

    def more(left):
        return left > TOLERANCE

    def step(left):
        for index in range(len(grams_now)):
            old = power[index]
            parts = split(product(old, old))
            power[index] = parts
            even[index] += product(split(even[index]), parts)
            odd[index] += product(split(odd[index]), parts)
        return left * left

    worst = worst * worst
    worst = worst * worst
    lax.while_loop(more, step, (worst * worst)[0, 0])
    results = []
    for index in range(len(grams_now)):
        even_now = 2.0 * even[index] - diag_one
        odd_now = 2.0 * odd[index]
        results.append((split(even_now - odd_now), split(even_now + odd_now)))
    return results


def solve_kernel(count, row, *refs):
    parts, out, sums, held, even, odd, power = refs[:count], *refs[count:]
    on_diag = unit(WIDTH)
    pairs = range(out.shape[0])
    each = parts[0].shape[0]
    for by, part in enumerate(parts):
        held[pl.ds(jnp.bitwise_xor(jnp.bitwise_and(row[0], count - 1), by) * each, each)] = part[...]
    off_total = jnp.zeros((1, 1), jnp.float32)
    diag_total = jnp.zeros((1, 1), jnp.float32)
    now = []
    for pair in pairs:
        gram_now = held[pair]
        if gram_now.shape[0] != WIDTH:
            gram_now = unpack(gram_now)
        squares = gram_now * gram_now
        off_total += total(jnp.where(on_diag, 0.0, squares))
        diag_total += total(jnp.where(on_diag, squares, 0.0))
        now.append(gram_now)
    first_lane = lax.broadcasted_iota(jnp.int32, sums.shape, 1) == 0
    sums[...] = jnp.where(first_lane, off_total, diag_total)
    so_far = None
    for sweep in range(ITERS):
        turns = rotations(now, on_diag, even, odd, power)
        if sweep < ITERS - 1:
            halves = [split(product(split(now[pair]), turns[pair][0])) for pair in pairs]
            now = [product(turns[pair][1], halves[pair]) for pair in pairs]
        if so_far is None:
            so_far = [turns[pair][0] for pair in pairs]
        elif sweep < ITERS - 1:
            so_far = [split(product(so_far[pair], turns[pair][0])) for pair in pairs]
        else:
            for pair in pairs:
                out[pair] = product(so_far[pair], turns[pair][0])


def solve(row, parts):
    each, height, _ = parts[0].shape
    pairs = each * len(parts)
    return pl.pallas_call(
        functools.partial(solve_kernel, len(parts)),
        out_shape=(
            jax.ShapeDtypeStruct((pairs, WIDTH, WIDTH), jnp.float32),
            jax.ShapeDtypeStruct((LAST_ROWS, WIDTH), jnp.float32),
        ),
        in_specs=[SMEM] + [VMEM] * len(parts),
        out_specs=(VMEM, VMEM),
        scratch_shapes=[
            pltpu.VMEM((pairs, height, WIDTH), jnp.float32),
            pltpu.VMEM((pairs, WIDTH, WIDTH), jnp.float32),
            pltpu.VMEM((pairs, WIDTH, WIDTH), jnp.float32),
            pltpu.VMEM((pairs, WIDTH, 2 * WIDTH), jnp.bfloat16),
        ],
        compiler_params=PARAMS,
        name="solve",
    )(row, *parts)


def turned(tracks, columns, held):
    results = []
    for pairs, places in tracks:
        for pair in range(pairs):
            value = jnp.concatenate([piece(columns, place, pair) for place in places], axis=0)
            results.append((value, len(results)))
    return lambda index: product(split(results[index][0]), split(held[index]))


def edge_kernel(tracks, where, sums, held, *refs):
    columns, near, far = refs[:-2], refs[-2], refs[-1]
    odd = lax.rem(where[0], 2) == 1
    rows = columns[0].shape[1]
    half = rows // 2
    blocks = len(tracks[0][1])
    low_lanes = lax.broadcasted_iota(jnp.int32, (half, WIDTH), 1) < BLOCK
    result = turned(tracks, columns, held)
    last = result(held.shape[0] - 1)
    first = result(0)
    for block in range(blocks):
        span = slice(block * half, (block + 1) * half)
        one = last[block * rows : (block + 1) * rows]
        up = jnp.where(low_lanes, one[:half], pltpu.roll(one[half:], BLOCK, 1))
        one = first[block * rows : (block + 1) * rows]
        down = jnp.where(low_lanes, pltpu.roll(one[:half], BLOCK, 1), one[half:])
        near[span] = jnp.where(odd, down, up)
        far[span] = jnp.where(odd, up, down)
    near[-LAST_ROWS:] = sums[...]


def edges(tracks, where, sums, columns, turns):
    half = len(tracks[0][1]) * columns[0].shape[1] // 2
    return pl.pallas_call(
        functools.partial(edge_kernel, tracks),
        out_shape=tuple(jax.ShapeDtypeStruct((height, WIDTH), jnp.float32) for height in (half + LAST_ROWS, half)),
        in_specs=[SMEM] + [VMEM] * (2 + len(columns)),
        out_specs=(VMEM,) * 2,
        compiler_params=PARAMS,
        name="edges",
    )(where, sums, turns, *columns)


def place_kernel(tracks, where, near, far, held, *refs):
    columns, out = refs[:-1], refs[-1]
    pairs = held.shape[0]
    rows = columns[0].shape[1]
    half = rows // 2
    blocks = len(tracks[0][1])
    odd = lax.rem(where[0], 2) == 1
    is_first = where[0] == 0
    is_last = where[0] == where[1] - 1
    low_lanes = lax.broadcasted_iota(jnp.int32, (rows, WIDTH), 1) < BLOCK
    result = turned(tracks, columns, held)
    rotated = [result(pair) for pair in range(pairs)]
    for block in range(blocks):
        span = slice(block * rows, (block + 1) * rows)
        own_place = jnp.bitwise_xor(where[2], block)
        own_rows = pl.ds(pl.multiple_of(own_place * rows, rows), rows)
        place_up = jnp.bitwise_xor(own_place, where[3])
        place_down = jnp.bitwise_xor(own_place, where[4])
        span_up = pl.ds(pl.multiple_of(place_up * half, half), half)
        arrived_up = jnp.where(odd, near[span_up], far[span_up])
        arrived_up = jnp.concatenate([arrived_up, pltpu.roll(arrived_up, BLOCK, 1)], axis=0)
        span_down = pl.ds(pl.multiple_of(place_down * half, half), half)
        arrived_down = jnp.where(odd, far[span_down], near[span_down])
        arrived_down = jnp.concatenate([pltpu.roll(arrived_down, BLOCK, 1), arrived_down], axis=0)
        for pair in range(pairs):
            if pair == 0:
                upper = jnp.where(is_first, rotated[0][span], arrived_up)
            else:
                upper = rotated[pair - 1][span]
                if pair == 1:
                    upper = jnp.where(is_first, pltpu.roll(upper, BLOCK, 1), upper)
            if pair == pairs - 1:
                lower = jnp.where(is_last, pltpu.roll(rotated[pair][span], BLOCK, 1), arrived_down)
            else:
                lower = rotated[pair + 1][span]
            out[own_rows, pair * WIDTH : (pair + 1) * WIDTH] = jnp.where(low_lanes, upper, lower)


def place(tracks, where, columns, near, far, turns):
    rows = columns[0].shape[1]
    blocks = len(tracks[0][1])
    pairs = sum(track[0] for track in tracks)
    return pl.pallas_call(
        functools.partial(place_kernel, tracks),
        out_shape=jax.ShapeDtypeStruct((blocks * rows, pairs * WIDTH), jnp.float32),
        in_specs=[SMEM] + [VMEM] * (3 + len(columns)),
        out_specs=VMEM,
        compiler_params=PARAMS,
        name="place",
    )(where, near, far, turns, *columns)


def swapped_in_twos(value, axis, first):
    pairs = []
    for i in range(first, lax.axis_size(axis) - 1, 2):
        pairs += [(i, i + 1), (i + 1, i)]
    return lax.ppermute(value, axis, pairs)


def swapped(value, axis, by):
    count = lax.axis_size(axis)
    return lax.ppermute(value, axis, [(i, i ^ by) for i in range(count)])


def on_device(r_factor, block_slots):
    pair_count = lax.axis_size("pair")
    row_count = lax.axis_size("row")
    pair_index = lax.axis_index("pair")
    row_index = lax.axis_index("row")
    local = r_factor.shape[1] // WIDTH // pair_count
    shared = local % 2 == 0 and row_count > 1 and row_count & (row_count - 1) == 0
    shares = 2 if shared else 1
    row = row_index.astype(jnp.int32).reshape(1)
    base = pair_index.astype(jnp.int32).reshape(1)
    if shared and pair_count == 8:
        plan = [(local, 0, local, (position,)) for position in range(pair_count)]
        arranged = gather(r_factor, block_slots, base, tuple(plan))
        here = arranged[0::2]
        near = [swapped(value, "pair", 1) for value in arranged[1::2]]
        here_two = swapped(here[1], "pair", 2)
        here_four = swapped(here[2], "pair", 4)
        own, *given = near_grams(here, near)
        taken = [swapped(value, "pair", by) for by, value in zip((2, 4, 6), given)]
        (on_six,) = joined((here[3], near[3]))
        here_two, here_four, on_six, taken = lax.optimization_barrier((here_two, here_four, on_six, taken))
        parts = merge(row, [own] + taken, shares)
        from_six = swapped(on_six, "pair", 6)
        tracks = ((local, tuple((position, 0) for position in range(pair_count - 1)) + ((pair_count - 2, 1),)),)
        bases = (pair_index, pair_index - 1, pair_index + 1)
    else:
        (arranged,) = gather(r_factor, block_slots, base, ((local, 0, local, None),))
        column = lax.all_to_all(arranged, "pair", split_axis=0, concat_axis=0, tiled=True)
        parts = grams(row, column, shares)
        columns = (column,)
        tracks = ((local, tuple((0, group) for group in range(pair_count))),)
        bases = (jnp.zeros_like(pair_index),) * 3
    if shared:
        half = parts[0] + swapped(parts[1], "row", 1)
        if pair_count == 8:
            near_two, near_four, half = lax.optimization_barrier((near[1], near[2], half))
            near_two = swapped(near_two, "pair", 2)
            near_four = swapped(near_four, "pair", 4)
            columns = (here[0], near[0], here_two, near_two, here_four, near_four, from_six)
        for bit in range(1, row_count.bit_length() - 1):
            half = half + swapped(half, "row", 1 << bit)
        parts = (half, swapped(half, "row", 1))
    else:
        parts = (lax.psum(parts[0], "row"),)
    turns, sums = solve(row, parts)
    bases = [jnp.clip(value, 0, pair_count - 1) for value in bases]
    where = jnp.stack([pair_index, jnp.int32(pair_count)] + bases).astype(jnp.int32)
    near, far = edges(tracks, where, sums, columns, turns)
    far = swapped_in_twos(far, "pair", 1)
    near = swapped_in_twos(near, "pair", 0)
    rotated = place(tracks, where, columns, near, far, turns)
    if pair_count == 8:
        sums = sums + near[-LAST_ROWS:]
        others = [swapped(sums, "pair", by) for by in (2, 4, 6)]
        others, rotated = lax.optimization_barrier((others, rotated))
        for other in others:
            sums = sums + other
    else:
        sums = lax.psum(sums, "pair")
    off_ratio = jnp.sqrt(sums[0, 0] / sums[0, 1])
    return (rotated, off_ratio)


def solution(mesh):
    in_specs = (P(("row", "pair"), None), P())
    out_specs = (P("row", "pair"), P())
    return jax.shard_map(
        on_device, mesh=mesh, in_specs=in_specs, out_specs=out_specs, check_vma=False
    )
```

```python
import functools

import jax
import jax.numpy as jnp
from jax import lax
from jax.experimental import pallas as pl
from jax.experimental.pallas import tpu as pltpu
from jax.sharding import PartitionSpec as P

BLOCK = 64
WIDTH = 2 * BLOCK
ITERS = 3
TOLERANCE = 1e-8
LAST_ROWS = 8
GATHER_CHUNKS = 2
GATHER_VMEM = 62 * 1024 * 1024
VMEM = pl.BlockSpec(memory_space=pltpu.VMEM)
SMEM = pl.BlockSpec(memory_space=pltpu.SMEM)
HBM = pl.BlockSpec(memory_space=pltpu.HBM)
PARAMS = pltpu.CompilerParams(vmem_limit_bytes=48 * 1024 * 1024)


def split(value):
    high = value.astype(jnp.bfloat16)
    low = (value - high.astype(jnp.float32)).astype(jnp.bfloat16)
    return jnp.concatenate([high, low], axis=1)


def product(left, right):
    both = jnp.dot(left, jnp.concatenate([right, right], axis=0), preferred_element_type=jnp.float32)
    half = both.shape[1] // 2
    return both[:, :half] + both[:, half:]


def unit(size):
    row_ids = lax.broadcasted_iota(jnp.int32, (size, size), 0)
    col_ids = lax.broadcasted_iota(jnp.int32, (size, size), 1)
    return row_ids == col_ids


def total(value):
    return jnp.sum(jnp.sum(value, axis=1, keepdims=True), axis=0, keepdims=True)


def gather_kernel(plan, slots, source, *outs):
    rows = source.shape[0]
    local = plan[0][0]
    base = slots[slots.shape[0] - 1]
    low_lanes = lax.broadcasted_iota(jnp.int32, (rows, WIDTH), 1) < BLOCK

    def tile(block):
        return source[:, pl.ds(pl.multiple_of(lax.shift_right_logical(block, 1) * WIDTH, WIDTH), WIDTH)]

    def one_pair(slot):
        upper_block, lower_block = slots[slot], slots[slot + 1]
        upper, lower = tile(upper_block), tile(lower_block)
        turned_over = pltpu.roll(jnp.where(low_lanes, lower, upper), BLOCK, 1)
        upper = jnp.where(jnp.bitwise_and(upper_block, 1) == 0, upper, turned_over)
        lower = jnp.where(jnp.bitwise_and(lower_block, 1) == 1, lower, turned_over)
        return jnp.where(low_lanes, upper, lower)

    for (_, first, positions), out in zip(plan, outs):
        count = out.shape[2] // WIDTH

        def one_group(group, place, first=first, count=count, out=out):
            for pair in range(count):
                value = one_pair(2 * (group * local + first + pair))
                out[place, :, pair * WIDTH : (pair + 1) * WIDTH] = value

        if positions is None:

            def step(group, carry, one_group=one_group):
                one_group(group, group)
                return carry

            lax.fori_loop(0, out.shape[0], step, 0)
        else:
            for place, position in enumerate(positions):
                one_group(jnp.bitwise_xor(base, position), place)


def gather(r_factor, block_slots, base, plan):
    rows = r_factor.shape[0]
    groups = r_factor.shape[1] // WIDTH // plan[0][0]
    shapes = []
    for _, _, taken, positions in plan:
        count = groups if positions is None else len(positions)
        shapes.append(jax.ShapeDtypeStruct((count, rows, taken * WIDTH), jnp.float32))
    return pl.pallas_call(
        functools.partial(gather_kernel, tuple((local, first, positions) for local, first, _, positions in plan)),
        out_shape=tuple(shapes),
        in_specs=[SMEM, VMEM],
        out_specs=(VMEM,) * len(shapes),
        compiler_params=PARAMS,
        name="gather",
    )(jnp.concatenate([block_slots, base]), r_factor)


def gram(pieces):
    parts = split(jnp.concatenate(pieces, axis=0))
    four = lax.dot_general(parts, parts, (((0,), (0,)), ((), ())), preferred_element_type=jnp.float32)
    half = four[:WIDTH] + four[WIDTH:]
    return half[:, :WIDTH] + half[:, WIDTH:]


def piece(refs, where, pair):
    operand, place = where
    return refs[operand][place, :, pair * WIDTH : (pair + 1) * WIDTH]


def deal(row, held, outs):
    each = outs[0].shape[0]
    for by, out in enumerate(outs):
        out[...] = held[pl.ds(jnp.bitwise_xor(jnp.bitwise_and(row, len(outs) - 1), by) * each, each)]


def grams_kernel(row, column, *refs):
    outs, held = refs[:-1], refs[-1]
    groups = column.shape[0]
    for pair in range(held.shape[0]):
        held[pair] = gram([piece([column], (0, group), pair) for group in range(groups)])
    deal(row[0], held, outs)


def grams(row, column, shares):
    pairs = column.shape[2] // WIDTH
    return pl.pallas_call(
        grams_kernel,
        out_shape=(jax.ShapeDtypeStruct((pairs // shares, WIDTH, WIDTH), jnp.float32),) * shares,
        in_specs=[SMEM, VMEM],
        out_specs=(VMEM,) * shares,
        scratch_shapes=[pltpu.VMEM((pairs, WIDTH, WIDTH), jnp.float32)],
        compiler_params=PARAMS,
        name="grams",
    )(row, column)


def pack(gram_matrix):
    half = WIDTH // 2
    top = gram_matrix[:half]
    last = pltpu.roll(gram_matrix[half:], half, 1)
    row_ids = lax.broadcasted_iota(jnp.int32, (half, WIDTH), 0)
    col_ids = lax.broadcasted_iota(jnp.int32, (half, WIDTH), 1)
    ends = jnp.sum(jnp.where(row_ids == col_ids, last, 0.0), axis=0, keepdims=True)
    both = jnp.where((col_ids < half) & (row_ids > col_ids), last, top)
    return jnp.concatenate([both, jnp.broadcast_to(ends, (LAST_ROWS, WIDTH))], axis=0)


def unpack(packed):
    half = WIDTH // 2
    both = packed[:half]
    ends = packed[half : half + 1]
    mirrored = jnp.transpose(jnp.concatenate([both, both], axis=0))
    row_ids = lax.broadcasted_iota(jnp.int32, (half, WIDTH), 0)
    col_ids = lax.broadcasted_iota(jnp.int32, (half, WIDTH), 1)
    top = jnp.where((col_ids < half) & (row_ids > col_ids), mirrored[:half], both)
    last = jnp.where(row_ids > col_ids, both, mirrored[:half])
    last = jnp.where(row_ids == col_ids, ends, last)
    bottom = jnp.where(col_ids < half, mirrored[half:], pltpu.roll(last, half, 1))
    return jnp.concatenate([top, bottom], axis=0)


PACKED = WIDTH // 2 + LAST_ROWS


def near_grams_kernel(*refs):
    count = len(refs) // 3
    for place in range(count):
        here, near, out = refs[place], refs[count + place], refs[2 * count + place]
        for pair in range(out.shape[0]):
            out[pair] = pack(gram([piece([ref], (0, 0), pair) for ref in (here, near)]))


def near_grams(here, near):
    pairs = here[0].shape[2] // WIDTH
    return pl.pallas_call(
        near_grams_kernel,
        out_shape=(jax.ShapeDtypeStruct((pairs, PACKED, WIDTH), jnp.float32),) * len(here),
        in_specs=[VMEM] * (2 * len(here)),
        out_specs=(VMEM,) * len(here),
        compiler_params=PARAMS,
        name="near_grams",
    )(*here, *near)


def joined_kernel(*refs):
    half = len(refs) // 3
    for side in range(half):
        for place in range(2):
            refs[2 * half + side][place] = refs[2 * side + place][0]


def joined(*sides):
    _, rows, cols = sides[0][0].shape
    return pl.pallas_call(
        joined_kernel,
        out_shape=(jax.ShapeDtypeStruct((2, rows, cols), jnp.float32),) * len(sides),
        in_specs=[VMEM] * (2 * len(sides)),
        out_specs=(VMEM,) * len(sides),
        compiler_params=PARAMS,
        name="joined",
    )(*[value for side in sides for value in side])


def merge_kernel(count, row, *refs):
    parts, outs, held = refs[:count], refs[count:-1], refs[-1]
    value = parts[0][...]
    for part in parts[1:]:
        value = value + part[...]
    held[...] = value
    deal(row[0], held, outs)


def merge(row, parts, shares):
    pairs, height, _ = parts[0].shape
    return pl.pallas_call(
        functools.partial(merge_kernel, len(parts)),
        out_shape=(jax.ShapeDtypeStruct((pairs // shares, height, WIDTH), jnp.float32),) * shares,
        in_specs=[SMEM] + [VMEM] * len(parts),
        out_specs=(VMEM,) * shares,
        scratch_shapes=[pltpu.VMEM((pairs, height, WIDTH), jnp.float32)],
        compiler_params=PARAMS,
        name="merge",
    )(row, *parts)


def rotations(grams_now, on_diag, even, odd, power):
    diag_one = jnp.where(on_diag, 1.0, 0.0)
    size = diag_one.shape[0]
    skews, skews_parts, squares = [], [], []
    for gram_now in grams_now:
        diag_part = jnp.where(on_diag, gram_now, 0.0)
        across = jnp.sum(diag_part, axis=1, keepdims=True)
        down = jnp.sum(diag_part, axis=0, keepdims=True)
        skews.append(gram_now * (across - down) / (2.0 * (across * across + down * down)))
    for skew in skews:
        skews_parts.append(split(skew))
        squares.append(product(skews_parts[-1], skews_parts[-1]))
    evens, odds, rests, worst = [], [], [], None
    for skew, parts, square in zip(skews, skews_parts, squares):
        bound = jnp.sqrt(0.5 * total(square * square))
        scale = 2.0 / (2.0 + bound)
        rate = bound / (2.0 + bound)
        worst = rate if worst is None else jnp.maximum(worst, rate)
        rest = (1.0 - scale) * diag_one + scale * square
        rest_parts = split(rest)
        first = product(jnp.concatenate([parts, rest_parts], axis=0), rest_parts)
        evens.append(scale * (diag_one + rest))
        odds.append(scale * (skew + first[:size]))
        rests.append(split(first[size:]))
    for index, rest_parts in enumerate(rests):
        stack = jnp.concatenate([split(evens[index]), split(odds[index]), rest_parts], axis=0)
        second = product(stack, rest_parts)
        evens[index] = evens[index] + second[:size]
        odds[index] = odds[index] + second[size : 2 * size]
        rests[index] = split(second[2 * size :])
    for index, rest_parts in enumerate(rests):
        third = product(jnp.concatenate([split(evens[index]), split(odds[index])], axis=0), rest_parts)
        even[index] = evens[index] + third[:size]
        odd[index] = odds[index] + third[size:]
        power[index] = rest_parts

    def more(left):
        return left > TOLERANCE

    def step(left):
        for index in range(len(grams_now)):
            old = power[index]
            parts = split(product(old, old))
            power[index] = parts
            even[index] += product(split(even[index]), parts)
            odd[index] += product(split(odd[index]), parts)
        return left * left

    worst = worst * worst
    worst = worst * worst
    lax.while_loop(more, step, (worst * worst)[0, 0])
    results = []
    for index in range(len(grams_now)):
        even_now = 2.0 * even[index] - diag_one
        odd_now = 2.0 * odd[index]
        results.append((split(even_now - odd_now), split(even_now + odd_now)))
    return results


def solve_kernel(count, row, *refs):
    parts, out, sums, held, even, odd, power = refs[:count], *refs[count:]
    on_diag = unit(WIDTH)
    pairs = range(out.shape[0])
    each = parts[0].shape[0]
    for by, part in enumerate(parts):
        held[pl.ds(jnp.bitwise_xor(jnp.bitwise_and(row[0], count - 1), by) * each, each)] = part[...]
    off_total = jnp.zeros((1, 1), jnp.float32)
    diag_total = jnp.zeros((1, 1), jnp.float32)
    now = []
    for pair in pairs:
        gram_now = held[pair]
        if gram_now.shape[0] != WIDTH:
            gram_now = unpack(gram_now)
        squares = gram_now * gram_now
        off_total += total(jnp.where(on_diag, 0.0, squares))
        diag_total += total(jnp.where(on_diag, squares, 0.0))
        now.append(gram_now)
    first_lane = lax.broadcasted_iota(jnp.int32, sums.shape, 1) == 0
    sums[...] = jnp.where(first_lane, off_total, diag_total)
    so_far = None
    for sweep in range(ITERS):
        turns = rotations(now, on_diag, even, odd, power)
        if sweep < ITERS - 1:
            halves = [split(product(split(now[pair]), turns[pair][0])) for pair in pairs]
            now = [product(turns[pair][1], halves[pair]) for pair in pairs]
        if so_far is None:
            so_far = [turns[pair][0] for pair in pairs]
        elif sweep < ITERS - 1:
            so_far = [split(product(so_far[pair], turns[pair][0])) for pair in pairs]
        else:
            for pair in pairs:
                out[pair] = product(so_far[pair], turns[pair][0])


def solve(row, parts):
    each, height, _ = parts[0].shape
    pairs = each * len(parts)
    return pl.pallas_call(
        functools.partial(solve_kernel, len(parts)),
        out_shape=(
            jax.ShapeDtypeStruct((pairs, WIDTH, WIDTH), jnp.float32),
            jax.ShapeDtypeStruct((LAST_ROWS, WIDTH), jnp.float32),
        ),
        in_specs=[SMEM] + [VMEM] * len(parts),
        out_specs=(VMEM, VMEM),
        scratch_shapes=[
            pltpu.VMEM((pairs, height, WIDTH), jnp.float32),
            pltpu.VMEM((pairs, WIDTH, WIDTH), jnp.float32),
            pltpu.VMEM((pairs, WIDTH, WIDTH), jnp.float32),
            pltpu.VMEM((pairs, WIDTH, 2 * WIDTH), jnp.bfloat16),
        ],
        compiler_params=PARAMS,
        name="solve",
    )(row, *parts)


def turned(tracks, columns, held):
    results = []
    for pairs, places in tracks:
        for pair in range(pairs):
            value = jnp.concatenate([piece(columns, place, pair) for place in places], axis=0)
            results.append((value, len(results)))
    return lambda index: product(split(results[index][0]), split(held[index]))


def edge_kernel(tracks, where, sums, held, *refs):
    columns, near, far = refs[:-2], refs[-2], refs[-1]
    odd = lax.rem(where[0], 2) == 1
    rows = columns[0].shape[1]
    half = rows // 2
    blocks = len(tracks[0][1])
    low_lanes = lax.broadcasted_iota(jnp.int32, (half, WIDTH), 1) < BLOCK
    result = turned(tracks, columns, held)
    last = result(held.shape[0] - 1)
    first = result(0)
    for block in range(blocks):
        span = slice(block * half, (block + 1) * half)
        one = last[block * rows : (block + 1) * rows]
        up = jnp.where(low_lanes, one[:half], pltpu.roll(one[half:], BLOCK, 1))
        one = first[block * rows : (block + 1) * rows]
        down = jnp.where(low_lanes, pltpu.roll(one[:half], BLOCK, 1), one[half:])
        near[span] = jnp.where(odd, down, up)
        far[span] = jnp.where(odd, up, down)
    near[-LAST_ROWS:] = sums[...]


def edges(tracks, where, sums, columns, turns):
    half = len(tracks[0][1]) * columns[0].shape[1] // 2
    return pl.pallas_call(
        functools.partial(edge_kernel, tracks),
        out_shape=tuple(jax.ShapeDtypeStruct((height, WIDTH), jnp.float32) for height in (half + LAST_ROWS, half)),
        in_specs=[SMEM] + [VMEM] * (2 + len(columns)),
        out_specs=(VMEM,) * 2,
        compiler_params=PARAMS,
        name="edges",
    )(where, sums, turns, *columns)


def place_kernel(tracks, where, near, held, *refs):
    columns, out, mate = refs[:-2], refs[-2], refs[-1]
    pairs = held.shape[0]
    rows = columns[0].shape[1]
    half = rows // 2
    blocks = len(tracks[0][1])
    odd = lax.rem(where[0], 2) == 1
    is_first = where[0] == 0
    is_last = where[0] == where[1] - 1
    low_lanes = lax.broadcasted_iota(jnp.int32, (rows, WIDTH), 1) < BLOCK
    result = turned(tracks, columns, held)
    rotated = [result(pair) for pair in range(pairs)]
    for block in range(blocks):
        span = slice(block * rows, (block + 1) * rows)
        own_place = jnp.bitwise_xor(where[2], block)
        own_rows = pl.ds(pl.multiple_of(own_place * rows, rows), rows)
        there = jnp.bitwise_xor(own_place, jnp.where(odd, where[3], where[4]))
        arrived = near[pl.ds(pl.multiple_of(there * half, half), half)]
        moved = pltpu.roll(arrived, BLOCK, 1)
        for pair in range(pairs):
            if pair == 0:
                upper = jnp.where(is_first, rotated[0][span], jnp.concatenate([arrived, moved], axis=0))
            else:
                upper = rotated[pair - 1][span]
                if pair == 1:
                    upper = jnp.where(is_first, pltpu.roll(upper, BLOCK, 1), upper)
            if pair == pairs - 1:
                own = pltpu.roll(rotated[pair][span], BLOCK, 1)
                lower = jnp.where(is_last, own, jnp.concatenate([moved, arrived], axis=0))
            else:
                lower = rotated[pair + 1][span]
            value = jnp.where(low_lanes, upper, lower)
            out[own_rows, pair * WIDTH : (pair + 1) * WIDTH] = value
            if pair == 0:
                first = value
            if pair == pairs - 1:
                mate[span] = jnp.where(odd, value, first)


def place(tracks, where, columns, near, turns):
    height = len(tracks[0][1]) * columns[0].shape[1]
    pairs = sum(track[0] for track in tracks)
    return pl.pallas_call(
        functools.partial(place_kernel, tracks),
        out_shape=(
            jax.ShapeDtypeStruct((height, pairs * WIDTH), jnp.float32),
            jax.ShapeDtypeStruct((height, WIDTH), jnp.float32),
        ),
        in_specs=[SMEM] + [VMEM] * (2 + len(columns)),
        out_specs=(VMEM, VMEM),
        compiler_params=PARAMS,
        name="place",
    )(where, near, turns, *columns)


def finish_kernel(blocks, count, where, far, mate, *refs):
    sums, (out, ratio, tile, sems) = refs[:count], refs[count + 1 :]
    value = sums[0][...]
    for other in sums[1:]:
        value = value + other[...]
    ratio[...] = jnp.sqrt(value[:1, :1] / value[:1, 1:2])
    rows = mate.shape[0] // blocks
    half = rows // 2
    odd = lax.rem(where[0], 2) == 1
    used = jnp.where(odd, where[0] < where[1] - 1, where[0] > 0)
    lanes = lax.broadcasted_iota(jnp.int32, (rows, WIDTH), 1)
    first_lane = jnp.where(used, jnp.where(odd, BLOCK, 0), WIDTH)
    here = (lanes >= first_lane) & (lanes < first_lane + BLOCK)
    column = pl.ds(pl.multiple_of(jnp.where(odd, out.shape[1] - WIDTH, 0), WIDTH), WIDTH)
    copies = []
    for block in range(blocks):
        span = pl.ds(block * rows, rows)
        own_place = jnp.bitwise_xor(where[2], block)
        there = jnp.bitwise_xor(own_place, jnp.where(odd, where[4], where[3]))
        arrived = far[pl.ds(pl.multiple_of(there * half, half), half)]
        moved = pltpu.roll(arrived, BLOCK, 1)
        both = jnp.concatenate([jnp.where(odd, moved, arrived), jnp.where(odd, arrived, moved)], axis=0)
        tile[span] = jnp.where(here, both, mate[span])
        own_rows = pl.ds(pl.multiple_of(own_place * rows, rows), rows)
        copies.append(pltpu.make_async_copy(tile.at[span], out.at[own_rows, column], sems.at[block]))
        copies[-1].start()
    for copy in copies:
        copy.wait()


def finish(blocks, where, far, mate, sums, rotated):
    return pl.pallas_call(
        functools.partial(finish_kernel, blocks, len(sums)),
        out_shape=(jax.ShapeDtypeStruct(rotated.shape, jnp.float32), jax.ShapeDtypeStruct((1, 1), jnp.float32)),
        in_specs=[SMEM] + [VMEM] * (2 + len(sums)) + [HBM],
        out_specs=(HBM, VMEM),
        input_output_aliases={3 + len(sums): 0},
        scratch_shapes=[pltpu.VMEM(mate.shape, jnp.float32), pltpu.SemaphoreType.DMA((blocks,))],
        compiler_params=PARAMS,
        name="finish",
    )(where, far, mate, *sums, rotated)


def swapped_in_twos(value, axis, first):
    pairs = []
    for i in range(first, lax.axis_size(axis) - 1, 2):
        pairs += [(i, i + 1), (i + 1, i)]
    return lax.ppermute(value, axis, pairs)


def swapped(value, axis, by):
    count = lax.axis_size(axis)
    return lax.ppermute(value, axis, [(i, i ^ by) for i in range(count)])


def on_device(r_factor, block_slots):
    pair_count = lax.axis_size("pair")
    row_count = lax.axis_size("row")
    pair_index = lax.axis_index("pair")
    row_index = lax.axis_index("row")
    local = r_factor.shape[1] // WIDTH // pair_count
    shared = local % 2 == 0 and row_count > 1 and row_count & (row_count - 1) == 0
    shares = 2 if shared else 1
    row = row_index.astype(jnp.int32).reshape(1)
    base = pair_index.astype(jnp.int32).reshape(1)
    if shared and pair_count == 8:
        plan = [(local, 0, local, (position,)) for position in range(pair_count)]
        arranged = gather(r_factor, block_slots, base, tuple(plan))
        here = arranged[0::2]
        near = [swapped(value, "pair", 1) for value in arranged[1::2]]
        here_two = swapped(here[1], "pair", 2)
        here_four = swapped(here[2], "pair", 4)
        own, *given = near_grams(here, near)
        taken = [swapped(value, "pair", by) for by, value in zip((2, 4, 6), given)]
        (on_six,) = joined((here[3], near[3]))
        here_two, here_four, on_six, taken = lax.optimization_barrier((here_two, here_four, on_six, taken))
        parts = merge(row, [own] + taken, shares)
        from_six = swapped(on_six, "pair", 6)
        tracks = ((local, tuple((position, 0) for position in range(pair_count - 1)) + ((pair_count - 2, 1),)),)
        bases = (pair_index, pair_index - 1, pair_index + 1)
    else:
        (arranged,) = gather(r_factor, block_slots, base, ((local, 0, local, None),))
        column = lax.all_to_all(arranged, "pair", split_axis=0, concat_axis=0, tiled=True)
        parts = grams(row, column, shares)
        columns = (column,)
        tracks = ((local, tuple((0, group) for group in range(pair_count))),)
        bases = (jnp.zeros_like(pair_index),) * 3
    if shared:
        half = parts[0] + swapped(parts[1], "row", 1)
        if pair_count == 8:
            near_two, near_four, half = lax.optimization_barrier((near[1], near[2], half))
            near_two = swapped(near_two, "pair", 2)
            near_four = swapped(near_four, "pair", 4)
            columns = (here[0], near[0], here_two, near_two, here_four, near_four, from_six)
        for bit in range(1, row_count.bit_length() - 1):
            half = half + swapped(half, "row", 1 << bit)
        parts = (half, swapped(half, "row", 1))
    else:
        parts = (lax.psum(parts[0], "row"),)
    turns, sums = solve(row, parts)
    bases = [jnp.clip(value, 0, pair_count - 1) for value in bases]
    where = jnp.stack([pair_index, jnp.int32(pair_count)] + bases).astype(jnp.int32)
    near, far = edges(tracks, where, sums, columns, turns)
    far = swapped_in_twos(far, "pair", 1)
    near = swapped_in_twos(near, "pair", 0)
    rotated, mate = place(tracks, where, columns, near, turns)
    if pair_count == 8:
        sums = sums + near[-LAST_ROWS:]
        sums = [sums] + [swapped(sums, "pair", by) for by in (2, 4, 6)]
    else:
        sums = [lax.psum(sums, "pair")]
    rotated, off_ratio = finish(pair_count, where, far, mate, sums, rotated)
    return (rotated, off_ratio.reshape(()))


def solution(mesh):
    in_specs = (P(("row", "pair"), None), P())
    out_specs = (P("row", "pair"), P())
    return jax.shard_map(
        on_device, mesh=mesh, in_specs=in_specs, out_specs=out_specs, check_vma=False
    )
```

```python
import functools

import jax
import jax.numpy as jnp
from jax import lax
from jax.experimental import pallas as pl
from jax.experimental.pallas import tpu as pltpu
from jax.sharding import PartitionSpec as P

BLOCK = 64
WIDTH = 2 * BLOCK
ITERS = 3
TOLERANCE = 1e-8
LAST_ROWS = 8
FAR_PARTS = 1
GATHER_CHUNKS = 2
GATHER_VMEM = 62 * 1024 * 1024
VMEM = pl.BlockSpec(memory_space=pltpu.VMEM)
SMEM = pl.BlockSpec(memory_space=pltpu.SMEM)
HBM = pl.BlockSpec(memory_space=pltpu.HBM)
PARAMS = pltpu.CompilerParams(vmem_limit_bytes=48 * 1024 * 1024)


def split(value):
    high = value.astype(jnp.bfloat16)
    low = (value - high.astype(jnp.float32)).astype(jnp.bfloat16)
    return jnp.concatenate([high, low], axis=1)


def product(left, right):
    both = jnp.dot(left, jnp.concatenate([right, right], axis=0), preferred_element_type=jnp.float32)
    half = both.shape[1] // 2
    return both[:, :half] + both[:, half:]


def unit(size):
    row_ids = lax.broadcasted_iota(jnp.int32, (size, size), 0)
    col_ids = lax.broadcasted_iota(jnp.int32, (size, size), 1)
    return row_ids == col_ids


def total(value):
    return jnp.sum(jnp.sum(value, axis=1, keepdims=True), axis=0, keepdims=True)


def gather_kernel(plan, slots, source, *outs):
    rows = source.shape[0]
    local = plan[0][0]
    base = slots[slots.shape[0] - 1]
    low_lanes = lax.broadcasted_iota(jnp.int32, (rows, WIDTH), 1) < BLOCK

    def tile(block):
        return source[:, pl.ds(pl.multiple_of(lax.shift_right_logical(block, 1) * WIDTH, WIDTH), WIDTH)]

    def one_pair(slot):
        upper_block, lower_block = slots[slot], slots[slot + 1]
        upper, lower = tile(upper_block), tile(lower_block)
        turned_over = pltpu.roll(jnp.where(low_lanes, lower, upper), BLOCK, 1)
        upper = jnp.where(jnp.bitwise_and(upper_block, 1) == 0, upper, turned_over)
        lower = jnp.where(jnp.bitwise_and(lower_block, 1) == 1, lower, turned_over)
        return jnp.where(low_lanes, upper, lower)

    for (_, first, positions), out in zip(plan, outs):
        count = out.shape[2] // WIDTH

        def one_group(group, place, first=first, count=count, out=out):
            for pair in range(count):
                value = one_pair(2 * (group * local + first + pair))
                out[place, :, pair * WIDTH : (pair + 1) * WIDTH] = value

        if positions is None:

            def step(group, carry, one_group=one_group):
                one_group(group, group)
                return carry

            lax.fori_loop(0, out.shape[0], step, 0)
        else:
            for place, position in enumerate(positions):
                one_group(jnp.bitwise_xor(base, position), place)


def gather(r_factor, block_slots, base, plan):
    rows = r_factor.shape[0]
    groups = r_factor.shape[1] // WIDTH // plan[0][0]
    shapes = []
    for _, _, taken, positions in plan:
        count = groups if positions is None else len(positions)
        shapes.append(jax.ShapeDtypeStruct((count, rows, taken * WIDTH), jnp.float32))
    return pl.pallas_call(
        functools.partial(gather_kernel, tuple((local, first, positions) for local, first, _, positions in plan)),
        out_shape=tuple(shapes),
        in_specs=[SMEM, VMEM],
        out_specs=(VMEM,) * len(shapes),
        compiler_params=PARAMS,
        name="gather",
    )(jnp.concatenate([block_slots, base]), r_factor)


def gram(pieces):
    parts = split(jnp.concatenate(pieces, axis=0))
    four = lax.dot_general(parts, parts, (((0,), (0,)), ((), ())), preferred_element_type=jnp.float32)
    half = four[:WIDTH] + four[WIDTH:]
    return half[:, :WIDTH] + half[:, WIDTH:]


def piece(refs, where, pair):
    operand, place = where
    return refs[operand][place, :, pair * WIDTH : (pair + 1) * WIDTH]


def deal(row, held, outs):
    each = outs[0].shape[0]
    for by, out in enumerate(outs):
        out[...] = held[pl.ds(jnp.bitwise_xor(jnp.bitwise_and(row, len(outs) - 1), by) * each, each)]


def grams_kernel(row, column, *refs):
    outs, held = refs[:-1], refs[-1]
    groups = column.shape[0]
    for pair in range(held.shape[0]):
        held[pair] = gram([piece([column], (0, group), pair) for group in range(groups)])
    deal(row[0], held, outs)


def grams(row, column, shares):
    pairs = column.shape[2] // WIDTH
    return pl.pallas_call(
        grams_kernel,
        out_shape=(jax.ShapeDtypeStruct((pairs // shares, WIDTH, WIDTH), jnp.float32),) * shares,
        in_specs=[SMEM, VMEM],
        out_specs=(VMEM,) * shares,
        scratch_shapes=[pltpu.VMEM((pairs, WIDTH, WIDTH), jnp.float32)],
        compiler_params=PARAMS,
        name="grams",
    )(row, column)


def pack(gram_matrix):
    half = WIDTH // 2
    top = gram_matrix[:half]
    last = pltpu.roll(gram_matrix[half:], half, 1)
    row_ids = lax.broadcasted_iota(jnp.int32, (half, WIDTH), 0)
    col_ids = lax.broadcasted_iota(jnp.int32, (half, WIDTH), 1)
    ends = jnp.sum(jnp.where(row_ids == col_ids, last, 0.0), axis=0, keepdims=True)
    both = jnp.where((col_ids < half) & (row_ids > col_ids), last, top)
    return jnp.concatenate([both, jnp.broadcast_to(ends, (LAST_ROWS, WIDTH))], axis=0)


def unpack(packed):
    half = WIDTH // 2
    both = packed[:half]
    ends = packed[half : half + 1]
    mirrored = jnp.transpose(jnp.concatenate([both, both], axis=0))
    row_ids = lax.broadcasted_iota(jnp.int32, (half, WIDTH), 0)
    col_ids = lax.broadcasted_iota(jnp.int32, (half, WIDTH), 1)
    top = jnp.where((col_ids < half) & (row_ids > col_ids), mirrored[:half], both)
    last = jnp.where(row_ids > col_ids, both, mirrored[:half])
    last = jnp.where(row_ids == col_ids, ends, last)
    bottom = jnp.where(col_ids < half, mirrored[half:], pltpu.roll(last, half, 1))
    return jnp.concatenate([top, bottom], axis=0)


PACKED = WIDTH // 2 + LAST_ROWS


def near_grams_kernel(*refs):
    count = len(refs) // 3
    for place in range(count):
        here, near, out = refs[place], refs[count + place], refs[2 * count + place]
        for pair in range(out.shape[0]):
            out[pair] = pack(gram([piece([ref], (0, 0), pair) for ref in (here, near)]))


def near_grams(here, near):
    pairs = here[0].shape[2] // WIDTH
    return pl.pallas_call(
        near_grams_kernel,
        out_shape=(jax.ShapeDtypeStruct((pairs, PACKED, WIDTH), jnp.float32),) * len(here),
        in_specs=[VMEM] * (2 * len(here)),
        out_specs=(VMEM,) * len(here),
        compiler_params=PARAMS,
        name="near_grams",
    )(*here, *near)


def joined_kernel(counts, after, *refs):
    del after
    sources, outs = refs[: sum(counts)], refs[sum(counts) :]
    for count, out in zip(counts, outs):
        for place in range(count):
            out[place] = sources[place][0]
        sources = sources[count:]


def joined(after, *sides):
    _, rows, cols = sides[0][0].shape
    counts = tuple(len(side) for side in sides)
    return pl.pallas_call(
        functools.partial(joined_kernel, counts),
        out_shape=tuple(jax.ShapeDtypeStruct((count, rows, cols), jnp.float32) for count in counts),
        in_specs=[pl.BlockSpec(memory_space=pl.ANY)] + [VMEM] * sum(counts),
        out_specs=(VMEM,) * len(sides),
        compiler_params=PARAMS,
        name="joined",
    )(after, *[value for side in sides for value in side])


def merge_kernel(count, row, *refs):
    parts, outs, held = refs[:count], refs[count:-1], refs[-1]
    value = parts[0][...]
    for part in parts[1:]:
        value = value + part[...]
    held[...] = value
    deal(row[0], held, outs)


def merge(row, parts, shares):
    pairs, height, _ = parts[0].shape
    return pl.pallas_call(
        functools.partial(merge_kernel, len(parts)),
        out_shape=(jax.ShapeDtypeStruct((pairs // shares, height, WIDTH), jnp.float32),) * shares,
        in_specs=[SMEM] + [VMEM] * len(parts),
        out_specs=(VMEM,) * shares,
        scratch_shapes=[pltpu.VMEM((pairs, height, WIDTH), jnp.float32)],
        compiler_params=PARAMS,
        name="merge",
    )(row, *parts)


def rotations(grams_now, on_diag, even, odd, power):
    diag_one = jnp.where(on_diag, 1.0, 0.0)
    size = diag_one.shape[0]
    skews, skews_parts, squares = [], [], []
    for gram_now in grams_now:
        diag_part = jnp.where(on_diag, gram_now, 0.0)
        across = jnp.sum(diag_part, axis=1, keepdims=True)
        down = jnp.sum(diag_part, axis=0, keepdims=True)
        skews.append(gram_now * (across - down) / (2.0 * (across * across + down * down)))
    for skew in skews:
        skews_parts.append(split(skew))
        squares.append(product(skews_parts[-1], skews_parts[-1]))
    evens, odds, rests, worst = [], [], [], None
    for skew, parts, square in zip(skews, skews_parts, squares):
        bound = jnp.sqrt(0.5 * total(square * square))
        scale = 2.0 / (2.0 + bound)
        rate = bound / (2.0 + bound)
        worst = rate if worst is None else jnp.maximum(worst, rate)
        rest = (1.0 - scale) * diag_one + scale * square
        rest_parts = split(rest)
        first = product(jnp.concatenate([parts, rest_parts], axis=0), rest_parts)
        evens.append(scale * (diag_one + rest))
        odds.append(scale * (skew + first[:size]))
        rests.append(split(first[size:]))
    for index, rest_parts in enumerate(rests):
        stack = jnp.concatenate([split(evens[index]), split(odds[index]), rest_parts], axis=0)
        second = product(stack, rest_parts)
        evens[index] = evens[index] + second[:size]
        odds[index] = odds[index] + second[size : 2 * size]
        rests[index] = split(second[2 * size :])
    for index, rest_parts in enumerate(rests):
        third = product(jnp.concatenate([split(evens[index]), split(odds[index])], axis=0), rest_parts)
        even[index] = evens[index] + third[:size]
        odd[index] = odds[index] + third[size:]
        power[index] = rest_parts

    def more(left):
        return left > TOLERANCE

    def step(left):
        for index in range(len(grams_now)):
            old = power[index]
            parts = split(product(old, old))
            power[index] = parts
            even[index] += product(split(even[index]), parts)
            odd[index] += product(split(odd[index]), parts)
        return left * left

    worst = worst * worst
    worst = worst * worst
    lax.while_loop(more, step, (worst * worst)[0, 0])
    results = []
    for index in range(len(grams_now)):
        even_now = 2.0 * even[index] - diag_one
        odd_now = 2.0 * odd[index]
        results.append((split(even_now - odd_now), split(even_now + odd_now)))
    return results


def solve_kernel(count, row, *refs):
    parts, out, sums, held, even, odd, power = refs[:count], *refs[count:]
    on_diag = unit(WIDTH)
    pairs = range(out.shape[0])
    each = parts[0].shape[0]
    for by, part in enumerate(parts):
        held[pl.ds(jnp.bitwise_xor(jnp.bitwise_and(row[0], count - 1), by) * each, each)] = part[...]
    off_total = jnp.zeros((1, 1), jnp.float32)
    diag_total = jnp.zeros((1, 1), jnp.float32)
    now = []
    for pair in pairs:
        gram_now = held[pair]
        if gram_now.shape[0] != WIDTH:
            gram_now = unpack(gram_now)
        squares = gram_now * gram_now
        off_total += total(jnp.where(on_diag, 0.0, squares))
        diag_total += total(jnp.where(on_diag, squares, 0.0))
        now.append(gram_now)
    first_lane = lax.broadcasted_iota(jnp.int32, sums.shape, 1) == 0
    sums[...] = jnp.where(first_lane, off_total, diag_total)
    so_far = None
    for sweep in range(ITERS):
        turns = rotations(now, on_diag, even, odd, power)
        if sweep < ITERS - 1:
            halves = [split(product(split(now[pair]), turns[pair][0])) for pair in pairs]
            now = [product(turns[pair][1], halves[pair]) for pair in pairs]
        if so_far is None:
            so_far = [turns[pair][0] for pair in pairs]
        elif sweep < ITERS - 1:
            so_far = [split(product(so_far[pair], turns[pair][0])) for pair in pairs]
        else:
            for pair in pairs:
                out[pair] = product(so_far[pair], turns[pair][0])


def solve(row, parts):
    each, height, _ = parts[0].shape
    pairs = each * len(parts)
    return pl.pallas_call(
        functools.partial(solve_kernel, len(parts)),
        out_shape=(
            jax.ShapeDtypeStruct((pairs, WIDTH, WIDTH), jnp.float32),
            jax.ShapeDtypeStruct((LAST_ROWS, WIDTH), jnp.float32),
        ),
        in_specs=[SMEM] + [VMEM] * len(parts),
        out_specs=(VMEM, VMEM),
        scratch_shapes=[
            pltpu.VMEM((pairs, height, WIDTH), jnp.float32),
            pltpu.VMEM((pairs, WIDTH, WIDTH), jnp.float32),
            pltpu.VMEM((pairs, WIDTH, WIDTH), jnp.float32),
            pltpu.VMEM((pairs, WIDTH, 2 * WIDTH), jnp.bfloat16),
        ],
        compiler_params=PARAMS,
        name="solve",
    )(row, *parts)


def turned(tracks, columns, held):
    results = []
    for pairs, places in tracks:
        for pair in range(pairs):
            value = jnp.concatenate([piece(columns, place, pair) for place in places], axis=0)
            results.append((value, len(results)))
    return lambda index: product(split(results[index][0]), split(held[index]))


def edge_kernel(tracks, parts, where, sums, held, *refs):
    columns, near, far = refs[: -1 - parts], refs[-1 - parts], refs[-parts:]
    odd = lax.rem(where[0], 2) == 1
    rows = columns[0].shape[1]
    half = rows // 2
    blocks = len(tracks[0][1])
    low_lanes = lax.broadcasted_iota(jnp.int32, (half, WIDTH), 1) < BLOCK
    result = turned(tracks, columns, held)
    last = result(held.shape[0] - 1)
    first = result(0)
    for block in range(blocks):
        span = slice(block * half, (block + 1) * half)
        one = last[block * rows : (block + 1) * rows]
        up = jnp.where(low_lanes, one[:half], pltpu.roll(one[half:], BLOCK, 1))
        one = first[block * rows : (block + 1) * rows]
        down = jnp.where(low_lanes, pltpu.roll(one[:half], BLOCK, 1), one[half:])
        near[span] = jnp.where(odd, down, up)
        each = blocks // parts
        far[block // each][block % each * half : (block % each + 1) * half] = jnp.where(odd, up, down)
    near[-LAST_ROWS:] = sums[...]


def edges(tracks, parts, where, sums, columns, turns):
    half = len(tracks[0][1]) * columns[0].shape[1] // 2
    heights = (half + LAST_ROWS,) + (half // parts,) * parts
    return pl.pallas_call(
        functools.partial(edge_kernel, tracks, parts),
        out_shape=tuple(jax.ShapeDtypeStruct((height, WIDTH), jnp.float32) for height in heights),
        in_specs=[SMEM] + [VMEM] * (2 + len(columns)),
        out_specs=(VMEM,) * (1 + parts),
        compiler_params=PARAMS,
        name="edges",
    )(where, sums, turns, *columns)


def place_kernel(tracks, where, near, held, *refs):
    columns, out, mate = refs[:-2], refs[-2], refs[-1]
    pairs = held.shape[0]
    rows = columns[0].shape[1]
    half = rows // 2
    blocks = len(tracks[0][1])
    odd = lax.rem(where[0], 2) == 1
    is_first = where[0] == 0
    is_last = where[0] == where[1] - 1
    low_lanes = lax.broadcasted_iota(jnp.int32, (rows, WIDTH), 1) < BLOCK
    result = turned(tracks, columns, held)
    rotated = [result(pair) for pair in range(pairs)]
    for block in range(blocks):
        span = slice(block * rows, (block + 1) * rows)
        own_place = jnp.bitwise_xor(where[2], block)
        own_rows = pl.ds(pl.multiple_of(own_place * rows, rows), rows)
        there = jnp.bitwise_xor(own_place, jnp.where(odd, where[3], where[4]))
        arrived = near[pl.ds(pl.multiple_of(there * half, half), half)]
        moved = pltpu.roll(arrived, BLOCK, 1)
        for pair in range(pairs):
            if pair == 0:
                upper = jnp.where(is_first, rotated[0][span], jnp.concatenate([arrived, moved], axis=0))
            else:
                upper = rotated[pair - 1][span]
                if pair == 1:
                    upper = jnp.where(is_first, pltpu.roll(upper, BLOCK, 1), upper)
            if pair == pairs - 1:
                own = pltpu.roll(rotated[pair][span], BLOCK, 1)
                lower = jnp.where(is_last, own, jnp.concatenate([moved, arrived], axis=0))
            else:
                lower = rotated[pair + 1][span]
            value = jnp.where(low_lanes, upper, lower)
            out[own_rows, pair * WIDTH : (pair + 1) * WIDTH] = value
            if pair == 0:
                first = value
            if pair == pairs - 1:
                mate[span] = jnp.where(odd, value, first)


def place(tracks, where, columns, near, turns):
    height = len(tracks[0][1]) * columns[0].shape[1]
    pairs = sum(track[0] for track in tracks)
    return pl.pallas_call(
        functools.partial(place_kernel, tracks),
        out_shape=(
            jax.ShapeDtypeStruct((height, pairs * WIDTH), jnp.float32),
            jax.ShapeDtypeStruct((height, WIDTH), jnp.float32),
        ),
        in_specs=[SMEM] + [VMEM] * (2 + len(columns)),
        out_specs=(VMEM, VMEM),
        compiler_params=PARAMS,
        name="place",
    )(where, near, turns, *columns)


def finish_kernel(blocks, parts, where, mate, *refs):
    far, sums, (_, out, ratio, tile, sems) = refs[:parts], refs[parts:-5], refs[-5:]
    rows = mate.shape[0] // blocks
    half = rows // 2
    each = blocks // parts
    odd = lax.rem(where[0], 2) == 1
    used = jnp.where(odd, where[0] < where[1] - 1, where[0] > 0)
    lanes = lax.broadcasted_iota(jnp.int32, (rows, WIDTH), 1)
    first_lane = jnp.where(used, jnp.where(odd, BLOCK, 0), WIDTH)
    here = (lanes >= first_lane) & (lanes < first_lane + BLOCK)
    column = pl.ds(pl.multiple_of(jnp.where(odd, out.shape[1] - WIDTH, 0), WIDTH), WIDTH)
    copies = []
    for block in range(blocks):
        span = pl.ds(block * rows, rows)
        own_place = jnp.bitwise_xor(where[2], block)
        there = jnp.bitwise_xor(own_place, jnp.where(odd, where[4], where[3]))
        far_rows = pl.ds(pl.multiple_of(lax.rem(there, each) * half, half), half)
        arrived = far[0][far_rows]
        for part in range(1, parts):
            arrived = jnp.where(there < part * each, arrived, far[part][far_rows])
        moved = pltpu.roll(arrived, BLOCK, 1)
        both = jnp.concatenate([jnp.where(odd, moved, arrived), jnp.where(odd, arrived, moved)], axis=0)
        tile[span] = jnp.where(here, both, mate[span])
        own_rows = pl.ds(pl.multiple_of(own_place * rows, rows), rows)
        copies.append(pltpu.make_async_copy(tile.at[span], out.at[own_rows, column], sems.at[block]))
        copies[-1].start()
    value = sums[0][...]
    for other in sums[1:]:
        value = value + other[...]
    ratio[...] = jnp.sqrt(value[:1, :1] / value[:1, 1:2])
    for copy in copies:
        copy.wait()


def finish(blocks, where, far, mate, sums, rotated):
    return pl.pallas_call(
        functools.partial(finish_kernel, blocks, len(far)),
        out_shape=(jax.ShapeDtypeStruct(rotated.shape, jnp.float32), jax.ShapeDtypeStruct((1, 1), jnp.float32)),
        in_specs=[SMEM] + [VMEM] * (1 + len(far) + len(sums)) + [HBM],
        out_specs=(HBM, VMEM),
        input_output_aliases={2 + len(far) + len(sums): 0},
        scratch_shapes=[pltpu.VMEM(mate.shape, jnp.float32), pltpu.SemaphoreType.DMA((blocks,))],
        compiler_params=PARAMS,
        name="finish",
    )(where, mate, *far, *sums, rotated)


def swapped_in_twos(value, axis, first):
    pairs = []
    for i in range(first, lax.axis_size(axis) - 1, 2):
        pairs += [(i, i + 1), (i + 1, i)]
    return lax.ppermute(value, axis, pairs)


def swapped(value, axis, by):
    count = lax.axis_size(axis)
    return lax.ppermute(value, axis, [(i, i ^ by) for i in range(count)])


def on_device(r_factor, block_slots):
    pair_count = lax.axis_size("pair")
    row_count = lax.axis_size("row")
    pair_index = lax.axis_index("pair")
    row_index = lax.axis_index("row")
    local = r_factor.shape[1] // WIDTH // pair_count
    shared = local % 2 == 0 and row_count > 1 and row_count & (row_count - 1) == 0
    shares = 2 if shared else 1
    row = row_index.astype(jnp.int32).reshape(1)
    base = pair_index.astype(jnp.int32).reshape(1)
    if shared and pair_count == 8:
        plan = [(local, 0, local, (position,)) for position in range(pair_count)]
        arranged = gather(r_factor, block_slots, base, tuple(plan))
        here = arranged[0::2]
        near = [swapped(value, "pair", 1) for value in arranged[1::2]]
        own, *given = near_grams(here, near)
        taken = [swapped(value, "pair", by) for by, value in zip((2, 4, 6), given)]
        going = joined(given[0], (here[1], near[1]), (here[2], near[2]), (here[3], near[3]))
        going, taken = lax.optimization_barrier((going, taken))
        parts = merge(row, [own] + taken, shares)
        from_far = [swapped(value, "pair", by) for by, value in zip((2, 4, 6), going)]
        columns = (here[0], near[0], *from_far)
        places = ((0, 0), (1, 0), (2, 0), (2, 1), (3, 0), (3, 1), (4, 0), (4, 1))
        tracks = ((local, places),)
        bases = (pair_index, pair_index - 1, pair_index + 1)
    else:
        (arranged,) = gather(r_factor, block_slots, base, ((local, 0, local, None),))
        column = lax.all_to_all(arranged, "pair", split_axis=0, concat_axis=0, tiled=True)
        parts = grams(row, column, shares)
        columns = (column,)
        tracks = ((local, tuple((0, group) for group in range(pair_count))),)
        bases = (jnp.zeros_like(pair_index),) * 3
    if shared:
        half = parts[0] + swapped(parts[1], "row", 1)
        for bit in range(1, row_count.bit_length() - 1):
            half = half + swapped(half, "row", 1 << bit)
        parts = (half, swapped(half, "row", 1))
    else:
        parts = (lax.psum(parts[0], "row"),)
    turns, sums = solve(row, parts)
    bases = [jnp.clip(value, 0, pair_count - 1) for value in bases]
    where = jnp.stack([pair_index, jnp.int32(pair_count)] + bases).astype(jnp.int32)
    near, *far = edges(tracks, FAR_PARTS if pair_count % FAR_PARTS == 0 else 1, where, sums, columns, turns)
    far = [swapped_in_twos(part, "pair", 1) for part in far]
    near = swapped_in_twos(near, "pair", 0)
    rotated, mate = place(tracks, where, columns, near, turns)
    if pair_count == 8:
        sums = sums + near[-LAST_ROWS:]
        sums = [sums] + [swapped(sums, "pair", by) for by in (2, 4, 6)]
    else:
        sums = [lax.psum(sums, "pair")]
    rotated, off_ratio = finish(pair_count, where, far, mate, sums, rotated)
    return (rotated, off_ratio.reshape(()))


def solution(mesh):
    in_specs = (P(("row", "pair"), None), P())
    out_specs = (P("row", "pair"), P())
    return jax.shard_map(
        on_device, mesh=mesh, in_specs=in_specs, out_specs=out_specs, check_vma=False
    )
```

```python
import functools

import jax
import jax.numpy as jnp
from jax import lax
from jax.experimental import pallas as pl
from jax.experimental.pallas import tpu as pltpu
from jax.sharding import PartitionSpec as P

BLOCK = 64
WIDTH = 2 * BLOCK
ITERS = 3
TOLERANCE = 1e-8
LAST_ROWS = 8
AHEAD = 3
FAR_PARTS = 1
GATHER_CHUNKS = 2
GATHER_VMEM = 62 * 1024 * 1024
VMEM = pl.BlockSpec(memory_space=pltpu.VMEM)
SMEM = pl.BlockSpec(memory_space=pltpu.SMEM)
HBM = pl.BlockSpec(memory_space=pltpu.HBM)
PARAMS = pltpu.CompilerParams(vmem_limit_bytes=48 * 1024 * 1024)


def split(value):
    high = value.astype(jnp.bfloat16)
    low = (value - high.astype(jnp.float32)).astype(jnp.bfloat16)
    return jnp.concatenate([high, low], axis=1)


def product(left, right):
    both = jnp.dot(left, jnp.concatenate([right, right], axis=0), preferred_element_type=jnp.float32)
    half = both.shape[1] // 2
    return both[:, :half] + both[:, half:]


def unit(size):
    row_ids = lax.broadcasted_iota(jnp.int32, (size, size), 0)
    col_ids = lax.broadcasted_iota(jnp.int32, (size, size), 1)
    return row_ids == col_ids


def total(value):
    return jnp.sum(jnp.sum(value, axis=1, keepdims=True), axis=0, keepdims=True)


def gather_kernel(plan, slots, source, *outs):
    rows = source.shape[0]
    local = plan[0][0]
    base = slots[slots.shape[0] - 1]
    low_lanes = lax.broadcasted_iota(jnp.int32, (rows, WIDTH), 1) < BLOCK

    def tile(block):
        return source[:, pl.ds(pl.multiple_of(lax.shift_right_logical(block, 1) * WIDTH, WIDTH), WIDTH)]

    def one_pair(slot):
        upper_block, lower_block = slots[slot], slots[slot + 1]
        upper, lower = tile(upper_block), tile(lower_block)
        turned_over = pltpu.roll(jnp.where(low_lanes, lower, upper), BLOCK, 1)
        upper = jnp.where(jnp.bitwise_and(upper_block, 1) == 0, upper, turned_over)
        lower = jnp.where(jnp.bitwise_and(lower_block, 1) == 1, lower, turned_over)
        return jnp.where(low_lanes, upper, lower)

    for (_, first, positions), out in zip(plan, outs):
        count = out.shape[2] // WIDTH

        def one_group(group, place, first=first, count=count, out=out):
            for pair in range(count):
                value = one_pair(2 * (group * local + first + pair))
                out[place, :, pair * WIDTH : (pair + 1) * WIDTH] = value

        if positions is None:

            def step(group, carry, one_group=one_group):
                one_group(group, group)
                return carry

            lax.fori_loop(0, out.shape[0], step, 0)
        else:
            for place, position in enumerate(positions):
                one_group(jnp.bitwise_xor(base, position), place)


def gather(r_factor, block_slots, base, plan):
    rows = r_factor.shape[0]
    groups = r_factor.shape[1] // WIDTH // plan[0][0]
    shapes = []
    for _, _, taken, positions in plan:
        count = groups if positions is None else len(positions)
        shapes.append(jax.ShapeDtypeStruct((count, rows, taken * WIDTH), jnp.float32))
    return pl.pallas_call(
        functools.partial(gather_kernel, tuple((local, first, positions) for local, first, _, positions in plan)),
        out_shape=tuple(shapes),
        in_specs=[SMEM, VMEM],
        out_specs=(VMEM,) * len(shapes),
        compiler_params=PARAMS,
        name="gather",
    )(jnp.concatenate([block_slots, base]), r_factor)


def gram(pieces):
    parts = split(jnp.concatenate(pieces, axis=0))
    four = lax.dot_general(parts, parts, (((0,), (0,)), ((), ())), preferred_element_type=jnp.float32)
    half = four[:WIDTH] + four[WIDTH:]
    return half[:, :WIDTH] + half[:, WIDTH:]


def piece(refs, where, pair):
    operand, place, first = where
    return refs[operand][place, :, (first + pair) * WIDTH : (first + pair + 1) * WIDTH]


def deal(row, held, outs):
    each = outs[0].shape[0]
    for by, out in enumerate(outs):
        out[...] = held[pl.ds(jnp.bitwise_xor(jnp.bitwise_and(row, len(outs) - 1), by) * each, each)]


def grams_kernel(row, column, *refs):
    outs, held = refs[:-1], refs[-1]
    groups = column.shape[0]
    for pair in range(held.shape[0]):
        held[pair] = gram([piece([column], (0, group, 0), pair) for group in range(groups)])
    deal(row[0], held, outs)


def grams(row, column, shares):
    pairs = column.shape[2] // WIDTH
    return pl.pallas_call(
        grams_kernel,
        out_shape=(jax.ShapeDtypeStruct((pairs // shares, WIDTH, WIDTH), jnp.float32),) * shares,
        in_specs=[SMEM, VMEM],
        out_specs=(VMEM,) * shares,
        scratch_shapes=[pltpu.VMEM((pairs, WIDTH, WIDTH), jnp.float32)],
        compiler_params=PARAMS,
        name="grams",
    )(row, column)


def pack(gram_matrix):
    half = WIDTH // 2
    top = gram_matrix[:half]
    last = pltpu.roll(gram_matrix[half:], half, 1)
    row_ids = lax.broadcasted_iota(jnp.int32, (half, WIDTH), 0)
    col_ids = lax.broadcasted_iota(jnp.int32, (half, WIDTH), 1)
    ends = jnp.sum(jnp.where(row_ids == col_ids, last, 0.0), axis=0, keepdims=True)
    both = jnp.where((col_ids < half) & (row_ids > col_ids), last, top)
    return jnp.concatenate([both, jnp.broadcast_to(ends, (LAST_ROWS, WIDTH))], axis=0)


def unpack(packed):
    half = WIDTH // 2
    both = packed[:half]
    ends = packed[half : half + 1]
    mirrored = jnp.transpose(jnp.concatenate([both, both], axis=0))
    row_ids = lax.broadcasted_iota(jnp.int32, (half, WIDTH), 0)
    col_ids = lax.broadcasted_iota(jnp.int32, (half, WIDTH), 1)
    top = jnp.where((col_ids < half) & (row_ids > col_ids), mirrored[:half], both)
    last = jnp.where(row_ids > col_ids, both, mirrored[:half])
    last = jnp.where(row_ids == col_ids, ends, last)
    bottom = jnp.where(col_ids < half, mirrored[half:], pltpu.roll(last, half, 1))
    return jnp.concatenate([top, bottom], axis=0)


PACKED = WIDTH // 2 + LAST_ROWS


def near_grams_kernel(plan, *refs):
    sources, outs = refs[: -len(plan)], refs[-len(plan) :]
    for places, out in zip(plan, outs):
        for pair in range(out.shape[0]):
            out[pair] = pack(gram([piece(sources, place, 0) for place in places[pair]]))


def near_grams(plan, *sources):
    return pl.pallas_call(
        functools.partial(near_grams_kernel, plan),
        out_shape=tuple(jax.ShapeDtypeStruct((len(places), PACKED, WIDTH), jnp.float32) for places in plan),
        in_specs=[VMEM] * len(sources),
        out_specs=(VMEM,) * len(plan),
        compiler_params=PARAMS,
        name="near_grams",
    )(*sources)


def joined_kernel(plan, after, *refs):
    del after
    sources, outs = refs[: -len(plan)], refs[-len(plan) :]
    for places, out in zip(plan, outs):
        for place, (source, first) in enumerate(places):
            out[place] = sources[source][0, :, first * WIDTH : first * WIDTH + out.shape[2]]


def joined(after, plan, *sources):
    rows = sources[0].shape[1]
    return pl.pallas_call(
        functools.partial(joined_kernel, tuple(places for _, places in plan)),
        out_shape=tuple(jax.ShapeDtypeStruct((len(places), rows, pairs * WIDTH), jnp.float32) for pairs, places in plan),
        in_specs=[pl.BlockSpec(memory_space=pl.ANY)] + [VMEM] * len(sources),
        out_specs=(VMEM,) * len(plan),
        compiler_params=PARAMS,
        name="joined",
    )(after, *sources)


def merge_kernel(count, row, *refs):
    parts, outs, held = refs[:count], refs[count:-1], refs[-1]
    value = parts[0][...]
    for part in parts[1:]:
        value = value + part[...]
    held[...] = value
    deal(row[0], held, outs)


def merge(row, parts, shares):
    pairs, height, _ = parts[0].shape
    return pl.pallas_call(
        functools.partial(merge_kernel, len(parts)),
        out_shape=(jax.ShapeDtypeStruct((pairs // shares, height, WIDTH), jnp.float32),) * shares,
        in_specs=[SMEM] + [VMEM] * len(parts),
        out_specs=(VMEM,) * shares,
        scratch_shapes=[pltpu.VMEM((pairs, height, WIDTH), jnp.float32)],
        compiler_params=PARAMS,
        name="merge",
    )(row, *parts)


def rotations(grams_now, on_diag, even, odd, power):
    diag_one = jnp.where(on_diag, 1.0, 0.0)
    size = diag_one.shape[0]
    skews, skews_parts, squares = [], [], []
    for gram_now in grams_now:
        diag_part = jnp.where(on_diag, gram_now, 0.0)
        across = jnp.sum(diag_part, axis=1, keepdims=True)
        down = jnp.sum(diag_part, axis=0, keepdims=True)
        skews.append(gram_now * (across - down) / (2.0 * (across * across + down * down)))
    for skew in skews:
        skews_parts.append(split(skew))
        squares.append(product(skews_parts[-1], skews_parts[-1]))
    evens, odds, rests, worst = [], [], [], None
    for skew, parts, square in zip(skews, skews_parts, squares):
        bound = jnp.sqrt(0.5 * total(square * square))
        scale = 2.0 / (2.0 + bound)
        rate = bound / (2.0 + bound)
        worst = rate if worst is None else jnp.maximum(worst, rate)
        rest = (1.0 - scale) * diag_one + scale * square
        rest_parts = split(rest)
        first = product(jnp.concatenate([parts, rest_parts], axis=0), rest_parts)
        evens.append(scale * (diag_one + rest))
        odds.append(scale * (skew + first[:size]))
        rests.append(split(first[size:]))
    for index, rest_parts in enumerate(rests):
        stack = jnp.concatenate([split(evens[index]), split(odds[index]), rest_parts], axis=0)
        second = product(stack, rest_parts)
        evens[index] = evens[index] + second[:size]
        odds[index] = odds[index] + second[size : 2 * size]
        rests[index] = split(second[2 * size :])
    for index, rest_parts in enumerate(rests):
        third = product(jnp.concatenate([split(evens[index]), split(odds[index])], axis=0), rest_parts)
        even[index] = evens[index] + third[:size]
        odd[index] = odds[index] + third[size:]
        power[index] = rest_parts

    def more(left):
        return left > TOLERANCE

    def step(left):
        for index in range(len(grams_now)):
            old = power[index]
            parts = split(product(old, old))
            power[index] = parts
            even[index] += product(split(even[index]), parts)
            odd[index] += product(split(odd[index]), parts)
        return left * left

    worst = worst * worst
    worst = worst * worst
    lax.while_loop(more, step, (worst * worst)[0, 0])
    results = []
    for index in range(len(grams_now)):
        even_now = 2.0 * even[index] - diag_one
        odd_now = 2.0 * odd[index]
        results.append((split(even_now - odd_now), split(even_now + odd_now)))
    return results


def solve_kernel(count, row, *refs):
    parts, out, sums, held, even, odd, power = refs[:count], *refs[count:]
    on_diag = unit(WIDTH)
    pairs = range(out.shape[0])
    each = parts[0].shape[0]
    for by, part in enumerate(parts):
        held[pl.ds(jnp.bitwise_xor(jnp.bitwise_and(row[0], count - 1), by) * each, each)] = part[...]
    off_total = jnp.zeros((1, 1), jnp.float32)
    diag_total = jnp.zeros((1, 1), jnp.float32)
    now = []
    for pair in pairs:
        gram_now = held[pair]
        if gram_now.shape[0] != WIDTH:
            gram_now = unpack(gram_now)
        squares = gram_now * gram_now
        off_total += total(jnp.where(on_diag, 0.0, squares))
        diag_total += total(jnp.where(on_diag, squares, 0.0))
        now.append(gram_now)
    first_lane = lax.broadcasted_iota(jnp.int32, sums.shape, 1) == 0
    sums[...] = jnp.where(first_lane, off_total, diag_total)
    so_far = None
    for sweep in range(ITERS):
        turns = rotations(now, on_diag, even, odd, power)
        if sweep < ITERS - 1:
            halves = [split(product(split(now[pair]), turns[pair][0])) for pair in pairs]
            now = [product(turns[pair][1], halves[pair]) for pair in pairs]
        if so_far is None:
            so_far = [turns[pair][0] for pair in pairs]
        elif sweep < ITERS - 1:
            so_far = [split(product(so_far[pair], turns[pair][0])) for pair in pairs]
        else:
            for pair in pairs:
                out[pair] = product(so_far[pair], turns[pair][0])


def solve(row, parts):
    each, height, _ = parts[0].shape
    pairs = each * len(parts)
    return pl.pallas_call(
        functools.partial(solve_kernel, len(parts)),
        out_shape=(
            jax.ShapeDtypeStruct((pairs, WIDTH, WIDTH), jnp.float32),
            jax.ShapeDtypeStruct((LAST_ROWS, WIDTH), jnp.float32),
        ),
        in_specs=[SMEM] + [VMEM] * len(parts),
        out_specs=(VMEM, VMEM),
        scratch_shapes=[
            pltpu.VMEM((pairs, height, WIDTH), jnp.float32),
            pltpu.VMEM((pairs, WIDTH, WIDTH), jnp.float32),
            pltpu.VMEM((pairs, WIDTH, WIDTH), jnp.float32),
            pltpu.VMEM((pairs, WIDTH, 2 * WIDTH), jnp.bfloat16),
        ],
        compiler_params=PARAMS,
        name="solve",
    )(row, *parts)


def turned(tracks, columns, held):
    results = []
    for pairs, places in tracks:
        for pair in range(pairs):
            value = jnp.concatenate([piece(columns, place, pair) for place in places], axis=0)
            results.append((value, len(results)))
    return lambda index: product(split(results[index][0]), split(held[index]))


def edge_kernel(tracks, parts, where, sums, held, *refs):
    columns, near, far = refs[: -1 - parts], refs[-1 - parts], refs[-parts:]
    odd = lax.rem(where[0], 2) == 1
    rows = columns[0].shape[1]
    half = rows // 2
    blocks = len(tracks[0][1])
    low_lanes = lax.broadcasted_iota(jnp.int32, (half, WIDTH), 1) < BLOCK
    result = turned(tracks, columns, held)
    last = result(held.shape[0] - 1)
    first = result(0)
    for block in range(blocks):
        span = slice(block * half, (block + 1) * half)
        one = last[block * rows : (block + 1) * rows]
        up = jnp.where(low_lanes, one[:half], pltpu.roll(one[half:], BLOCK, 1))
        one = first[block * rows : (block + 1) * rows]
        down = jnp.where(low_lanes, pltpu.roll(one[:half], BLOCK, 1), one[half:])
        near[span] = jnp.where(odd, down, up)
        each = blocks // parts
        far[block // each][block % each * half : (block % each + 1) * half] = jnp.where(odd, up, down)
    near[-LAST_ROWS:] = sums[...]


def edges(tracks, parts, where, sums, columns, turns):
    half = len(tracks[0][1]) * columns[0].shape[1] // 2
    heights = (half + LAST_ROWS,) + (half // parts,) * parts
    return pl.pallas_call(
        functools.partial(edge_kernel, tracks, parts),
        out_shape=tuple(jax.ShapeDtypeStruct((height, WIDTH), jnp.float32) for height in heights),
        in_specs=[SMEM] + [VMEM] * (2 + len(columns)),
        out_specs=(VMEM,) * (1 + parts),
        compiler_params=PARAMS,
        name="edges",
    )(where, sums, turns, *columns)


def place_kernel(tracks, where, near, held, *refs):
    columns, out, mate = refs[:-2], refs[-2], refs[-1]
    pairs = held.shape[0]
    rows = columns[0].shape[1]
    half = rows // 2
    blocks = len(tracks[0][1])
    odd = lax.rem(where[0], 2) == 1
    is_first = where[0] == 0
    is_last = where[0] == where[1] - 1
    low_lanes = lax.broadcasted_iota(jnp.int32, (rows, WIDTH), 1) < BLOCK
    result = turned(tracks, columns, held)
    rotated = [result(pair) for pair in range(pairs)]
    for block in range(blocks):
        span = slice(block * rows, (block + 1) * rows)
        own_place = jnp.bitwise_xor(where[2], block)
        own_rows = pl.ds(pl.multiple_of(own_place * rows, rows), rows)
        there = jnp.bitwise_xor(own_place, jnp.where(odd, where[3], where[4]))
        arrived = near[pl.ds(pl.multiple_of(there * half, half), half)]
        moved = pltpu.roll(arrived, BLOCK, 1)
        for pair in range(pairs):
            if pair == 0:
                upper = jnp.where(is_first, rotated[0][span], jnp.concatenate([arrived, moved], axis=0))
            else:
                upper = rotated[pair - 1][span]
                if pair == 1:
                    upper = jnp.where(is_first, pltpu.roll(upper, BLOCK, 1), upper)
            if pair == pairs - 1:
                own = pltpu.roll(rotated[pair][span], BLOCK, 1)
                lower = jnp.where(is_last, own, jnp.concatenate([moved, arrived], axis=0))
            else:
                lower = rotated[pair + 1][span]
            value = jnp.where(low_lanes, upper, lower)
            out[own_rows, pair * WIDTH : (pair + 1) * WIDTH] = value
            if pair == 0:
                first = value
            if pair == pairs - 1:
                mate[span] = jnp.where(odd, value, first)


def place(tracks, where, columns, near, turns):
    height = len(tracks[0][1]) * columns[0].shape[1]
    pairs = sum(track[0] for track in tracks)
    return pl.pallas_call(
        functools.partial(place_kernel, tracks),
        out_shape=(
            jax.ShapeDtypeStruct((height, pairs * WIDTH), jnp.float32),
            jax.ShapeDtypeStruct((height, WIDTH), jnp.float32),
        ),
        in_specs=[SMEM] + [VMEM] * (2 + len(columns)),
        out_specs=(VMEM, VMEM),
        compiler_params=PARAMS,
        name="place",
    )(where, near, turns, *columns)


def finish_kernel(blocks, parts, where, mate, *refs):
    far, sums, (_, out, ratio, tile, held, sems) = refs[:parts], refs[parts:-6], refs[-6:]
    rows = mate.shape[0] // blocks
    half = rows // 2
    each = blocks // parts
    odd = lax.rem(where[0], 2) == 1
    used = jnp.where(odd, where[0] < where[1] - 1, where[0] > 0)
    lanes = lax.broadcasted_iota(jnp.int32, (rows, WIDTH), 1)
    first_lane = jnp.where(used, jnp.where(odd, BLOCK, 0), WIDTH)
    here = (lanes >= first_lane) & (lanes < first_lane + BLOCK)
    column = pl.ds(pl.multiple_of(jnp.where(odd, out.shape[1] - WIDTH, 0), WIDTH), WIDTH)
    copies = []
    value = sums[0][...]
    for other in sums[1:]:
        value = value + other[...]
    held[...] = jnp.sqrt(value[:1, :1] / value[:1, 1:2])
    copies.append(pltpu.make_async_copy(held, ratio, sems.at[blocks]))
    copies[-1].start()
    for block in range(blocks):
        span = pl.ds(block * rows, rows)
        own_place = jnp.bitwise_xor(where[2], block)
        there = jnp.bitwise_xor(own_place, jnp.where(odd, where[4], where[3]))
        far_rows = pl.ds(pl.multiple_of(lax.rem(there, each) * half, half), half)
        arrived = far[0][far_rows]
        for part in range(1, parts):
            arrived = jnp.where(there < part * each, arrived, far[part][far_rows])
        moved = pltpu.roll(arrived, BLOCK, 1)
        both = jnp.concatenate([jnp.where(odd, moved, arrived), jnp.where(odd, arrived, moved)], axis=0)
        tile[span] = jnp.where(here, both, mate[span])
        own_rows = pl.ds(pl.multiple_of(own_place * rows, rows), rows)
        copies.append(pltpu.make_async_copy(tile.at[span], out.at[own_rows, column], sems.at[block]))
        copies[-1].start()
    for copy in copies:
        copy.wait()


def finish(blocks, where, far, mate, sums, rotated):
    return pl.pallas_call(
        functools.partial(finish_kernel, blocks, len(far)),
        out_shape=(jax.ShapeDtypeStruct(rotated.shape, jnp.float32), jax.ShapeDtypeStruct((1, 1), jnp.float32)),
        in_specs=[SMEM] + [VMEM] * (1 + len(far) + len(sums)) + [HBM],
        out_specs=(HBM, HBM),
        input_output_aliases={2 + len(far) + len(sums): 0},
        scratch_shapes=[
            pltpu.VMEM(mate.shape, jnp.float32),
            pltpu.VMEM((1, 1), jnp.float32),
            pltpu.SemaphoreType.DMA((blocks + 1,)),
        ],
        compiler_params=PARAMS,
        name="finish",
    )(where, mate, *far, *sums, rotated)


def swapped_in_twos(value, axis, first):
    pairs = []
    for i in range(first, lax.axis_size(axis) - 1, 2):
        pairs += [(i, i + 1), (i + 1, i)]
    return lax.ppermute(value, axis, pairs)


def swapped(value, axis, by):
    count = lax.axis_size(axis)
    return lax.ppermute(value, axis, [(i, i ^ by) for i in range(count)])


def on_device(r_factor, block_slots):
    pair_count = lax.axis_size("pair")
    row_count = lax.axis_size("row")
    pair_index = lax.axis_index("pair")
    row_index = lax.axis_index("row")
    local = r_factor.shape[1] // WIDTH // pair_count
    shared = local % 2 == 0 and row_count > 1 and row_count & (row_count - 1) == 0
    shares = 2 if shared else 1
    row = row_index.astype(jnp.int32).reshape(1)
    base = pair_index.astype(jnp.int32).reshape(1)
    if shared and pair_count == 8:
        ahead = local * AHEAD // 4
        plan = [(local, 0, local, (position,)) for position in (0, 2, 4, 1, 3, 5, 7)]
        plan += [(local, 0, ahead, (6,)), (local, ahead, local - ahead, (6,))]
        arranged = gather(r_factor, block_slots, base, tuple(plan))
        here, early, late = arranged[:3], arranged[7], arranged[8]
        near = [swapped(value, "pair", 1) for value in arranged[3:7]]
        early = swapped(early, "pair", 6)
        plan = [[((side, 0, pair), (side + 3, 0, pair)) for pair in range(local)] for side in range(3)]
        plan.append([((7, 0, pair), (6, 0, pair)) for pair in range(ahead)])
        plan[3] += [((8, 0, pair - ahead), (6, 0, pair)) for pair in range(ahead, local)]
        own, *given = near_grams(plan, *here, *near, arranged[7], late)
        taken = [swapped(value, "pair", by) for by, value in zip((2, 4, 6), given)]
        single = tuple((4, pair) for pair in range(local)) + tuple((5, pair) for pair in range(local - ahead))
        plan = ((local, ((0, 0), (2, 0))), (local, ((1, 0), (3, 0))), (1, single))
        going = joined(given[0], plan, here[1], here[2], near[1], near[2], near[3], late)
        early, going, taken = lax.optimization_barrier((early, going, taken))
        parts = merge(row, [own] + taken, shares)
        from_far = [swapped(value, "pair", by) for by, value in zip((2, 4, 6), going)]
        columns = (here[0], near[0], early, *from_far)
        tracks = []
        for pair in range(local):
            places = [(operand, place, pair) for operand, place in ((0, 0), (1, 0), (3, 0), (3, 1), (4, 0), (4, 1))]
            places.append((2, 0, pair) if pair < ahead else (5, local + pair - ahead, 0))
            tracks.append((1, (*places, (5, pair, 0))))
        tracks = tuple(tracks)
        bases = (pair_index, pair_index - 1, pair_index + 1)
    else:
        (arranged,) = gather(r_factor, block_slots, base, ((local, 0, local, None),))
        column = lax.all_to_all(arranged, "pair", split_axis=0, concat_axis=0, tiled=True)
        parts = grams(row, column, shares)
        columns = (column,)
        tracks = ((local, tuple((0, group, 0) for group in range(pair_count))),)
        bases = (jnp.zeros_like(pair_index),) * 3
    if shared:
        half = parts[0] + swapped(parts[1], "row", 1)
        for bit in range(1, row_count.bit_length() - 1):
            half = half + swapped(half, "row", 1 << bit)
        parts = (half, swapped(half, "row", 1))
    else:
        parts = (lax.psum(parts[0], "row"),)
    turns, sums = solve(row, parts)
    bases = [jnp.clip(value, 0, pair_count - 1) for value in bases]
    where = jnp.stack([pair_index, jnp.int32(pair_count)] + bases).astype(jnp.int32)
    near, *far = edges(tracks, FAR_PARTS if pair_count % FAR_PARTS == 0 else 1, where, sums, columns, turns)
    far = [swapped_in_twos(part, "pair", 1) for part in far]
    near = swapped_in_twos(near, "pair", 0)
    rotated, mate = place(tracks, where, columns, near, turns)
    if pair_count == 8:
        sums = sums + near[-LAST_ROWS:]
        sums = [sums] + [swapped(sums, "pair", by) for by in (2, 4, 6)]
    else:
        sums = [lax.psum(sums, "pair")]
    rotated, off_ratio = finish(pair_count, where, far, mate, sums, rotated)
    return (rotated, off_ratio.reshape(()))


def solution(mesh):
    in_specs = (P(("row", "pair"), None), P())
    out_specs = (P("row", "pair"), P())
    return jax.shard_map(
        on_device, mesh=mesh, in_specs=in_specs, out_specs=out_specs, check_vma=False
    )
```

```python
import functools

import jax
import jax.numpy as jnp
from jax import lax
from jax.experimental import pallas as pl
from jax.experimental.pallas import tpu as pltpu
from jax.sharding import PartitionSpec as P

BLOCK = 64
WIDTH = 2 * BLOCK
ITERS = 3
TOLERANCE = 1e-8
LAST_ROWS = 8
AHEAD = 3
FAR_PARTS = 1
GATHER_CHUNKS = 2
GATHER_VMEM = 62 * 1024 * 1024
VMEM = pl.BlockSpec(memory_space=pltpu.VMEM)
SMEM = pl.BlockSpec(memory_space=pltpu.SMEM)
HBM = pl.BlockSpec(memory_space=pltpu.HBM)
PARAMS = pltpu.CompilerParams(vmem_limit_bytes=48 * 1024 * 1024)


def split(value):
    high = value.astype(jnp.bfloat16)
    low = (value - high.astype(jnp.float32)).astype(jnp.bfloat16)
    return jnp.concatenate([high, low], axis=1)


def product(left, right):
    both = jnp.dot(left, jnp.concatenate([right, right], axis=0), preferred_element_type=jnp.float32)
    half = both.shape[1] // 2
    return both[:, :half] + both[:, half:]


def unit(size):
    row_ids = lax.broadcasted_iota(jnp.int32, (size, size), 0)
    col_ids = lax.broadcasted_iota(jnp.int32, (size, size), 1)
    return row_ids == col_ids


def total(value):
    return jnp.sum(jnp.sum(value, axis=1, keepdims=True), axis=0, keepdims=True)


def gather_kernel(plan, slots, source, *outs):
    rows = source.shape[0]
    local = plan[0][0]
    base = slots[slots.shape[0] - 1]
    low_lanes = lax.broadcasted_iota(jnp.int32, (rows, WIDTH), 1) < BLOCK

    def tile(block):
        return source[:, pl.ds(pl.multiple_of(lax.shift_right_logical(block, 1) * WIDTH, WIDTH), WIDTH)]

    def one_pair(slot):
        upper_block, lower_block = slots[slot], slots[slot + 1]
        upper, lower = tile(upper_block), tile(lower_block)
        turned_over = pltpu.roll(jnp.where(low_lanes, lower, upper), BLOCK, 1)
        upper = jnp.where(jnp.bitwise_and(upper_block, 1) == 0, upper, turned_over)
        lower = jnp.where(jnp.bitwise_and(lower_block, 1) == 1, lower, turned_over)
        return jnp.where(low_lanes, upper, lower)

    for (_, first, positions), out in zip(plan, outs):
        count = out.shape[2] // WIDTH

        def one_group(group, place, first=first, count=count, out=out):
            for pair in range(count):
                value = one_pair(2 * (group * local + first + pair))
                out[place, :, pair * WIDTH : (pair + 1) * WIDTH] = value

        if positions is None:

            def step(group, carry, one_group=one_group):
                one_group(group, group)
                return carry

            lax.fori_loop(0, out.shape[0], step, 0)
        else:
            for place, position in enumerate(positions):
                one_group(jnp.bitwise_xor(base, position), place)


def gather(r_factor, block_slots, base, plan):
    rows = r_factor.shape[0]
    groups = r_factor.shape[1] // WIDTH // plan[0][0]
    shapes = []
    for _, _, taken, positions in plan:
        count = groups if positions is None else len(positions)
        shapes.append(jax.ShapeDtypeStruct((count, rows, taken * WIDTH), jnp.float32))
    return pl.pallas_call(
        functools.partial(gather_kernel, tuple((local, first, positions) for local, first, _, positions in plan)),
        out_shape=tuple(shapes),
        in_specs=[SMEM, VMEM],
        out_specs=(VMEM,) * len(shapes),
        compiler_params=PARAMS,
        name="gather",
    )(jnp.concatenate([block_slots, base]), r_factor)


def gram(pieces):
    parts = split(jnp.concatenate(pieces, axis=0))
    four = lax.dot_general(parts, parts, (((0,), (0,)), ((), ())), preferred_element_type=jnp.float32)
    half = four[:WIDTH] + four[WIDTH:]
    return half[:, :WIDTH] + half[:, WIDTH:]


def piece(refs, where, pair):
    operand, place, first = where
    return refs[operand][place, :, (first + pair) * WIDTH : (first + pair + 1) * WIDTH]


def deal(row, held, outs):
    each = outs[0].shape[0]
    for by, out in enumerate(outs):
        out[...] = held[pl.ds(jnp.bitwise_xor(jnp.bitwise_and(row, len(outs) - 1), by) * each, each)]


def grams_kernel(row, column, *refs):
    outs, held = refs[:-1], refs[-1]
    groups = column.shape[0]
    for pair in range(held.shape[0]):
        held[pair] = gram([piece([column], (0, group, 0), pair) for group in range(groups)])
    deal(row[0], held, outs)


def grams(row, column, shares):
    pairs = column.shape[2] // WIDTH
    return pl.pallas_call(
        grams_kernel,
        out_shape=(jax.ShapeDtypeStruct((pairs // shares, WIDTH, WIDTH), jnp.float32),) * shares,
        in_specs=[SMEM, VMEM],
        out_specs=(VMEM,) * shares,
        scratch_shapes=[pltpu.VMEM((pairs, WIDTH, WIDTH), jnp.float32)],
        compiler_params=PARAMS,
        name="grams",
    )(row, column)


def pack(gram_matrix):
    half = WIDTH // 2
    top = gram_matrix[:half]
    last = pltpu.roll(gram_matrix[half:], half, 1)
    row_ids = lax.broadcasted_iota(jnp.int32, (half, WIDTH), 0)
    col_ids = lax.broadcasted_iota(jnp.int32, (half, WIDTH), 1)
    ends = jnp.sum(jnp.where(row_ids == col_ids, last, 0.0), axis=0, keepdims=True)
    both = jnp.where((col_ids < half) & (row_ids > col_ids), last, top)
    return jnp.concatenate([both, jnp.broadcast_to(ends, (LAST_ROWS, WIDTH))], axis=0)


def unpack(packed):
    half = WIDTH // 2
    both = packed[:half]
    ends = packed[half : half + 1]
    mirrored = jnp.transpose(jnp.concatenate([both, both], axis=0))
    row_ids = lax.broadcasted_iota(jnp.int32, (half, WIDTH), 0)
    col_ids = lax.broadcasted_iota(jnp.int32, (half, WIDTH), 1)
    top = jnp.where((col_ids < half) & (row_ids > col_ids), mirrored[:half], both)
    last = jnp.where(row_ids > col_ids, both, mirrored[:half])
    last = jnp.where(row_ids == col_ids, ends, last)
    bottom = jnp.where(col_ids < half, mirrored[half:], pltpu.roll(last, half, 1))
    return jnp.concatenate([top, bottom], axis=0)


PACKED = WIDTH // 2 + LAST_ROWS


def near_grams_kernel(plan, *refs):
    sources, outs = refs[: -len(plan)], refs[-len(plan) :]
    for places, out in zip(plan, outs):
        for pair in range(out.shape[0]):
            out[pair] = pack(gram([piece(sources, place, 0) for place in places[pair]]))


def near_grams(plan, *sources):
    return pl.pallas_call(
        functools.partial(near_grams_kernel, plan),
        out_shape=tuple(jax.ShapeDtypeStruct((len(places), PACKED, WIDTH), jnp.float32) for places in plan),
        in_specs=[VMEM] * len(sources),
        out_specs=(VMEM,) * len(plan),
        compiler_params=PARAMS,
        name="near_grams",
    )(*sources)


def joined_kernel(plan, after, *refs):
    del after
    sources, outs = refs[: -len(plan)], refs[-len(plan) :]
    for places, out in zip(plan, outs):
        for place, (source, first) in enumerate(places):
            out[place] = sources[source][0, :, first * WIDTH : first * WIDTH + out.shape[2]]


def joined(after, plan, *sources):
    rows = sources[0].shape[1]
    return pl.pallas_call(
        functools.partial(joined_kernel, tuple(places for _, places in plan)),
        out_shape=tuple(jax.ShapeDtypeStruct((len(places), rows, pairs * WIDTH), jnp.float32) for pairs, places in plan),
        in_specs=[pl.BlockSpec(memory_space=pl.ANY)] + [VMEM] * len(sources),
        out_specs=(VMEM,) * len(plan),
        compiler_params=PARAMS,
        name="joined",
    )(after, *sources)


def merge_kernel(count, row, *refs):
    parts, outs, held = refs[:count], refs[count:-1], refs[-1]
    value = parts[0][...]
    for part in parts[1:]:
        value = value + part[...]
    held[...] = value
    deal(row[0], held, outs)


def merge(row, parts, shares):
    pairs, height, _ = parts[0].shape
    return pl.pallas_call(
        functools.partial(merge_kernel, len(parts)),
        out_shape=(jax.ShapeDtypeStruct((pairs // shares, height, WIDTH), jnp.float32),) * shares,
        in_specs=[SMEM] + [VMEM] * len(parts),
        out_specs=(VMEM,) * shares,
        scratch_shapes=[pltpu.VMEM((pairs, height, WIDTH), jnp.float32)],
        compiler_params=PARAMS,
        name="merge",
    )(row, *parts)


def rotations(grams_now, on_diag, even, odd, power):
    diag_one = jnp.where(on_diag, 1.0, 0.0)
    size = diag_one.shape[0]
    skews, skews_parts, squares = [], [], []
    for gram_now in grams_now:
        diag_part = jnp.where(on_diag, gram_now, 0.0)
        across = jnp.sum(diag_part, axis=1, keepdims=True)
        down = jnp.sum(diag_part, axis=0, keepdims=True)
        skew = gram_now * (across - down) / (2.0 * (across * across + down * down))
        skews.append(jnp.clip(skew, -0.25, 0.25))
    for skew in skews:
        skews_parts.append(split(skew))
        squares.append(product(skews_parts[-1], skews_parts[-1]))
    evens, odds, rests, worst = [], [], [], None
    for skew, parts, square in zip(skews, skews_parts, squares):
        bound = jnp.sqrt(0.5 * total(square * square))
        scale = 2.0 / (2.0 + bound)
        rate = bound / (2.0 + bound)
        worst = rate if worst is None else jnp.maximum(worst, rate)
        rest = (1.0 - scale) * diag_one + scale * square
        rest_parts = split(rest)
        first = product(jnp.concatenate([parts, rest_parts], axis=0), rest_parts)
        evens.append(scale * (diag_one + rest))
        odds.append(scale * (skew + first[:size]))
        rests.append(split(first[size:]))
    for index, rest_parts in enumerate(rests):
        stack = jnp.concatenate([split(evens[index]), split(odds[index]), rest_parts], axis=0)
        second = product(stack, rest_parts)
        evens[index] = evens[index] + second[:size]
        odds[index] = odds[index] + second[size : 2 * size]
        rests[index] = split(second[2 * size :])
    for index, rest_parts in enumerate(rests):
        third = product(jnp.concatenate([split(evens[index]), split(odds[index])], axis=0), rest_parts)
        even[index] = evens[index] + third[:size]
        odd[index] = odds[index] + third[size:]
        power[index] = rest_parts

    def more(left):
        return left > TOLERANCE

    def step(left):
        for index in range(len(grams_now)):
            old = power[index]
            parts = split(product(old, old))
            power[index] = parts
            even[index] += product(split(even[index]), parts)
            odd[index] += product(split(odd[index]), parts)
        return left * left

    worst = worst * worst
    worst = worst * worst
    left = (worst * worst)[0, 0]
    lax.while_loop(more, step, left)

    def refine(_, carry):
        for index in range(len(grams_now)):
            parts = split(skews[index])
            even_now, odd_now = even[index], odd[index]
            even_parts, odd_parts = split(even_now), split(odd_now)
            even_rest = split(diag_one - even_now + product(parts, odd_parts))
            odd_rest = split(product(parts, even_parts) - odd_now)
            even[index] = even_now + product(even_parts, even_rest) + product(odd_parts, odd_rest)
            odd[index] = odd_now + product(even_parts, odd_rest) + product(odd_parts, even_rest)
        return carry

    lax.fori_loop(0, jnp.where(left > TOLERANCE, 2, 0), refine, 0)
    results = []
    for index in range(len(grams_now)):
        even_now = 2.0 * even[index] - diag_one
        odd_now = 2.0 * odd[index]
        results.append((split(even_now - odd_now), split(even_now + odd_now)))
    return results


def solve_kernel(count, row, *refs):
    parts, out, sums, held, even, odd, power = refs[:count], *refs[count:]
    on_diag = unit(WIDTH)
    pairs = range(out.shape[0])
    each = parts[0].shape[0]
    for by, part in enumerate(parts):
        held[pl.ds(jnp.bitwise_xor(jnp.bitwise_and(row[0], count - 1), by) * each, each)] = part[...]
    off_total = jnp.zeros((1, 1), jnp.float32)
    diag_total = jnp.zeros((1, 1), jnp.float32)
    now = []
    for pair in pairs:
        gram_now = held[pair]
        if gram_now.shape[0] != WIDTH:
            gram_now = unpack(gram_now)
        squares = gram_now * gram_now
        off_total += total(jnp.where(on_diag, 0.0, squares))
        diag_total += total(jnp.where(on_diag, squares, 0.0))
        now.append(gram_now)
    first_lane = lax.broadcasted_iota(jnp.int32, sums.shape, 1) == 0
    sums[...] = jnp.where(first_lane, off_total, diag_total)
    so_far = None
    for sweep in range(ITERS):
        turns = rotations(now, on_diag, even, odd, power)
        if sweep < ITERS - 1:
            halves = [split(product(split(now[pair]), turns[pair][0])) for pair in pairs]
            now = [product(turns[pair][1], halves[pair]) for pair in pairs]
        if so_far is None:
            so_far = [turns[pair][0] for pair in pairs]
        elif sweep < ITERS - 1:
            so_far = [split(product(so_far[pair], turns[pair][0])) for pair in pairs]
        else:
            for pair in pairs:
                out[pair] = product(so_far[pair], turns[pair][0])


def solve(row, parts):
    each, height, _ = parts[0].shape
    pairs = each * len(parts)
    return pl.pallas_call(
        functools.partial(solve_kernel, len(parts)),
        out_shape=(
            jax.ShapeDtypeStruct((pairs, WIDTH, WIDTH), jnp.float32),
            jax.ShapeDtypeStruct((LAST_ROWS, WIDTH), jnp.float32),
        ),
        in_specs=[SMEM] + [VMEM] * len(parts),
        out_specs=(VMEM, VMEM),
        scratch_shapes=[
            pltpu.VMEM((pairs, height, WIDTH), jnp.float32),
            pltpu.VMEM((pairs, WIDTH, WIDTH), jnp.float32),
            pltpu.VMEM((pairs, WIDTH, WIDTH), jnp.float32),
            pltpu.VMEM((pairs, WIDTH, 2 * WIDTH), jnp.bfloat16),
        ],
        compiler_params=PARAMS,
        name="solve",
    )(row, *parts)


def turned(tracks, columns, held):
    results = []
    for pairs, places in tracks:
        for pair in range(pairs):
            value = jnp.concatenate([piece(columns, place, pair) for place in places], axis=0)
            results.append((value, len(results)))
    return lambda index: product(split(results[index][0]), split(held[index]))


def edge_kernel(tracks, parts, where, sums, held, *refs):
    columns, near, far = refs[: -1 - parts], refs[-1 - parts], refs[-parts:]
    odd = lax.rem(where[0], 2) == 1
    rows = columns[0].shape[1]
    half = rows // 2
    blocks = len(tracks[0][1])
    low_lanes = lax.broadcasted_iota(jnp.int32, (half, WIDTH), 1) < BLOCK
    result = turned(tracks, columns, held)
    last = result(held.shape[0] - 1)
    first = result(0)
    for block in range(blocks):
        span = slice(block * half, (block + 1) * half)
        one = last[block * rows : (block + 1) * rows]
        up = jnp.where(low_lanes, one[:half], pltpu.roll(one[half:], BLOCK, 1))
        one = first[block * rows : (block + 1) * rows]
        down = jnp.where(low_lanes, pltpu.roll(one[:half], BLOCK, 1), one[half:])
        near[span] = jnp.where(odd, down, up)
        each = blocks // parts
        far[block // each][block % each * half : (block % each + 1) * half] = jnp.where(odd, up, down)
    near[-LAST_ROWS:] = sums[...]


def edges(tracks, parts, where, sums, columns, turns):
    half = len(tracks[0][1]) * columns[0].shape[1] // 2
    heights = (half + LAST_ROWS,) + (half // parts,) * parts
    return pl.pallas_call(
        functools.partial(edge_kernel, tracks, parts),
        out_shape=tuple(jax.ShapeDtypeStruct((height, WIDTH), jnp.float32) for height in heights),
        in_specs=[SMEM] + [VMEM] * (2 + len(columns)),
        out_specs=(VMEM,) * (1 + parts),
        compiler_params=PARAMS,
        name="edges",
    )(where, sums, turns, *columns)


def place_kernel(tracks, where, near, held, *refs):
    columns, out, mate = refs[:-2], refs[-2], refs[-1]
    pairs = held.shape[0]
    rows = columns[0].shape[1]
    half = rows // 2
    blocks = len(tracks[0][1])
    odd = lax.rem(where[0], 2) == 1
    is_first = where[0] == 0
    is_last = where[0] == where[1] - 1
    low_lanes = lax.broadcasted_iota(jnp.int32, (rows, WIDTH), 1) < BLOCK
    result = turned(tracks, columns, held)
    rotated = [result(pair) for pair in range(pairs)]
    for block in range(blocks):
        span = slice(block * rows, (block + 1) * rows)
        own_place = jnp.bitwise_xor(where[2], block)
        own_rows = pl.ds(pl.multiple_of(own_place * rows, rows), rows)
        there = jnp.bitwise_xor(own_place, jnp.where(odd, where[3], where[4]))
        arrived = near[pl.ds(pl.multiple_of(there * half, half), half)]
        moved = pltpu.roll(arrived, BLOCK, 1)
        for pair in range(pairs):
            if pair == 0:
                upper = jnp.where(is_first, rotated[0][span], jnp.concatenate([arrived, moved], axis=0))
            else:
                upper = rotated[pair - 1][span]
                if pair == 1:
                    upper = jnp.where(is_first, pltpu.roll(upper, BLOCK, 1), upper)
            if pair == pairs - 1:
                own = pltpu.roll(rotated[pair][span], BLOCK, 1)
                lower = jnp.where(is_last, own, jnp.concatenate([moved, arrived], axis=0))
            else:
                lower = rotated[pair + 1][span]
            value = jnp.where(low_lanes, upper, lower)
            out[own_rows, pair * WIDTH : (pair + 1) * WIDTH] = value
            if pair == 0:
                first = value
            if pair == pairs - 1:
                mate[span] = jnp.where(odd, value, first)


def place(tracks, where, columns, near, turns):
    height = len(tracks[0][1]) * columns[0].shape[1]
    pairs = sum(track[0] for track in tracks)
    return pl.pallas_call(
        functools.partial(place_kernel, tracks),
        out_shape=(
            jax.ShapeDtypeStruct((height, pairs * WIDTH), jnp.float32),
            jax.ShapeDtypeStruct((height, WIDTH), jnp.float32),
        ),
        in_specs=[SMEM] + [VMEM] * (2 + len(columns)),
        out_specs=(VMEM, VMEM),
        compiler_params=PARAMS,
        name="place",
    )(where, near, turns, *columns)


def finish_kernel(blocks, parts, where, mate, *refs):
    far, sums, (_, out, ratio, tile, held, sems) = refs[:parts], refs[parts:-6], refs[-6:]
    rows = mate.shape[0] // blocks
    half = rows // 2
    each = blocks // parts
    odd = lax.rem(where[0], 2) == 1
    used = jnp.where(odd, where[0] < where[1] - 1, where[0] > 0)
    lanes = lax.broadcasted_iota(jnp.int32, (rows, WIDTH), 1)
    first_lane = jnp.where(used, jnp.where(odd, BLOCK, 0), WIDTH)
    here = (lanes >= first_lane) & (lanes < first_lane + BLOCK)
    column = pl.ds(pl.multiple_of(jnp.where(odd, out.shape[1] - WIDTH, 0), WIDTH), WIDTH)
    copies = []
    value = sums[0][...]
    for other in sums[1:]:
        value = value + other[...]
    held[...] = jnp.sqrt(value[:1, :1] / value[:1, 1:2])
    copies.append(pltpu.make_async_copy(held, ratio, sems.at[blocks]))
    copies[-1].start()
    for block in range(blocks):
        span = pl.ds(block * rows, rows)
        own_place = jnp.bitwise_xor(where[2], block)
        there = jnp.bitwise_xor(own_place, jnp.where(odd, where[4], where[3]))
        far_rows = pl.ds(pl.multiple_of(lax.rem(there, each) * half, half), half)
        arrived = far[0][far_rows]
        for part in range(1, parts):
            arrived = jnp.where(there < part * each, arrived, far[part][far_rows])
        moved = pltpu.roll(arrived, BLOCK, 1)
        both = jnp.concatenate([jnp.where(odd, moved, arrived), jnp.where(odd, arrived, moved)], axis=0)
        tile[span] = jnp.where(here, both, mate[span])
        own_rows = pl.ds(pl.multiple_of(own_place * rows, rows), rows)
        copies.append(pltpu.make_async_copy(tile.at[span], out.at[own_rows, column], sems.at[block]))
        copies[-1].start()
    for copy in copies:
        copy.wait()


def finish(blocks, where, far, mate, sums, rotated):
    return pl.pallas_call(
        functools.partial(finish_kernel, blocks, len(far)),
        out_shape=(jax.ShapeDtypeStruct(rotated.shape, jnp.float32), jax.ShapeDtypeStruct((1, 1), jnp.float32)),
        in_specs=[SMEM] + [VMEM] * (1 + len(far) + len(sums)) + [HBM],
        out_specs=(HBM, HBM),
        input_output_aliases={2 + len(far) + len(sums): 0},
        scratch_shapes=[
            pltpu.VMEM(mate.shape, jnp.float32),
            pltpu.VMEM((1, 1), jnp.float32),
            pltpu.SemaphoreType.DMA((blocks + 1,)),
        ],
        compiler_params=PARAMS,
        name="finish",
    )(where, mate, *far, *sums, rotated)


def swapped_in_twos(value, axis, first):
    pairs = []
    for i in range(first, lax.axis_size(axis) - 1, 2):
        pairs += [(i, i + 1), (i + 1, i)]
    return lax.ppermute(value, axis, pairs)


def swapped(value, axis, by):
    count = lax.axis_size(axis)
    return lax.ppermute(value, axis, [(i, i ^ by) for i in range(count)])


def on_device(r_factor, block_slots):
    pair_count = lax.axis_size("pair")
    row_count = lax.axis_size("row")
    pair_index = lax.axis_index("pair")
    row_index = lax.axis_index("row")
    local = r_factor.shape[1] // WIDTH // pair_count
    shared = local % 2 == 0 and row_count > 1 and row_count & (row_count - 1) == 0
    shares = 2 if shared else 1
    row = row_index.astype(jnp.int32).reshape(1)
    base = pair_index.astype(jnp.int32).reshape(1)
    if shared and pair_count == 8:
        ahead = local * AHEAD // 4
        plan = [(local, 0, local, (position,)) for position in (0, 2, 4, 1, 3, 5, 7)]
        plan += [(local, 0, ahead, (6,)), (local, ahead, local - ahead, (6,))]
        arranged = gather(r_factor, block_slots, base, tuple(plan))
        here, early, late = arranged[:3], arranged[7], arranged[8]
        near = [swapped(value, "pair", 1) for value in arranged[3:7]]
        early = swapped(early, "pair", 6)
        plan = [[((side, 0, pair), (side + 3, 0, pair)) for pair in range(local)] for side in range(3)]
        plan.append([((7, 0, pair), (6, 0, pair)) for pair in range(ahead)])
        plan[3] += [((8, 0, pair - ahead), (6, 0, pair)) for pair in range(ahead, local)]
        own, *given = near_grams(plan, *here, *near, arranged[7], late)
        taken = [swapped(value, "pair", by) for by, value in zip((2, 4, 6), given)]
        single = tuple((4, pair) for pair in range(local)) + tuple((5, pair) for pair in range(local - ahead))
        plan = ((local, ((0, 0), (2, 0))), (local, ((1, 0), (3, 0))), (1, single))
        going = joined(given[0], plan, here[1], here[2], near[1], near[2], near[3], late)
        early, going, taken = lax.optimization_barrier((early, going, taken))
        parts = merge(row, [own] + taken, shares)
        from_far = [swapped(value, "pair", by) for by, value in zip((2, 4, 6), going)]
        columns = (here[0], near[0], early, *from_far)
        tracks = []
        for pair in range(local):
            places = [(operand, place, pair) for operand, place in ((0, 0), (1, 0), (3, 0), (3, 1), (4, 0), (4, 1))]
            places.append((2, 0, pair) if pair < ahead else (5, local + pair - ahead, 0))
            tracks.append((1, (*places, (5, pair, 0))))
        tracks = tuple(tracks)
        bases = (pair_index, pair_index - 1, pair_index + 1)
    else:
        (arranged,) = gather(r_factor, block_slots, base, ((local, 0, local, None),))
        column = lax.all_to_all(arranged, "pair", split_axis=0, concat_axis=0, tiled=True)
        parts = grams(row, column, shares)
        columns = (column,)
        tracks = ((local, tuple((0, group, 0) for group in range(pair_count))),)
        bases = (jnp.zeros_like(pair_index),) * 3
    if shared:
        half = parts[0] + swapped(parts[1], "row", 1)
        for bit in range(1, row_count.bit_length() - 1):
            half = half + swapped(half, "row", 1 << bit)
        parts = (half, swapped(half, "row", 1))
    else:
        parts = (lax.psum(parts[0], "row"),)
    turns, sums = solve(row, parts)
    bases = [jnp.clip(value, 0, pair_count - 1) for value in bases]
    where = jnp.stack([pair_index, jnp.int32(pair_count)] + bases).astype(jnp.int32)
    near, *far = edges(tracks, FAR_PARTS if pair_count % FAR_PARTS == 0 else 1, where, sums, columns, turns)
    far = [swapped_in_twos(part, "pair", 1) for part in far]
    near = swapped_in_twos(near, "pair", 0)
    rotated, mate = place(tracks, where, columns, near, turns)
    if pair_count == 8:
        sums = sums + near[-LAST_ROWS:]
        sums = [sums] + [swapped(sums, "pair", by) for by in (2, 4, 6)]
    else:
        sums = [lax.psum(sums, "pair")]
    rotated, off_ratio = finish(pair_count, where, far, mate, sums, rotated)
    return (rotated, off_ratio.reshape(()))


def solution(mesh):
    in_specs = (P(("row", "pair"), None), P())
    out_specs = (P("row", "pair"), P())
    return jax.shard_map(
        on_device, mesh=mesh, in_specs=in_specs, out_specs=out_specs, check_vma=False
    )
```

```python
import functools

import jax
import jax.numpy as jnp
from jax import lax
from jax.experimental import pallas as pl
from jax.experimental.pallas import tpu as pltpu
from jax.sharding import PartitionSpec as P

BLOCK = 64
WIDTH = 2 * BLOCK
ITERS = 3
TOLERANCE = 1e-8
LAST_ROWS = 8
AHEAD = 3
FAR_PARTS = 1
GATHER_CHUNKS = 2
GATHER_VMEM = 62 * 1024 * 1024
VMEM = pl.BlockSpec(memory_space=pltpu.VMEM)
SMEM = pl.BlockSpec(memory_space=pltpu.SMEM)
HBM = pl.BlockSpec(memory_space=pltpu.HBM)
PARAMS = pltpu.CompilerParams(vmem_limit_bytes=48 * 1024 * 1024)


def split(value):
    high = value.astype(jnp.bfloat16)
    low = (value - high.astype(jnp.float32)).astype(jnp.bfloat16)
    return jnp.concatenate([high, low], axis=1)


def product(left, right):
    both = jnp.dot(left, jnp.concatenate([right, right], axis=0), preferred_element_type=jnp.float32)
    half = both.shape[1] // 2
    return both[:, :half] + both[:, half:]


def unit(size):
    row_ids = lax.broadcasted_iota(jnp.int32, (size, size), 0)
    col_ids = lax.broadcasted_iota(jnp.int32, (size, size), 1)
    return row_ids == col_ids


def total(value):
    return jnp.sum(jnp.sum(value, axis=1, keepdims=True), axis=0, keepdims=True)


def gather_kernel(plan, slots, source, *outs):
    rows = source.shape[0]
    local = plan[0][0]
    base = slots[slots.shape[0] - 1]
    low_lanes = lax.broadcasted_iota(jnp.int32, (rows, WIDTH), 1) < BLOCK

    def tile(block):
        return source[:, pl.ds(pl.multiple_of(lax.shift_right_logical(block, 1) * WIDTH, WIDTH), WIDTH)]

    def one_pair(slot):
        upper_block, lower_block = slots[slot], slots[slot + 1]
        upper, lower = tile(upper_block), tile(lower_block)
        turned_over = pltpu.roll(jnp.where(low_lanes, lower, upper), BLOCK, 1)
        upper = jnp.where(jnp.bitwise_and(upper_block, 1) == 0, upper, turned_over)
        lower = jnp.where(jnp.bitwise_and(lower_block, 1) == 1, lower, turned_over)
        return jnp.where(low_lanes, upper, lower)

    for (_, first, positions), out in zip(plan, outs):
        count = out.shape[2] // WIDTH

        def one_group(group, place, first=first, count=count, out=out):
            for pair in range(count):
                value = one_pair(2 * (group * local + first + pair))
                out[place, :, pair * WIDTH : (pair + 1) * WIDTH] = value

        if positions is None:

            def step(group, carry, one_group=one_group):
                one_group(group, group)
                return carry

            lax.fori_loop(0, out.shape[0], step, 0)
        else:
            for place, position in enumerate(positions):
                one_group(jnp.bitwise_xor(base, position), place)


def gather(r_factor, block_slots, base, plan):
    rows = r_factor.shape[0]
    groups = r_factor.shape[1] // WIDTH // plan[0][0]
    shapes = []
    for _, _, taken, positions in plan:
        count = groups if positions is None else len(positions)
        shapes.append(jax.ShapeDtypeStruct((count, rows, taken * WIDTH), jnp.float32))
    return pl.pallas_call(
        functools.partial(gather_kernel, tuple((local, first, positions) for local, first, _, positions in plan)),
        out_shape=tuple(shapes),
        in_specs=[SMEM, VMEM],
        out_specs=(VMEM,) * len(shapes),
        compiler_params=PARAMS,
        name="gather",
    )(jnp.concatenate([block_slots, base]), r_factor)


def gram(pieces):
    parts = split(jnp.concatenate(pieces, axis=0))
    four = lax.dot_general(parts, parts, (((0,), (0,)), ((), ())), preferred_element_type=jnp.float32)
    half = four[:WIDTH] + four[WIDTH:]
    return half[:, :WIDTH] + half[:, WIDTH:]


def piece(refs, where, pair):
    operand, place, first = where
    return refs[operand][place, :, (first + pair) * WIDTH : (first + pair + 1) * WIDTH]


def deal(row, held, outs):
    each = outs[0].shape[0]
    for by, out in enumerate(outs):
        out[...] = held[pl.ds(jnp.bitwise_xor(jnp.bitwise_and(row, len(outs) - 1), by) * each, each)]


def grams_kernel(row, column, *refs):
    outs, held = refs[:-1], refs[-1]
    groups = column.shape[0]
    for pair in range(held.shape[0]):
        held[pair] = gram([piece([column], (0, group, 0), pair) for group in range(groups)])
    deal(row[0], held, outs)


def grams(row, column, shares):
    pairs = column.shape[2] // WIDTH
    return pl.pallas_call(
        grams_kernel,
        out_shape=(jax.ShapeDtypeStruct((pairs // shares, WIDTH, WIDTH), jnp.float32),) * shares,
        in_specs=[SMEM, VMEM],
        out_specs=(VMEM,) * shares,
        scratch_shapes=[pltpu.VMEM((pairs, WIDTH, WIDTH), jnp.float32)],
        compiler_params=PARAMS,
        name="grams",
    )(row, column)


def pack(gram_matrix):
    half = WIDTH // 2
    top = gram_matrix[:half]
    last = pltpu.roll(gram_matrix[half:], half, 1)
    row_ids = lax.broadcasted_iota(jnp.int32, (half, WIDTH), 0)
    col_ids = lax.broadcasted_iota(jnp.int32, (half, WIDTH), 1)
    ends = jnp.sum(jnp.where(row_ids == col_ids, last, 0.0), axis=0, keepdims=True)
    both = jnp.where((col_ids < half) & (row_ids > col_ids), last, top)
    return jnp.concatenate([both, jnp.broadcast_to(ends, (LAST_ROWS, WIDTH))], axis=0)


def unpack(packed):
    half = WIDTH // 2
    both = packed[:half]
    ends = packed[half : half + 1]
    mirrored = jnp.transpose(jnp.concatenate([both, both], axis=0))
    row_ids = lax.broadcasted_iota(jnp.int32, (half, WIDTH), 0)
    col_ids = lax.broadcasted_iota(jnp.int32, (half, WIDTH), 1)
    top = jnp.where((col_ids < half) & (row_ids > col_ids), mirrored[:half], both)
    last = jnp.where(row_ids > col_ids, both, mirrored[:half])
    last = jnp.where(row_ids == col_ids, ends, last)
    bottom = jnp.where(col_ids < half, mirrored[half:], pltpu.roll(last, half, 1))
    return jnp.concatenate([top, bottom], axis=0)


PACKED = WIDTH // 2 + LAST_ROWS


def near_grams_kernel(plan, *refs):
    sources, outs = refs[: -len(plan)], refs[-len(plan) :]
    for places, out in zip(plan, outs):
        for pair in range(out.shape[0]):
            out[pair] = pack(gram([piece(sources, place, 0) for place in places[pair]]))


def near_grams(plan, *sources):
    return pl.pallas_call(
        functools.partial(near_grams_kernel, plan),
        out_shape=tuple(jax.ShapeDtypeStruct((len(places), PACKED, WIDTH), jnp.float32) for places in plan),
        in_specs=[VMEM] * len(sources),
        out_specs=(VMEM,) * len(plan),
        compiler_params=PARAMS,
        name="near_grams",
    )(*sources)


def joined_kernel(plan, after, *refs):
    del after
    sources, outs = refs[: -len(plan)], refs[-len(plan) :]
    for places, out in zip(plan, outs):
        for place, (source, first) in enumerate(places):
            out[place] = sources[source][0, :, first * WIDTH : first * WIDTH + out.shape[2]]


def joined(after, plan, *sources):
    rows = sources[0].shape[1]
    return pl.pallas_call(
        functools.partial(joined_kernel, tuple(places for _, places in plan)),
        out_shape=tuple(jax.ShapeDtypeStruct((len(places), rows, pairs * WIDTH), jnp.float32) for pairs, places in plan),
        in_specs=[pl.BlockSpec(memory_space=pl.ANY)] + [VMEM] * len(sources),
        out_specs=(VMEM,) * len(plan),
        compiler_params=PARAMS,
        name="joined",
    )(after, *sources)


def merge_kernel(count, row, *refs):
    parts, outs, held = refs[:count], refs[count:-1], refs[-1]
    value = parts[0][...]
    for part in parts[1:]:
        value = value + part[...]
    held[...] = value
    deal(row[0], held, outs)


def merge(row, parts, shares):
    pairs, height, _ = parts[0].shape
    return pl.pallas_call(
        functools.partial(merge_kernel, len(parts)),
        out_shape=(jax.ShapeDtypeStruct((pairs // shares, height, WIDTH), jnp.float32),) * shares,
        in_specs=[SMEM] + [VMEM] * len(parts),
        out_specs=(VMEM,) * shares,
        scratch_shapes=[pltpu.VMEM((pairs, height, WIDTH), jnp.float32)],
        compiler_params=PARAMS,
        name="merge",
    )(row, *parts)


def rotations(grams_now, on_diag, even, odd, power):
    diag_one = jnp.where(on_diag, 1.0, 0.0)
    size = diag_one.shape[0]
    skews, skews_parts, squares = [], [], []
    for gram_now in grams_now:
        diag_part = jnp.where(on_diag, gram_now, 0.0)
        across = jnp.sum(diag_part, axis=1, keepdims=True)
        down = jnp.sum(diag_part, axis=0, keepdims=True)
        skew = gram_now * (across - down) / (2.0 * (across * across + down * down))
        skews.append(jnp.clip(skew, -0.25, 0.25))
    for skew in skews:
        skews_parts.append(split(skew))
        squares.append(product(skews_parts[-1], skews_parts[-1]))
    evens, odds, rests, worst = [], [], [], None
    for skew, parts, square in zip(skews, skews_parts, squares):
        bound = jnp.sqrt(0.5 * total(square * square))
        scale = 2.0 / (2.0 + bound)
        rate = bound / (2.0 + bound)
        worst = rate if worst is None else jnp.maximum(worst, rate)
        rest = (1.0 - scale) * diag_one + scale * square
        rest_parts = split(rest)
        first = product(jnp.concatenate([parts, rest_parts], axis=0), rest_parts)
        evens.append(scale * (diag_one + rest))
        odds.append(scale * (skew + first[:size]))
        rests.append(split(first[size:]))
    for index, rest_parts in enumerate(rests):
        stack = jnp.concatenate([split(evens[index]), split(odds[index]), rest_parts], axis=0)
        second = product(stack, rest_parts)
        evens[index] = evens[index] + second[:size]
        odds[index] = odds[index] + second[size : 2 * size]
        rests[index] = split(second[2 * size :])
    for index, rest_parts in enumerate(rests):
        third = product(jnp.concatenate([split(evens[index]), split(odds[index])], axis=0), rest_parts)
        even[index] = evens[index] + third[:size]
        odd[index] = odds[index] + third[size:]
        power[index] = rest_parts

    def more(left):
        return left > TOLERANCE

    def step(left):
        for index in range(len(grams_now)):
            old = power[index]
            parts = split(product(old, old))
            power[index] = parts
            even[index] += product(split(even[index]), parts)
            odd[index] += product(split(odd[index]), parts)
        return left * left

    worst = worst * worst
    worst = worst * worst
    left = (worst * worst)[0, 0]
    lax.while_loop(more, step, left)

    def refine(_, carry):
        for index in range(len(grams_now)):
            parts = split(skews[index])
            even_now, odd_now = even[index], odd[index]
            even_parts, odd_parts = split(even_now), split(odd_now)
            even_rest = split(diag_one - even_now + product(parts, odd_parts))
            odd_rest = split(product(parts, even_parts) - odd_now)
            even[index] = even_now + product(even_parts, even_rest) + product(odd_parts, odd_rest)
            odd[index] = odd_now + product(even_parts, odd_rest) + product(odd_parts, even_rest)
        return carry

    lax.fori_loop(0, jnp.where(left > TOLERANCE, 2, 0), refine, 0)
    results = []
    for index in range(len(grams_now)):
        even_now = 2.0 * even[index] - diag_one
        odd_now = 2.0 * odd[index]
        results.append((split(even_now - odd_now), split(even_now + odd_now)))
    return results


def solve_kernel(count, row, *refs):
    parts, out, sums, held, even, odd, power = refs[:count], *refs[count:]
    on_diag = unit(WIDTH)
    pairs = range(out.shape[0])
    each = parts[0].shape[0]
    for by, part in enumerate(parts):
        held[pl.ds(jnp.bitwise_xor(jnp.bitwise_and(row[0], count - 1), by) * each, each)] = part[...]
    off_total = jnp.zeros((1, 1), jnp.float32)
    diag_total = jnp.zeros((1, 1), jnp.float32)
    now = []
    for pair in pairs:
        gram_now = held[pair]
        if gram_now.shape[0] != WIDTH:
            gram_now = unpack(gram_now)
        squares = gram_now * gram_now
        off_total += total(jnp.where(on_diag, 0.0, squares))
        diag_total += total(jnp.where(on_diag, squares, 0.0))
        now.append(gram_now)
    first_lane = lax.broadcasted_iota(jnp.int32, sums.shape, 1) == 0
    sums[...] = jnp.where(first_lane, off_total, diag_total)
    so_far = None
    for sweep in range(ITERS):
        turns = rotations(now, on_diag, even, odd, power)
        if sweep < ITERS - 1:
            halves = [split(product(split(now[pair]), turns[pair][0])) for pair in pairs]
            now = [product(turns[pair][1], halves[pair]) for pair in pairs]
        if so_far is None:
            so_far = [turns[pair][0] for pair in pairs]
        elif sweep < ITERS - 1:
            so_far = [split(product(so_far[pair], turns[pair][0])) for pair in pairs]
        else:
            for pair in pairs:
                out[pair] = product(so_far[pair], turns[pair][0])


def solve(row, parts):
    each, height, _ = parts[0].shape
    pairs = each * len(parts)
    return pl.pallas_call(
        functools.partial(solve_kernel, len(parts)),
        out_shape=(
            jax.ShapeDtypeStruct((pairs, WIDTH, WIDTH), jnp.float32),
            jax.ShapeDtypeStruct((LAST_ROWS, WIDTH), jnp.float32),
        ),
        in_specs=[SMEM] + [VMEM] * len(parts),
        out_specs=(VMEM, VMEM),
        scratch_shapes=[
            pltpu.VMEM((pairs, height, WIDTH), jnp.float32),
            pltpu.VMEM((pairs, WIDTH, WIDTH), jnp.float32),
            pltpu.VMEM((pairs, WIDTH, WIDTH), jnp.float32),
            pltpu.VMEM((pairs, WIDTH, 2 * WIDTH), jnp.bfloat16),
        ],
        compiler_params=PARAMS,
        name="solve",
    )(row, *parts)


def turned(tracks, columns, held):
    results = []
    for pairs, places in tracks:
        for pair in range(pairs):
            value = jnp.concatenate([piece(columns, place, pair) for place in places], axis=0)
            results.append((value, len(results)))
    return lambda index: product(split(results[index][0]), split(held[index]))


def edge_kernel(tracks, parts, where, sums, held, *refs):
    columns, near, far = refs[: -1 - parts], refs[-1 - parts], refs[-parts:]
    odd = lax.rem(where[0], 2) == 1
    rows = columns[0].shape[1]
    half = rows // 2
    blocks = len(tracks[0][1])
    low_lanes = lax.broadcasted_iota(jnp.int32, (half, WIDTH), 1) < BLOCK
    result = turned(tracks, columns, held)
    last = result(held.shape[0] - 1)
    first = result(0)
    for block in range(blocks):
        span = slice(block * half, (block + 1) * half)
        one = last[block * rows : (block + 1) * rows]
        up = jnp.where(low_lanes, one[:half], pltpu.roll(one[half:], BLOCK, 1))
        one = first[block * rows : (block + 1) * rows]
        down = jnp.where(low_lanes, pltpu.roll(one[:half], BLOCK, 1), one[half:])
        near[span] = jnp.where(odd, down, up)
        each = blocks // parts
        far[block // each][block % each * half : (block % each + 1) * half] = jnp.where(odd, up, down)
    near[-LAST_ROWS:] = sums[...]


def edges(tracks, parts, where, sums, columns, turns):
    half = len(tracks[0][1]) * columns[0].shape[1] // 2
    heights = (half + LAST_ROWS,) + (half // parts,) * parts
    return pl.pallas_call(
        functools.partial(edge_kernel, tracks, parts),
        out_shape=tuple(jax.ShapeDtypeStruct((height, WIDTH), jnp.float32) for height in heights),
        in_specs=[SMEM] + [VMEM] * (2 + len(columns)),
        out_specs=(VMEM,) * (1 + parts),
        compiler_params=PARAMS,
        name="edges",
    )(where, sums, turns, *columns)


def place_kernel(tracks, where, near, held, *refs):
    columns, out, mate = refs[:-2], refs[-2], refs[-1]
    pairs = held.shape[0]
    rows = columns[0].shape[1]
    half = rows // 2
    blocks = len(tracks[0][1])
    odd = lax.rem(where[0], 2) == 1
    is_first = where[0] == 0
    is_last = where[0] == where[1] - 1
    low_lanes = lax.broadcasted_iota(jnp.int32, (rows, WIDTH), 1) < BLOCK
    result = turned(tracks, columns, held)
    rotated = [result(pair) for pair in range(pairs)]
    for block in range(blocks):
        span = slice(block * rows, (block + 1) * rows)
        own_place = jnp.bitwise_xor(where[2], block)
        own_rows = pl.ds(pl.multiple_of(own_place * rows, rows), rows)
        there = jnp.bitwise_xor(own_place, jnp.where(odd, where[3], where[4]))
        arrived = near[pl.ds(pl.multiple_of(there * half, half), half)]
        moved = pltpu.roll(arrived, BLOCK, 1)
        for pair in range(pairs):
            if pair == 0:
                upper = jnp.where(is_first, rotated[0][span], jnp.concatenate([arrived, moved], axis=0))
            else:
                upper = rotated[pair - 1][span]
                if pair == 1:
                    upper = jnp.where(is_first, pltpu.roll(upper, BLOCK, 1), upper)
            if pair == pairs - 1:
                own = pltpu.roll(rotated[pair][span], BLOCK, 1)
                lower = jnp.where(is_last, own, jnp.concatenate([moved, arrived], axis=0))
            else:
                lower = rotated[pair + 1][span]
            value = jnp.where(low_lanes, upper, lower)
            out[own_rows, pair * WIDTH : (pair + 1) * WIDTH] = value
            if pair == 0:
                first = value
            if pair == pairs - 1:
                mate[span] = jnp.where(odd, value, first)


def place(tracks, where, columns, near, turns):
    height = len(tracks[0][1]) * columns[0].shape[1]
    pairs = sum(track[0] for track in tracks)
    return pl.pallas_call(
        functools.partial(place_kernel, tracks),
        out_shape=(
            jax.ShapeDtypeStruct((height, pairs * WIDTH), jnp.float32),
            jax.ShapeDtypeStruct((height, WIDTH), jnp.float32),
        ),
        in_specs=[SMEM] + [VMEM] * (2 + len(columns)),
        out_specs=(VMEM, VMEM),
        compiler_params=PARAMS,
        name="place",
    )(where, near, turns, *columns)


def finish_kernel(blocks, parts, where, mate, *refs):
    far, sums, (_, out, ratio, tile, held, sems) = refs[:parts], refs[parts:-6], refs[-6:]
    rows = mate.shape[0] // blocks
    half = rows // 2
    each = blocks // parts
    odd = lax.rem(where[0], 2) == 1
    used = jnp.where(odd, where[0] < where[1] - 1, where[0] > 0)
    lanes = lax.broadcasted_iota(jnp.int32, (rows, WIDTH), 1)
    first_lane = jnp.where(used, jnp.where(odd, BLOCK, 0), WIDTH)
    here = (lanes >= first_lane) & (lanes < first_lane + BLOCK)
    column = pl.ds(pl.multiple_of(jnp.where(odd, out.shape[1] - WIDTH, 0), WIDTH), WIDTH)
    copies = []
    value = sums[0][...]
    for other in sums[1:]:
        value = value + other[...]
    held[...] = jnp.sqrt(value[:1, :1] / value[:1, 1:2])
    copies.append(pltpu.make_async_copy(held, ratio, sems.at[blocks]))
    copies[-1].start()
    for block in range(blocks):
        span = pl.ds(block * rows, rows)
        own_place = jnp.bitwise_xor(where[2], block)
        there = jnp.bitwise_xor(own_place, jnp.where(odd, where[4], where[3]))
        far_rows = pl.ds(pl.multiple_of(lax.rem(there, each) * half, half), half)
        arrived = far[0][far_rows]
        for part in range(1, parts):
            arrived = jnp.where(there < part * each, arrived, far[part][far_rows])
        moved = pltpu.roll(arrived, BLOCK, 1)
        both = jnp.concatenate([jnp.where(odd, moved, arrived), jnp.where(odd, arrived, moved)], axis=0)
        tile[span] = jnp.where(here, both, mate[span])
        own_rows = pl.ds(pl.multiple_of(own_place * rows, rows), rows)
        copies.append(pltpu.make_async_copy(tile.at[span], out.at[own_rows, column], sems.at[block]))
        copies[-1].start()
    for copy in copies:
        copy.wait()


def finish(blocks, where, far, mate, sums, rotated):
    return pl.pallas_call(
        functools.partial(finish_kernel, blocks, len(far)),
        out_shape=(jax.ShapeDtypeStruct(rotated.shape, jnp.float32), jax.ShapeDtypeStruct((1, 1), jnp.float32)),
        in_specs=[SMEM] + [VMEM] * (1 + len(far) + len(sums)) + [HBM],
        out_specs=(HBM, HBM),
        input_output_aliases={2 + len(far) + len(sums): 0},
        scratch_shapes=[
            pltpu.VMEM(mate.shape, jnp.float32),
            pltpu.VMEM((1, 1), jnp.float32),
            pltpu.SemaphoreType.DMA((blocks + 1,)),
        ],
        compiler_params=PARAMS,
        name="finish",
    )(where, mate, *far, *sums, rotated)


def swapped_in_twos(value, axis, first):
    pairs = []
    for i in range(first, lax.axis_size(axis) - 1, 2):
        pairs += [(i, i + 1), (i + 1, i)]
    return lax.ppermute(value, axis, pairs)


def swapped(value, axis, by):
    count = lax.axis_size(axis)
    return lax.ppermute(value, axis, [(i, i ^ by) for i in range(count)])


def on_device(r_factor, block_slots):
    pair_count = lax.axis_size("pair")
    row_count = lax.axis_size("row")
    pair_index = lax.axis_index("pair")
    row_index = lax.axis_index("row")
    local = r_factor.shape[1] // WIDTH // pair_count
    shared = local % 2 == 0 and row_count > 1 and row_count & (row_count - 1) == 0
    shares = 2 if shared else 1
    row = row_index.astype(jnp.int32).reshape(1)
    base = pair_index.astype(jnp.int32).reshape(1)
    if shared and pair_count == 8:
        ahead = local * AHEAD // 4
        plan = [(local, 0, local, (position,)) for position in (0, 2, 4, 1, 3, 5, 7)]
        plan += [(local, 0, ahead, (6,)), (local, ahead, local - ahead, (6,))]
        arranged = gather(r_factor, block_slots, base, tuple(plan))
        here, early, late = arranged[:3], arranged[7], arranged[8]
        near = [swapped(value, "pair", 1) for value in arranged[3:7]]
        early = swapped(early, "pair", 6)
        plan = [[((side, 0, pair), (side + 3, 0, pair)) for pair in range(local)] for side in range(3)]
        plan.append([((7, 0, pair), (6, 0, pair)) for pair in range(ahead)])
        plan[3] += [((8, 0, pair - ahead), (6, 0, pair)) for pair in range(ahead, local)]
        own, *given = near_grams(plan, *here, *near, arranged[7], late)
        taken = [swapped(value, "pair", by) for by, value in zip((2, 4, 6), given)]
        single = tuple((4, pair) for pair in range(local)) + tuple((5, pair) for pair in range(local - ahead))
        cut = (len(single) + 1) // 2
        plan = ((local, ((0, 0), (2, 0))), (local, ((1, 0), (3, 0))), (1, single[:cut]), (1, single[cut:]))
        *going, six_first, six_last = joined(given[0], plan, here[1], here[2], near[1], near[2], near[3], late)
        early, going, taken = lax.optimization_barrier((early, going, taken))
        parts = merge(row, [own] + taken, shares)
        from_far = [swapped(value, "pair", by) for by, value in zip((2, 4), going)]
        from_far += [swapped(value, "pair", 6) for value in (six_first, six_last)]
        columns = (here[0], near[0], early, *from_far)
        six = [(5, index, 0) for index in range(cut)] + [(6, index, 0) for index in range(len(single) - cut)]
        tracks = []
        for pair in range(local):
            places = [(operand, place, pair) for operand, place in ((0, 0), (1, 0), (3, 0), (3, 1), (4, 0), (4, 1))]
            places.append((2, 0, pair) if pair < ahead else six[local + pair - ahead])
            tracks.append((1, (*places, six[pair])))
        tracks = tuple(tracks)
        bases = (pair_index, pair_index - 1, pair_index + 1)
    else:
        (arranged,) = gather(r_factor, block_slots, base, ((local, 0, local, None),))
        column = lax.all_to_all(arranged, "pair", split_axis=0, concat_axis=0, tiled=True)
        parts = grams(row, column, shares)
        columns = (column,)
        tracks = ((local, tuple((0, group, 0) for group in range(pair_count))),)
        bases = (jnp.zeros_like(pair_index),) * 3
    if shared:
        half = parts[0] + swapped(parts[1], "row", 1)
        for bit in range(1, row_count.bit_length() - 1):
            half = half + swapped(half, "row", 1 << bit)
        parts = (half, swapped(half, "row", 1))
    else:
        parts = (lax.psum(parts[0], "row"),)
    turns, sums = solve(row, parts)
    bases = [jnp.clip(value, 0, pair_count - 1) for value in bases]
    where = jnp.stack([pair_index, jnp.int32(pair_count)] + bases).astype(jnp.int32)
    near, *far = edges(tracks, FAR_PARTS if pair_count % FAR_PARTS == 0 else 1, where, sums, columns, turns)
    far = [swapped_in_twos(part, "pair", 1) for part in far]
    near = swapped_in_twos(near, "pair", 0)
    rotated, mate = place(tracks, where, columns, near, turns)
    if pair_count == 8:
        sums = sums + near[-LAST_ROWS:]
        sums = [sums] + [swapped(sums, "pair", by) for by in (2, 4, 6)]
    else:
        sums = [lax.psum(sums, "pair")]
    rotated, off_ratio = finish(pair_count, where, far, mate, sums, rotated)
    return (rotated, off_ratio.reshape(()))


def solution(mesh):
    in_specs = (P(("row", "pair"), None), P())
    out_specs = (P("row", "pair"), P())
    return jax.shard_map(
        on_device, mesh=mesh, in_specs=in_specs, out_specs=out_specs, check_vma=False
    )
```

```python
import functools

import jax
import jax.numpy as jnp
from jax import lax
from jax.experimental import pallas as pl
from jax.experimental.pallas import tpu as pltpu
from jax.sharding import PartitionSpec as P

BLOCK = 64
WIDTH = 2 * BLOCK
ITERS = 3
TOLERANCE = 1e-8
LAST_ROWS = 8
AHEAD = 3
FAR_PARTS = 1
GATHER_CHUNKS = 2
GATHER_VMEM = 62 * 1024 * 1024
VMEM = pl.BlockSpec(memory_space=pltpu.VMEM)
SMEM = pl.BlockSpec(memory_space=pltpu.SMEM)
HBM = pl.BlockSpec(memory_space=pltpu.HBM)
PARAMS = pltpu.CompilerParams(vmem_limit_bytes=48 * 1024 * 1024)


def split(value):
    high = value.astype(jnp.bfloat16)
    low = (value - high.astype(jnp.float32)).astype(jnp.bfloat16)
    return jnp.concatenate([high, low], axis=1)


def product(left, right):
    both = jnp.dot(left, jnp.concatenate([right, right], axis=0), preferred_element_type=jnp.float32)
    half = both.shape[1] // 2
    return both[:, :half] + both[:, half:]


def unit(size):
    row_ids = lax.broadcasted_iota(jnp.int32, (size, size), 0)
    col_ids = lax.broadcasted_iota(jnp.int32, (size, size), 1)
    return row_ids == col_ids


def total(value):
    return jnp.sum(jnp.sum(value, axis=1, keepdims=True), axis=0, keepdims=True)


def gather_kernel(plan, slots, source, *outs):
    rows = source.shape[0]
    local = plan[0][0]
    base = slots[slots.shape[0] - 1]
    low_lanes = lax.broadcasted_iota(jnp.int32, (rows, WIDTH), 1) < BLOCK

    def tile(block):
        return source[:, pl.ds(pl.multiple_of(lax.shift_right_logical(block, 1) * WIDTH, WIDTH), WIDTH)]

    def one_pair(slot):
        upper_block, lower_block = slots[slot], slots[slot + 1]
        upper, lower = tile(upper_block), tile(lower_block)
        turned_over = pltpu.roll(jnp.where(low_lanes, lower, upper), BLOCK, 1)
        upper = jnp.where(jnp.bitwise_and(upper_block, 1) == 0, upper, turned_over)
        lower = jnp.where(jnp.bitwise_and(lower_block, 1) == 1, lower, turned_over)
        return jnp.where(low_lanes, upper, lower)

    for (_, first, positions), out in zip(plan, outs):
        count = out.shape[2] // WIDTH

        def one_group(group, place, first=first, count=count, out=out):
            for pair in range(count):
                value = one_pair(2 * (group * local + first + pair))
                out[place, :, pair * WIDTH : (pair + 1) * WIDTH] = value

        if positions is None:

            def step(group, carry, one_group=one_group):
                one_group(group, group)
                return carry

            lax.fori_loop(0, out.shape[0], step, 0)
        else:
            for place, position in enumerate(positions):
                one_group(jnp.bitwise_xor(base, position), place)


def gather(r_factor, block_slots, base, plan):
    rows = r_factor.shape[0]
    groups = r_factor.shape[1] // WIDTH // plan[0][0]
    shapes = []
    for _, _, taken, positions in plan:
        count = groups if positions is None else len(positions)
        shapes.append(jax.ShapeDtypeStruct((count, rows, taken * WIDTH), jnp.float32))
    return pl.pallas_call(
        functools.partial(gather_kernel, tuple((local, first, positions) for local, first, _, positions in plan)),
        out_shape=tuple(shapes),
        in_specs=[SMEM, VMEM],
        out_specs=(VMEM,) * len(shapes),
        compiler_params=PARAMS,
        name="gather",
    )(jnp.concatenate([block_slots, base]), r_factor)


def gram(pieces):
    parts = split(jnp.concatenate(pieces, axis=0))
    four = lax.dot_general(parts, parts, (((0,), (0,)), ((), ())), preferred_element_type=jnp.float32)
    half = four[:WIDTH] + four[WIDTH:]
    return half[:, :WIDTH] + half[:, WIDTH:]


def piece(refs, where, pair):
    operand, place, first = where
    return refs[operand][place, :, (first + pair) * WIDTH : (first + pair + 1) * WIDTH]


def deal(row, held, outs):
    each = outs[0].shape[0]
    for by, out in enumerate(outs):
        out[...] = held[pl.ds(jnp.bitwise_xor(jnp.bitwise_and(row, len(outs) - 1), by) * each, each)]


def grams_kernel(row, column, *refs):
    outs, held = refs[:-1], refs[-1]
    groups = column.shape[0]
    for pair in range(held.shape[0]):
        held[pair] = gram([piece([column], (0, group, 0), pair) for group in range(groups)])
    deal(row[0], held, outs)


def grams(row, column, shares):
    pairs = column.shape[2] // WIDTH
    return pl.pallas_call(
        grams_kernel,
        out_shape=(jax.ShapeDtypeStruct((pairs // shares, WIDTH, WIDTH), jnp.float32),) * shares,
        in_specs=[SMEM, VMEM],
        out_specs=(VMEM,) * shares,
        scratch_shapes=[pltpu.VMEM((pairs, WIDTH, WIDTH), jnp.float32)],
        compiler_params=PARAMS,
        name="grams",
    )(row, column)


def pack(gram_matrix):
    half = WIDTH // 2
    top = gram_matrix[:half]
    last = pltpu.roll(gram_matrix[half:], half, 1)
    row_ids = lax.broadcasted_iota(jnp.int32, (half, WIDTH), 0)
    col_ids = lax.broadcasted_iota(jnp.int32, (half, WIDTH), 1)
    ends = jnp.sum(jnp.where(row_ids == col_ids, last, 0.0), axis=0, keepdims=True)
    both = jnp.where((col_ids < half) & (row_ids > col_ids), last, top)
    return jnp.concatenate([both, jnp.broadcast_to(ends, (LAST_ROWS, WIDTH))], axis=0)


def unpack(packed):
    half = WIDTH // 2
    both = packed[:half]
    ends = packed[half : half + 1]
    mirrored = jnp.transpose(jnp.concatenate([both, both], axis=0))
    row_ids = lax.broadcasted_iota(jnp.int32, (half, WIDTH), 0)
    col_ids = lax.broadcasted_iota(jnp.int32, (half, WIDTH), 1)
    top = jnp.where((col_ids < half) & (row_ids > col_ids), mirrored[:half], both)
    last = jnp.where(row_ids > col_ids, both, mirrored[:half])
    last = jnp.where(row_ids == col_ids, ends, last)
    bottom = jnp.where(col_ids < half, mirrored[half:], pltpu.roll(last, half, 1))
    return jnp.concatenate([top, bottom], axis=0)


PACKED = WIDTH // 2 + LAST_ROWS


def near_grams_kernel(plan, *refs):
    sources, outs = refs[: -len(plan)], refs[-len(plan) :]
    for places, out in zip(plan, outs):
        for pair in range(out.shape[0]):
            out[pair] = pack(gram([piece(sources, place, 0) for place in places[pair]]))


def near_grams(plan, *sources):
    return pl.pallas_call(
        functools.partial(near_grams_kernel, plan),
        out_shape=tuple(jax.ShapeDtypeStruct((len(places), PACKED, WIDTH), jnp.float32) for places in plan),
        in_specs=[VMEM] * len(sources),
        out_specs=(VMEM,) * len(plan),
        compiler_params=PARAMS,
        name="near_grams",
    )(*sources)


def joined_kernel(plan, after, *refs):
    del after
    sources, outs = refs[: -len(plan)], refs[-len(plan) :]
    for places, out in zip(plan, outs):
        for place, (source, first) in enumerate(places):
            out[place] = sources[source][0, :, first * WIDTH : first * WIDTH + out.shape[2]]


def joined(after, plan, *sources):
    rows = sources[0].shape[1]
    return pl.pallas_call(
        functools.partial(joined_kernel, tuple(places for _, places in plan)),
        out_shape=tuple(jax.ShapeDtypeStruct((len(places), rows, pairs * WIDTH), jnp.float32) for pairs, places in plan),
        in_specs=[pl.BlockSpec(memory_space=pl.ANY)] + [VMEM] * len(sources),
        out_specs=(VMEM,) * len(plan),
        compiler_params=PARAMS,
        name="joined",
    )(after, *sources)


def merge_kernel(count, row, *refs):
    parts, outs, held = refs[:count], refs[count:-1], refs[-1]
    value = parts[0][...]
    for part in parts[1:]:
        value = value + part[...]
    held[...] = value
    deal(row[0], held, outs)


def merge(row, parts, shares):
    pairs, height, _ = parts[0].shape
    return pl.pallas_call(
        functools.partial(merge_kernel, len(parts)),
        out_shape=(jax.ShapeDtypeStruct((pairs // shares, height, WIDTH), jnp.float32),) * shares,
        in_specs=[SMEM] + [VMEM] * len(parts),
        out_specs=(VMEM,) * shares,
        scratch_shapes=[pltpu.VMEM((pairs, height, WIDTH), jnp.float32)],
        compiler_params=PARAMS,
        name="merge",
    )(row, *parts)


def rotations(grams_now, on_diag, even, odd, power):
    diag_one = jnp.where(on_diag, 1.0, 0.0)
    size = diag_one.shape[0]
    skews, skews_parts, squares = [], [], []
    for gram_now in grams_now:
        diag_part = jnp.where(on_diag, gram_now, 0.0)
        across = jnp.sum(diag_part, axis=1, keepdims=True)
        down = jnp.sum(diag_part, axis=0, keepdims=True)
        skew = gram_now * (across - down) / (2.0 * (across * across + down * down))
        skews.append(jnp.clip(skew, -0.25, 0.25))
    for skew in skews:
        skews_parts.append(split(skew))
        squares.append(product(skews_parts[-1], skews_parts[-1]))
    evens, odds, rests, worst = [], [], [], None
    for skew, parts, square in zip(skews, skews_parts, squares):
        bound = jnp.sqrt(0.5 * total(square * square))
        scale = 2.0 / (2.0 + bound)
        rate = bound / (2.0 + bound)
        worst = rate if worst is None else jnp.maximum(worst, rate)
        rest = (1.0 - scale) * diag_one + scale * square
        rest_parts = split(rest)
        first = product(jnp.concatenate([parts, rest_parts], axis=0), rest_parts)
        evens.append(scale * (diag_one + rest))
        odds.append(scale * (skew + first[:size]))
        rests.append(split(first[size:]))
    for index, rest_parts in enumerate(rests):
        stack = jnp.concatenate([split(evens[index]), split(odds[index]), rest_parts], axis=0)
        second = product(stack, rest_parts)
        evens[index] = evens[index] + second[:size]
        odds[index] = odds[index] + second[size : 2 * size]
        rests[index] = split(second[2 * size :])
    for index, rest_parts in enumerate(rests):
        third = product(jnp.concatenate([split(evens[index]), split(odds[index])], axis=0), rest_parts)
        even[index] = evens[index] + third[:size]
        odd[index] = odds[index] + third[size:]
        power[index] = rest_parts

    def more(left):
        return left > TOLERANCE

    def step(left):
        for index in range(len(grams_now)):
            old = power[index]
            parts = split(product(old, old))
            power[index] = parts
            even[index] += product(split(even[index]), parts)
            odd[index] += product(split(odd[index]), parts)
        return left * left

    worst = worst * worst
    worst = worst * worst
    left = (worst * worst)[0, 0]
    lax.while_loop(more, step, left)

    def refine(_, carry):
        for index in range(len(grams_now)):
            parts = split(skews[index])
            even_now, odd_now = even[index], odd[index]
            even_parts, odd_parts = split(even_now), split(odd_now)
            even_rest = split(diag_one - even_now + product(parts, odd_parts))
            odd_rest = split(product(parts, even_parts) - odd_now)
            even[index] = even_now + product(even_parts, even_rest) + product(odd_parts, odd_rest)
            odd[index] = odd_now + product(even_parts, odd_rest) + product(odd_parts, even_rest)
        return carry

    lax.fori_loop(0, jnp.where(left > TOLERANCE, 2, 0), refine, 0)
    results = []
    for index in range(len(grams_now)):
        even_now = 2.0 * even[index] - diag_one
        odd_now = 2.0 * odd[index]
        results.append((split(even_now - odd_now), split(even_now + odd_now)))
    return results


def solve_kernel(count, row, *refs):
    parts, out, sums, held, even, odd, power = refs[:count], *refs[count:]
    on_diag = unit(WIDTH)
    pairs = range(out.shape[0])
    each = parts[0].shape[0]
    for by, part in enumerate(parts):
        held[pl.ds(jnp.bitwise_xor(jnp.bitwise_and(row[0], count - 1), by) * each, each)] = part[...]
    off_total = jnp.zeros((1, 1), jnp.float32)
    diag_total = jnp.zeros((1, 1), jnp.float32)
    now = []
    for pair in pairs:
        gram_now = held[pair]
        if gram_now.shape[0] != WIDTH:
            gram_now = unpack(gram_now)
        squares = gram_now * gram_now
        off_total += total(jnp.where(on_diag, 0.0, squares))
        diag_total += total(jnp.where(on_diag, squares, 0.0))
        now.append(gram_now)
    first_lane = lax.broadcasted_iota(jnp.int32, sums.shape, 1) == 0
    sums[...] = jnp.where(first_lane, off_total, diag_total)
    so_far = None
    for sweep in range(ITERS):
        turns = rotations(now, on_diag, even, odd, power)
        if sweep < ITERS - 1:
            halves = [split(product(split(now[pair]), turns[pair][0])) for pair in pairs]
            now = [product(turns[pair][1], halves[pair]) for pair in pairs]
        if so_far is None:
            so_far = [turns[pair][0] for pair in pairs]
        elif sweep < ITERS - 1:
            so_far = [split(product(so_far[pair], turns[pair][0])) for pair in pairs]
        else:
            for pair in pairs:
                out[pair] = product(so_far[pair], turns[pair][0])


def solve(row, parts):
    each, height, _ = parts[0].shape
    pairs = each * len(parts)
    return pl.pallas_call(
        functools.partial(solve_kernel, len(parts)),
        out_shape=(
            jax.ShapeDtypeStruct((pairs, WIDTH, WIDTH), jnp.float32),
            jax.ShapeDtypeStruct((LAST_ROWS, WIDTH), jnp.float32),
        ),
        in_specs=[SMEM] + [VMEM] * len(parts),
        out_specs=(VMEM, VMEM),
        scratch_shapes=[
            pltpu.VMEM((pairs, height, WIDTH), jnp.float32),
            pltpu.VMEM((pairs, WIDTH, WIDTH), jnp.float32),
            pltpu.VMEM((pairs, WIDTH, WIDTH), jnp.float32),
            pltpu.VMEM((pairs, WIDTH, 2 * WIDTH), jnp.bfloat16),
        ],
        compiler_params=PARAMS,
        name="solve",
    )(row, *parts)


def turned(tracks, columns, held):
    results = []
    for pairs, places in tracks:
        for pair in range(pairs):
            value = jnp.concatenate([piece(columns, place, pair) for place in places], axis=0)
            results.append((value, len(results)))
    return lambda index: product(split(results[index][0]), split(held[index]))


def edge_kernel(tracks, parts, where, sums, held, *refs):
    columns, near, far = refs[: -1 - parts], refs[-1 - parts], refs[-parts:]
    odd = lax.rem(where[0], 2) == 1
    rows = columns[0].shape[1]
    half = rows // 2
    blocks = len(tracks[0][1])
    low_lanes = lax.broadcasted_iota(jnp.int32, (half, WIDTH), 1) < BLOCK
    result = turned(tracks, columns, held)
    last = result(held.shape[0] - 1)
    first = result(0)
    for block in range(blocks):
        span = slice(block * half, (block + 1) * half)
        one = last[block * rows : (block + 1) * rows]
        up = jnp.where(low_lanes, one[:half], pltpu.roll(one[half:], BLOCK, 1))
        one = first[block * rows : (block + 1) * rows]
        down = jnp.where(low_lanes, pltpu.roll(one[:half], BLOCK, 1), one[half:])
        near[span] = jnp.where(odd, down, up)
        each = blocks // parts
        far[block // each][block % each * half : (block % each + 1) * half] = jnp.where(odd, up, down)
    near[-LAST_ROWS:] = sums[...]


def edges(tracks, parts, where, sums, columns, turns):
    half = len(tracks[0][1]) * columns[0].shape[1] // 2
    heights = (half + LAST_ROWS,) + (half // parts,) * parts
    return pl.pallas_call(
        functools.partial(edge_kernel, tracks, parts),
        out_shape=tuple(jax.ShapeDtypeStruct((height, WIDTH), jnp.float32) for height in heights),
        in_specs=[SMEM] + [VMEM] * (2 + len(columns)),
        out_specs=(VMEM,) * (1 + parts),
        compiler_params=PARAMS,
        name="edges",
    )(where, sums, turns, *columns)


def place_kernel(tracks, where, near, held, *refs):
    columns, out, mate = refs[:-2], refs[-2], refs[-1]
    pairs = held.shape[0]
    rows = columns[0].shape[1]
    half = rows // 2
    blocks = len(tracks[0][1])
    odd = lax.rem(where[0], 2) == 1
    is_first = where[0] == 0
    is_last = where[0] == where[1] - 1
    low_lanes = lax.broadcasted_iota(jnp.int32, (rows, WIDTH), 1) < BLOCK
    result = turned(tracks, columns, held)
    rotated = [result(pair) for pair in range(pairs)]
    for block in range(blocks):
        span = slice(block * rows, (block + 1) * rows)
        own_place = jnp.bitwise_xor(where[2], block)
        own_rows = pl.ds(pl.multiple_of(own_place * rows, rows), rows)
        there = jnp.bitwise_xor(own_place, jnp.where(odd, where[3], where[4]))
        arrived = near[pl.ds(pl.multiple_of(there * half, half), half)]
        moved = pltpu.roll(arrived, BLOCK, 1)
        for pair in range(pairs):
            if pair == 0:
                upper = jnp.where(is_first, rotated[0][span], jnp.concatenate([arrived, moved], axis=0))
            else:
                upper = rotated[pair - 1][span]
                if pair == 1:
                    upper = jnp.where(is_first, pltpu.roll(upper, BLOCK, 1), upper)
            if pair == pairs - 1:
                own = pltpu.roll(rotated[pair][span], BLOCK, 1)
                lower = jnp.where(is_last, own, jnp.concatenate([moved, arrived], axis=0))
            else:
                lower = rotated[pair + 1][span]
            value = jnp.where(low_lanes, upper, lower)
            out[own_rows, pair * WIDTH : (pair + 1) * WIDTH] = value
            if pair == 0:
                first = value
            if pair == pairs - 1:
                mate[span] = jnp.where(odd, value, first)


def place(tracks, where, columns, near, turns):
    height = len(tracks[0][1]) * columns[0].shape[1]
    pairs = sum(track[0] for track in tracks)
    return pl.pallas_call(
        functools.partial(place_kernel, tracks),
        out_shape=(
            jax.ShapeDtypeStruct((height, pairs * WIDTH), jnp.float32),
            jax.ShapeDtypeStruct((height, WIDTH), jnp.float32),
        ),
        in_specs=[SMEM] + [VMEM] * (2 + len(columns)),
        out_specs=(VMEM, VMEM),
        compiler_params=PARAMS,
        name="place",
    )(where, near, turns, *columns)


def finish_kernel(blocks, parts, where, mate, *refs):
    far, sums, (_, out, ratio, tile, held, sems) = refs[:parts], refs[parts:-6], refs[-6:]
    rows = mate.shape[0] // blocks
    half = rows // 2
    each = blocks // parts
    odd = lax.rem(where[0], 2) == 1
    used = jnp.where(odd, where[0] < where[1] - 1, where[0] > 0)
    lanes = lax.broadcasted_iota(jnp.int32, (rows, WIDTH), 1)
    first_lane = jnp.where(used, jnp.where(odd, BLOCK, 0), WIDTH)
    here = (lanes >= first_lane) & (lanes < first_lane + BLOCK)
    column = pl.ds(pl.multiple_of(jnp.where(odd, out.shape[1] - WIDTH, 0), WIDTH), WIDTH)
    copies = []
    value = sums[0][...]
    for other in sums[1:]:
        value = value + other[...]
    held[...] = jnp.sqrt(value[:1, :1] / value[:1, 1:2])
    copies.append(pltpu.make_async_copy(held, ratio, sems.at[blocks]))
    copies[-1].start()
    for block in range(blocks):
        span = pl.ds(block * rows, rows)
        own_place = jnp.bitwise_xor(where[2], block)
        there = jnp.bitwise_xor(own_place, jnp.where(odd, where[4], where[3]))
        far_rows = pl.ds(pl.multiple_of(lax.rem(there, each) * half, half), half)
        arrived = far[0][far_rows]
        for part in range(1, parts):
            arrived = jnp.where(there < part * each, arrived, far[part][far_rows])
        moved = pltpu.roll(arrived, BLOCK, 1)
        both = jnp.concatenate([jnp.where(odd, moved, arrived), jnp.where(odd, arrived, moved)], axis=0)
        tile[span] = jnp.where(here, both, mate[span])
        own_rows = pl.ds(pl.multiple_of(own_place * rows, rows), rows)
        copies.append(pltpu.make_async_copy(tile.at[span], out.at[own_rows, column], sems.at[block]))
        copies[-1].start()
    for copy in copies:
        copy.wait()


def finish(blocks, where, far, mate, sums, rotated):
    return pl.pallas_call(
        functools.partial(finish_kernel, blocks, len(far)),
        out_shape=(jax.ShapeDtypeStruct(rotated.shape, jnp.float32), jax.ShapeDtypeStruct((1, 1), jnp.float32)),
        in_specs=[SMEM] + [VMEM] * (1 + len(far) + len(sums)) + [HBM],
        out_specs=(HBM, HBM),
        input_output_aliases={2 + len(far) + len(sums): 0},
        scratch_shapes=[
            pltpu.VMEM(mate.shape, jnp.float32),
            pltpu.VMEM((1, 1), jnp.float32),
            pltpu.SemaphoreType.DMA((blocks + 1,)),
        ],
        compiler_params=PARAMS,
        name="finish",
    )(where, mate, *far, *sums, rotated)


def swapped_in_twos(value, axis, first):
    pairs = []
    for i in range(first, lax.axis_size(axis) - 1, 2):
        pairs += [(i, i + 1), (i + 1, i)]
    return lax.ppermute(value, axis, pairs)


def swapped(value, axis, by):
    count = lax.axis_size(axis)
    return lax.ppermute(value, axis, [(i, i ^ by) for i in range(count)])


def on_device(r_factor, block_slots):
    pair_count = lax.axis_size("pair")
    row_count = lax.axis_size("row")
    pair_index = lax.axis_index("pair")
    row_index = lax.axis_index("row")
    local = r_factor.shape[1] // WIDTH // pair_count
    shared = local % 2 == 0 and row_count > 1 and row_count & (row_count - 1) == 0
    shares = 2 if shared else 1
    row = row_index.astype(jnp.int32).reshape(1)
    base = pair_index.astype(jnp.int32).reshape(1)
    if shared and pair_count == 8:
        ahead = local * AHEAD // 4
        plan = [(local, 0, local, (position,)) for position in (0, 2, 4, 1, 3, 5, 7)]
        plan += [(local, 0, ahead, (6,)), (local, ahead, local - ahead, (6,))]
        arranged = gather(r_factor, block_slots, base, tuple(plan))
        here, early, late = arranged[:3], arranged[7], arranged[8]
        near = [swapped(value, "pair", 1) for value in arranged[3:7]]
        early = swapped(early, "pair", 6)
        plan = [[((side, 0, pair), (side + 3, 0, pair)) for pair in range(local)] for side in range(3)]
        plan.append([((7, 0, pair), (6, 0, pair)) for pair in range(ahead)])
        plan[3] += [((8, 0, pair - ahead), (6, 0, pair)) for pair in range(ahead, local)]
        own, *given = near_grams(plan, *here, *near, arranged[7], late)
        taken = [swapped(value, "pair", by) for by, value in zip((2, 4, 6), given)]
        single = tuple((4, pair) for pair in range(local)) + tuple((5, pair) for pair in range(local - ahead))
        cut = (len(single) + 1) // 2
        plan = ((local, ((0, 0), (2, 0))), (local, ((1, 0), (3, 0))), (1, single[:cut]), (1, single[cut:]))
        *going, six_first, six_last = joined(given[0], plan, here[1], here[2], near[1], near[2], near[3], late)
        early, going, taken = lax.optimization_barrier((early, going, taken))
        parts = merge(row, [own] + taken, shares)
        from_far = [swapped(value, "pair", by) for by, value in zip((2, 4), going)]
        from_far += [swapped(value, "pair", 6) for value in (six_first, six_last)]
        columns = (here[0], near[0], early, *from_far)
        six = [(5, index, 0) for index in range(cut)] + [(6, index, 0) for index in range(len(single) - cut)]
        tracks = []
        for pair in range(local):
            places = [(operand, place, pair) for operand, place in ((0, 0), (1, 0), (3, 0), (3, 1), (4, 0), (4, 1))]
            places.append((2, 0, pair) if pair < ahead else six[local + pair - ahead])
            tracks.append((1, (*places, six[pair])))
        tracks = tuple(tracks)
        bases = (pair_index, pair_index - 1, pair_index + 1)
    else:
        (arranged,) = gather(r_factor, block_slots, base, ((local, 0, local, None),))
        column = lax.all_to_all(arranged, "pair", split_axis=0, concat_axis=0, tiled=True)
        parts = grams(row, column, shares)
        columns = (column,)
        tracks = ((local, tuple((0, group, 0) for group in range(pair_count))),)
        bases = (jnp.zeros_like(pair_index),) * 3
    if shared:
        half = parts[0] + swapped(parts[1], "row", 1)
        for bit in range(1, row_count.bit_length() - 1):
            half = half + swapped(half, "row", 1 << bit)
        parts = (half, swapped(half, "row", 1))
    else:
        parts = (lax.psum(parts[0], "row"),)
    turns, sums = solve(row, parts)
    bases = [jnp.clip(value, 0, pair_count - 1) for value in bases]
    where = jnp.stack([pair_index, jnp.int32(pair_count)] + bases).astype(jnp.int32)
    near, *far = edges(tracks, FAR_PARTS if pair_count % FAR_PARTS == 0 else 1, where, sums, columns, turns)
    far = [swapped_in_twos(part, "pair", 1) for part in far]
    near = swapped_in_twos(near, "pair", 0)
    rotated, mate = place(tracks, where, columns, near, turns)
    if pair_count == 8:
        sums = sums + near[-LAST_ROWS:]
        sums = [sums] + [swapped(sums, "pair", by) for by in (6, 4, 2)]
    else:
        sums = [lax.psum(sums, "pair")]
    rotated, off_ratio = finish(pair_count, where, far, mate, sums, rotated)
    return (rotated, off_ratio.reshape(()))


def solution(mesh):
    in_specs = (P(("row", "pair"), None), P())
    out_specs = (P("row", "pair"), P())
    return jax.shard_map(
        on_device, mesh=mesh, in_specs=in_specs, out_specs=out_specs, check_vma=False
    )
```
